32 devices in a mesh: groups: 2 (over y), gx: 4 (over x, core), gy: 4 (over z).
Axes of the slice: x: 2, y: 2, z: 4, core: 2. Of those that a mesh axis runs over, the one named last changes fastest.
Arguments:
- inputs: bfloat16 [64, 16384], P('groups', 'gx'), parts along dimension 0, may hold values from -16 to 16
- gain: float32 [16384], P('gx'), may hold values from 0.5 to 1.5
- w_query: bfloat16 [16384, 8192], P('gx', 'gy'), may hold values from -0.046875 to 0.046875
- w_key: bfloat16 [16384, 512], P('gx', 'gy'), may hold values from -0.1875 to 0.1875
- w_value: bfloat16 [16384, 512], P('gx', 'gy'), may hold values from -0.046875 to 0.046875
- w_output: bfloat16 [8192, 16384], P('gy', 'gx'), may hold values from -0.0625 to 0.0625
- key_cache: bfloat16 [64, 2048, 512], P(('groups', 'gx'), None, 'gy'), parts along dimension 0, may hold values from -1000 to 1000
- value_cache: bfloat16 [64, 2048, 512], P(('groups', 'gx'), None, 'gy'), parts along dimension 0, may hold values from -6 to 6
- lengths: int32 [64], P(('groups', 'gx')), parts along dimension 0, may hold values from 1024 to 2048, as said below
Outputs:
- outputs: bfloat16 [64, 16384], P('groups', 'gx'), parts along dimension 0
The draws below stay inside these ranges and needn't reach their ends.
There are 2 independent parts, one for each index of `groups`. The reference program is written for one: setup_inputs(seed, part) draws one part's arguments, and reference() takes and returns one part's arrays. A program takes and returns all parts, laid end to end along the dimension named above; an argument that names none is the same for every part. Nothing has to cross between parts.
Inputs may be any that keep to these rules, and one draw needn't show every extreme that they name: The new token stands at position lengths[b]; some row has 2048.
All inputs are finite; a program needn't handle non-finite values.
Results may differ from the reference program's by a relative error of at most 0.0083.
Values may be sent and summed in bfloat16 or wider, within the bound.
No kernel may reach another device: no remote copies, remote signals or barrier semaphores. Data moves between devices by JAX's collectives and lax.ppermute only.
A program may use at most 128 MiB of HBM per device.

```python
import jax
import jax.numpy as jnp
from jax import lax

D = 16384
HD = 128
GROUP = 16
S = 2048
KVH = 4
H = 64
B = 32


def draw_inputs(key, part):
    key = jax.random.fold_in(key, 11)
    first = jax.random.fold_in(key, 0)
    third = jax.random.fold_in(key, 2)
    blocks = (D + 127) // 128
    loudness = jnp.exp(jax.random.uniform(third, (B, blocks), jnp.float32, jnp.log(0.3), jnp.log(3.0)))
    columns = jnp.repeat(loudness, 128, axis=1)[:, :D]
    base = jnp.clip(jax.random.normal(first, (B, D), jnp.float32), -6.0, 6.0)
    return jnp.clip(0.6 * base * columns, -16.0, 16.0).astype(jnp.bfloat16)


def draw_key_cache(key, part):
    key = jax.random.fold_in(key, 23)
    first = jax.random.fold_in(key, 0)
    base = 1.5 * jnp.clip(jax.random.normal(first, (B, S, KVH * HD), jnp.float32), -6.0, 6.0)
    return base.astype(jnp.bfloat16)


def draw_lengths(key, part):
    key = jax.random.fold_in(key, 37)
    first, second = jax.random.split(key)
    counts = jax.random.randint(first, (B,), S // 2, S + 1)
    chosen = jax.random.randint(second, (), 0, B)
    return counts.at[chosen].set(S).astype(jnp.int32)


def steps_of(own_key, dims, cuts, smallest, top_value):
    level = 1.0
    for position, blocks in cuts:
        heights = jax.random.uniform(jax.random.fold_in(jax.random.fold_in(own_key, 6), position), (blocks,), jnp.float32, smallest / len(cuts), top_value / len(cuts))
        level = level * jnp.repeat(jnp.exp(heights), dims[position] // blocks).reshape((-1,) + (1,) * (len(dims) - 1 - position))
    return level


def bell_draw(rng, shape, scale, most, cuts=(), held_as=jnp.bfloat16):
    result = scale * jax.random.normal(rng, shape, jnp.float32)
    if cuts:
        result = result * steps_of(rng, shape, cuts, -0.22, 0.18)
    return jnp.clip(result, -most, most).astype(held_as)


def setup_inputs(seed: int = 0, part: int = 0) -> dict:
    key_list = jax.random.split(jax.random.key(seed), 10)
    part_keys = jax.random.split(jax.random.fold_in(key_list[9], part), 10)
    return {
        "inputs": draw_inputs(jax.random.fold_in(jax.random.fold_in(key_list[9], part), 71), part),
        "gain": jnp.clip(1.0 + 0.1 * jax.random.normal(key_list[1], (D,), jnp.float32), 0.5, 1.5),
        "w_query": bell_draw(key_list[2], (D, H * HD), D ** -0.5, 0.046875, ((0, 4), (1, 4))),
        "w_key": bell_draw(key_list[3], (D, KVH * HD), (D // 16) ** -0.5, 0.1875, ((0, 4), (1, 4))),
        "w_value": bell_draw(key_list[4], (D, KVH * HD), D ** -0.5, 0.046875, ((0, 4), (1, 4))),
        "w_output": bell_draw(key_list[5], (H * HD, D), (H * HD) ** -0.5, 0.0625, ((0, 4), (1, 4))),
        "key_cache": draw_key_cache(jax.random.fold_in(jax.random.fold_in(key_list[9], part), 71), part),
        "value_cache": bell_draw(part_keys[7], (B, S, KVH * HD), 1.0, 6.0, ((0, 4), (2, 4))),
        "lengths": draw_lengths(jax.random.fold_in(jax.random.fold_in(key_list[9], part), 71), part),
    }


eps = 1e-05
rope_base = 500000.0

def angles_for(lengths, half):
    inverse = rope_base ** (-(jnp.arange(half, dtype=jnp.float32) * 2.0 / (2 * half)))
    return lengths.astype(jnp.float32)[:, None] * inverse[None, :]

def rotate(values, angles):
    half = values.shape[-1] // 2
    cosine = jnp.cos(angles)
    sine = jnp.sin(angles)
    first = values[..., :half]
    second = values[..., half:]
    return jnp.concatenate([first * cosine - second * sine, second * cosine + first * sine], -1)

def attend(queries, new_keys, new_values, keys, values, lengths):
    factor = queries.shape[-1] ** (-0.5)
    slots = keys.shape[1]
    scores = jnp.einsum('rkgd,rskd->rkgs', queries.astype(jnp.float32), keys.astype(jnp.float32)) * factor
    own = lax.optimization_barrier(jnp.sum(queries.astype(jnp.float32) * new_keys.astype(jnp.float32)[:, :, None, :], -1)) * factor
    valid = jnp.arange(slots)[None, None, None, :] < lengths[:, None, None, None]
    top = jnp.maximum(lax.optimization_barrier(jnp.max(jnp.where(valid, scores, -jnp.inf), -1)), own)
    probs = jnp.where(valid, jnp.exp(scores - top[..., None]), 0.0)
    own_prob = jnp.exp(own - top)
    total = lax.optimization_barrier(jnp.sum(probs, -1)) + own_prob
    weights = (probs / total[..., None]).astype(jnp.bfloat16)
    own_weight = (own_prob / total).astype(jnp.bfloat16)
    mixed = jnp.einsum('rkgs,rskd->rkgd', weights.astype(jnp.float32), values.astype(jnp.float32))
    mixed = mixed + own_weight.astype(jnp.float32)[..., None] * new_values.astype(jnp.float32)[:, :, None, :]
    return mixed.astype(jnp.bfloat16)

def reference(inputs, gain, w_query, w_key, w_value, w_output, key_cache, value_cache, lengths):
    widened = inputs.astype(jnp.float32)
    scale_rows = lax.rsqrt(lax.optimization_barrier(jnp.sum(widened * widened, 1)) / D + eps)
    scaled = (widened * gain).astype(jnp.bfloat16)
    queries = jnp.dot(scaled, w_query, preferred_element_type=jnp.float32) * scale_rows[:, None]
    keys = jnp.dot(scaled, w_key, preferred_element_type=jnp.float32) * scale_rows[:, None]
    values = jnp.dot(scaled, w_value, preferred_element_type=jnp.float32) * scale_rows[:, None]
    angles = angles_for(lengths, HD // 2)
    new_queries = rotate(queries.reshape(B, KVH, GROUP, HD), angles[:, None, None, :]).astype(jnp.bfloat16)
    new_keys = rotate(keys.reshape(B, KVH, HD), angles[:, None, :]).astype(jnp.bfloat16)
    new_values = values.reshape(B, KVH, HD).astype(jnp.bfloat16)

    def one_head(index):
        query_part = lax.dynamic_index_in_dim(new_queries, index, 1, keepdims=True)
        key_part = lax.dynamic_index_in_dim(new_keys, index, 1, keepdims=True)
        value_part = lax.dynamic_index_in_dim(new_values, index, 1, keepdims=True)
        start = (index * HD).astype(jnp.int32)
        cached_keys = lax.dynamic_slice_in_dim(key_cache, start, HD, 2)[:, :, None, :]
        cached_values = lax.dynamic_slice_in_dim(value_cache, start, HD, 2)[:, :, None, :]
        return attend(query_part, key_part, value_part, cached_keys, cached_values, lengths)[:, 0]
    heads = lax.map(one_head, jnp.arange(KVH, dtype=jnp.int32))
    heads = heads.transpose(1, 0, 2, 3).reshape(B, H * HD)
    projected = jnp.dot(heads, w_output, preferred_element_type=jnp.float32)
    return (widened + projected).astype(jnp.bfloat16)
```

```python
import jax
import jax.numpy as jnp
from jax import lax
from jax.sharding import PartitionSpec as P

HD = 128
EPS = 1e-05
ROPE_BASE = 500000.0


def rotate(values, cosine, sine):
    half = values.shape[-1] // 2
    first = values[..., :half]
    second = values[..., half:]
    return jnp.concatenate([first * cosine - second * sine, second * cosine + first * sine], -1)


def attend(queries, new_keys, new_values, keys, values, lengths):
    factor = queries.shape[-1] ** (-0.5)
    slots = keys.shape[1]
    scores = jnp.einsum("rgd,rsd->rgs", queries, keys, preferred_element_type=jnp.float32) * factor
    own = (
        jnp.sum(queries.astype(jnp.float32) * new_keys.astype(jnp.float32)[:, None, :], -1) * factor
    )
    valid = jnp.arange(slots)[None, None, :] < lengths[:, None, None]
    top = jnp.maximum(jnp.max(jnp.where(valid, scores, -jnp.inf), -1), own)
    probs = jnp.where(valid, jnp.exp(scores - top[..., None]), 0.0)
    own_prob = jnp.exp(own - top)
    total = jnp.sum(probs, -1) + own_prob
    weights = (probs / total[..., None]).astype(jnp.bfloat16)
    own_weight = (own_prob / total).astype(jnp.bfloat16)
    mixed = jnp.einsum("rgs,rsd->rgd", weights, values, preferred_element_type=jnp.float32)
    mixed = (
        mixed
        + own_weight.astype(jnp.float32)[..., None] * new_values.astype(jnp.float32)[:, None, :]
    )
    return mixed.astype(jnp.bfloat16)


def swap(value, axis, size, mask):
    return lax.ppermute(value, axis, [(i, i ^ mask) for i in range(size)])


def scatter_sum(value, axis, size, sent):
    rows = value.shape[0] // size
    me = lax.axis_index(axis)
    block = lambda who: lax.dynamic_slice_in_dim(value, who * rows, rows, 0)
    arrived = [swap(block(me ^ mask).astype(sent), axis, size, mask) for mask in range(1, size)]
    total = block(me)
    for item in arrived:
        total = total + item.astype(jnp.float32)
    return total


def gather(value, axis, size):
    me = lax.axis_index(axis)
    rows = value.shape[0]
    result = jnp.zeros((rows * size,) + value.shape[1:], value.dtype)
    for mask in range(size):
        item = swap(value, axis, size, mask) if mask else value
        result = lax.dynamic_update_slice_in_dim(result, item, (me ^ mask) * rows, 0)
    return result


def solution(mesh):
    size_x = mesh.shape["gx"]
    size_y = mesh.shape["gy"]

    def shards(inputs, gain, w_query, w_key, w_value, w_output, key_cache, value_cache, lengths):
        widened = inputs.astype(jnp.float32)
        scaled = (widened * gain).astype(jnp.bfloat16)
        width = w_query.shape[1]
        model = inputs.shape[1] * size_x
        squares = jnp.sum(widened * widened, 1, keepdims=True)
        dot = lambda w: jnp.dot(scaled, w, preferred_element_type=jnp.float32)
        packed = jnp.concatenate(
            [
                dot(w_query),
                dot(w_key),
                dot(w_value),
                jnp.broadcast_to(squares, (squares.shape[0], HD)),
            ],
            1,
        )
        summed = scatter_sum(packed, "gx", size_x, jnp.float32)
        rows = summed.shape[0]
        scale_rows = lax.rsqrt(summed[:, width + 2 * HD :][:, :1] / model + EPS)
        summed = summed[:, : width + 2 * HD] * scale_rows
        half = HD // 2
        inverse = ROPE_BASE ** (-(jnp.arange(half, dtype=jnp.float32) * 2.0 / HD))
        angles = lengths.astype(jnp.float32)[:, None] * inverse[None, :]
        cosine, sine = jnp.cos(angles), jnp.sin(angles)
        queries = summed[:, :width].reshape(rows, width // HD, HD)
        keys = summed[:, width : width + HD]
        values = summed[:, width + HD :]
        new_queries = rotate(queries, cosine[:, None], sine[:, None]).astype(jnp.bfloat16)
        new_keys = rotate(keys, cosine, sine).astype(jnp.bfloat16)
        heads = attend(
            new_queries, new_keys, values.astype(jnp.bfloat16), key_cache, value_cache, lengths
        )
        heads = gather(heads.reshape(rows, width), "gx", size_x)
        partial_out = jnp.dot(heads, w_output, preferred_element_type=jnp.float32)
        mine = scatter_sum(partial_out, "gy", size_y, jnp.bfloat16)
        count = mine.shape[0]
        residual = lax.dynamic_slice_in_dim(inputs, lax.axis_index("gy") * count, count, 0)
        return gather((mine + residual.astype(jnp.float32)).astype(jnp.bfloat16), "gy", size_y)

    placed = (
        P("groups", "gx"),
        P("gx"),
        P("gx", "gy"),
        P("gx", "gy"),
        P("gx", "gy"),
        P("gy", "gx"),
        P(("groups", "gx"), None, "gy"),
        P(("groups", "gx"), None, "gy"),
        P(("groups", "gx")),
    )
    return jax.shard_map(
        shards, mesh=mesh, in_specs=placed, out_specs=P("groups", "gx"), check_vma=False
    )
```

```python
import jax
import jax.numpy as jnp
from jax import lax
from jax.sharding import PartitionSpec as P

HD = 128
EPS = 1e-05
ROPE_BASE = 500000.0


def rotate(values, cosine, sine):
    half = values.shape[-1] // 2
    first = values[..., :half]
    second = values[..., half:]
    return jnp.concatenate([first * cosine - second * sine, second * cosine + first * sine], -1)


def attend(queries, new_keys, new_values, keys, values, lengths):
    factor = queries.shape[-1] ** (-0.5)
    slots = keys.shape[1]
    scores = jnp.einsum("rgd,rsd->rgs", queries, keys, preferred_element_type=jnp.float32) * factor
    own = (
        jnp.sum(queries.astype(jnp.float32) * new_keys.astype(jnp.float32)[:, None, :], -1) * factor
    )
    valid = jnp.arange(slots)[None, None, :] < lengths[:, None, None]
    top = jnp.maximum(jnp.max(jnp.where(valid, scores, -jnp.inf), -1), own)
    probs = jnp.where(valid, jnp.exp(scores - top[..., None]), 0.0)
    own_prob = jnp.exp(own - top)
    total = jnp.sum(probs, -1) + own_prob
    weights = (probs / total[..., None]).astype(jnp.bfloat16)
    own_weight = (own_prob / total).astype(jnp.bfloat16)
    mixed = jnp.einsum("rgs,rsd->rgd", weights, values, preferred_element_type=jnp.float32)
    mixed = (
        mixed
        + own_weight.astype(jnp.float32)[..., None] * new_values.astype(jnp.float32)[:, None, :]
    )
    return mixed.astype(jnp.bfloat16)


def scatter_sum(value, axis, size, sent):
    rows = value.shape[0] // size
    blocks = value.reshape((size, rows) + value.shape[1:]).astype(sent)
    arrived = lax.all_to_all(blocks, axis, 0, 0, tiled=True)
    return jnp.sum(arrived.astype(jnp.float32), 0)


def gather(value, axis, size):
    rows = value.shape[0]
    blocks = jnp.broadcast_to(value[None], (size,) + value.shape)
    arrived = lax.all_to_all(blocks, axis, 0, 0, tiled=True)
    return arrived.reshape((rows * size,) + value.shape[1:])


def solution(mesh):
    size_x = mesh.shape["gx"]
    size_y = mesh.shape["gy"]

    def shards(inputs, gain, w_query, w_key, w_value, w_output, key_cache, value_cache, lengths):
        widened = inputs.astype(jnp.float32)
        scaled = (widened * gain).astype(jnp.bfloat16)
        width = w_query.shape[1]
        model = inputs.shape[1] * size_x
        squares = jnp.sum(widened * widened, 1, keepdims=True)
        dot = lambda w: jnp.dot(scaled, w, preferred_element_type=jnp.float32)
        packed = jnp.concatenate(
            [
                dot(w_query),
                dot(w_key),
                dot(w_value),
                jnp.broadcast_to(squares, (squares.shape[0], HD)),
            ],
            1,
        )
        summed = scatter_sum(packed, "gx", size_x, jnp.float32)
        rows = summed.shape[0]
        scale_rows = lax.rsqrt(summed[:, width + 2 * HD :][:, :1] / model + EPS)
        summed = summed[:, : width + 2 * HD] * scale_rows
        half = HD // 2
        inverse = ROPE_BASE ** (-(jnp.arange(half, dtype=jnp.float32) * 2.0 / HD))
        angles = lengths.astype(jnp.float32)[:, None] * inverse[None, :]
        cosine, sine = jnp.cos(angles), jnp.sin(angles)
        queries = summed[:, :width].reshape(rows, width // HD, HD)
        keys = summed[:, width : width + HD]
        values = summed[:, width + HD :]
        new_queries = rotate(queries, cosine[:, None], sine[:, None]).astype(jnp.bfloat16)
        new_keys = rotate(keys, cosine, sine).astype(jnp.bfloat16)
        heads = attend(
            new_queries, new_keys, values.astype(jnp.bfloat16), key_cache, value_cache, lengths
        )
        heads = gather(heads.reshape(rows, width), "gx", size_x)
        partial_out = jnp.dot(heads, w_output, preferred_element_type=jnp.float32)
        mine = scatter_sum(partial_out, "gy", size_y, jnp.bfloat16)
        count = mine.shape[0]
        residual = lax.dynamic_slice_in_dim(inputs, lax.axis_index("gy") * count, count, 0)
        return gather((mine + residual.astype(jnp.float32)).astype(jnp.bfloat16), "gy", size_y)

    placed = (
        P("groups", "gx"),
        P("gx"),
        P("gx", "gy"),
        P("gx", "gy"),
        P("gx", "gy"),
        P("gy", "gx"),
        P(("groups", "gx"), None, "gy"),
        P(("groups", "gx"), None, "gy"),
        P(("groups", "gx")),
    )
    return jax.shard_map(
        shards, mesh=mesh, in_specs=placed, out_specs=P("groups", "gx"), check_vma=False
    )
```

```python
import functools

import jax
import jax.numpy as jnp
from jax import lax
from jax.experimental import pallas as pl
from jax.experimental.pallas import tpu as pltpu
from jax.sharding import PartitionSpec as P

HD = 128
EPS = 1e-05
ROPE_BASE = 500000.0
CHUNK = 256
F32 = jnp.float32
BF16 = jnp.bfloat16

ANY = pl.BlockSpec(memory_space=pl.ANY)
VMEM = pl.BlockSpec(memory_space=pltpu.VMEM)
SMEM = pl.BlockSpec(memory_space=pltpu.SMEM)
MIB = 1 << 20


def columns(index, width):
    return pl.ds(pl.multiple_of(index * width, HD), width)


def params(mib):
    return pltpu.CompilerParams(vmem_limit_bytes=mib * MIB)


def cost(flops, nbytes):
    return pl.CostEstimate(flops=flops, bytes_accessed=nbytes, transcendentals=0)


def in_vmem(value):
    return pltpu.with_memory_space_constraint(value, pltpu.VMEM)


def in_hbm(value):
    return pltpu.with_memory_space_constraint(value, pltpu.HBM)


def project(size, x_hbm, gain_hbm, wq_hbm, wk_hbm, wv_hbm, *refs):
    outs = refs[:size]
    x, gain, wq, wk, wv, scaled, total, sems = refs[size:]
    depth = x.shape[1]
    steps = depth // CHUNK
    pairs = [(x_hbm, x), (gain_hbm, gain), (wk_hbm, wk), (wv_hbm, wv)]
    small = [pltpu.make_async_copy(a, b, sems.at[steps + i]) for i, (a, b) in enumerate(pairs)]
    large = []
    for step in range(steps):
        part = pl.ds(step * CHUNK, CHUNK)
        large.append(pltpu.make_async_copy(wq_hbm.at[part], wq.at[part], sems.at[step]))
    small[0].start()
    small[1].start()
    for copy in large[:2]:
        copy.start()
    small[2].start()
    small[3].start()
    for copy in large[2:]:
        copy.start()
    small[0].wait()
    small[1].wait()
    wide = x[...].astype(F32)
    scaled[...] = (wide * gain[...]).astype(BF16)
    squares = jnp.sum(wide * wide, 1, keepdims=True)
    width = wq.shape[1]
    dot = functools.partial(jnp.dot, preferred_element_type=F32)
    for step, copy in enumerate(large):
        copy.wait()
        part = slice(step * CHUNK, (step + 1) * CHUNK)
        term = dot(scaled[:, part], wq[part])
        if step == 0:
            total[:, :width] = term
        else:
            total[:, :width] += term
        if step == 1:
            small[2].wait()
            total[:, width : width + HD] = dot(scaled[...], wk[...])
            small[3].wait()
            total[:, width + HD : width + 2 * HD] = dot(scaled[...], wv[...])
            total[:, width + 2 * HD :] = jnp.broadcast_to(squares, (squares.shape[0], HD))
    rows = outs[0].shape[0]
    me = lax.axis_index("gx")
    for mask in range(size):
        start = pl.multiple_of((me ^ mask) * rows, 8)
        outs[mask][...] = total[pl.ds(start, rows), :].astype(outs[mask].dtype)


def fetch_pieces(masks, width, w_hbm, pieces, sems, first):
    me = lax.axis_index("gy")
    copies = []
    for i, mask in enumerate(masks):
        source = w_hbm.at[:, columns(me ^ mask, width)]
        copies.append(pltpu.make_async_copy(source, pieces[i], sems.at[first + i]))
    return copies


def fetch_caches(masks, after, k_hbm, v_hbm, w_hbm, k, v, *refs):
    del after
    *pieces, sems = refs
    copies = [
        pltpu.make_async_copy(k_hbm, k, sems.at[0]),
        pltpu.make_async_copy(v_hbm, v, sems.at[1]),
    ]
    copies += fetch_pieces(masks, pieces[0].shape[1], w_hbm, pieces, sems, 2)
    for copy in copies:
        copy.start()
    for copy in copies:
        copy.wait()


def fetch_weights(masks, after, x_hbm, w_hbm, x, *refs):
    del after
    *pieces, sems = refs
    width = x.shape[1]
    copies = [
        pltpu.make_async_copy(x_hbm.at[:, columns(lax.axis_index("gy"), width)], x, sems.at[0])
    ]
    copies += fetch_pieces(masks, width, w_hbm, pieces, sems, 1)
    for copy in copies:
        copy.start()
    for copy in copies:
        copy.wait()


def attention(size, model, masks, lengths, cosine, sine, k, v, w_hbm, *refs):
    arrived = refs[:size]
    heads = refs[size]
    pieces = refs[size + 1 : size + 1 + len(masks)]
    q_rows, o_rows, sems = refs[size + 1 + len(masks) :]
    copies = fetch_pieces(masks, pieces[0].shape[1], w_hbm, pieces, sems, 0) if masks else []
    for copy in copies:
        copy.start()
    rows, slots = k.shape[0], k.shape[1]
    group = heads.shape[1] // HD
    width = group * HD
    summed = arrived[0][...]
    for item in arrived[1:]:
        summed = summed + item[...].astype(F32)
    scale = lax.rsqrt(summed[:, width + 2 * HD :] / model + EPS)
    cosines, sines = cosine[...], sine[...]

    def turn(value):
        return value * cosines + pltpu.roll(value, HD // 2, 1) * sines

    for head in range(group):
        part = summed[:, head * HD : (head + 1) * HD] * scale
        q_rows[head] = turn(part).astype(BF16).astype(F32)
    new_keys = turn(summed[:, width : width + HD] * scale).astype(BF16).astype(F32)
    new_values = (summed[:, width + HD : width + 2 * HD] * scale).astype(BF16).astype(F32)
    factor = HD ** (-0.5)
    slot = lax.broadcasted_iota(jnp.int32, (group, slots), 1)
    for row in range(rows):
        queries = q_rows[:, row, :]
        scores = (
            lax.dot_general(
                queries.astype(BF16), k[row], (((1,), (1,)), ((), ())), preferred_element_type=F32
            )
            * factor
        )
        own = jnp.sum(queries * new_keys[row : row + 1], 1, keepdims=True) * factor
        scores = jnp.where(slot < lengths[row], scores, -jnp.inf)
        top = jnp.maximum(jnp.max(scores, 1, keepdims=True), own)
        probs = jnp.exp(scores - top)
        own_prob = jnp.exp(own - top)
        share = 1.0 / (jnp.sum(probs, 1, keepdims=True) + own_prob)
        weights = (probs * share).astype(BF16)
        own_weight = (own_prob * share).astype(BF16).astype(F32)
        mixed = jnp.dot(weights, v[row], preferred_element_type=F32)
        o_rows[:, row, :] = mixed + own_weight * new_values[row : row + 1]
    for head in range(group):
        heads[:, head * HD : (head + 1) * HD] = o_rows[head].astype(BF16)
    for copy in copies:
        copy.wait()


def project_out(size, w, *refs):
    blocks, out, gathered = refs[:size], refs[size], refs[size + 1]
    me = lax.axis_index("gx")
    rows = blocks[0].shape[0]
    for mask in range(size):
        gathered[pl.ds(pl.multiple_of((me ^ mask) * rows, 8), rows), :] = blocks[mask][...].astype(F32)
    out[...] = jnp.dot(
        gathered[...].astype(BF16), w[...], preferred_element_type=F32
    ).astype(out.dtype)


def finish(x, own, *refs):
    *arrived, out = refs
    total = own[...]
    for item in arrived:
        total = total + item[...].astype(F32)
    out[...] = (x[...].astype(F32) + total).astype(BF16)


def assemble(size, *refs):
    blocks, out, sems = refs[:size], refs[size], refs[size + 1]
    me = lax.axis_index("gy")
    width = blocks[0].shape[1]
    copies = []
    for mask in range(size):
        target = out.at[:, columns(me ^ mask, width)]
        copies.append(pltpu.make_async_copy(blocks[mask], target, sems.at[mask]))
    for copy in copies:
        copy.start()
    for copy in copies:
        copy.wait()


def swap(value, axis, size, mask):
    return lax.ppermute(value, axis, [(i, i ^ mask) for i in range(size)])


def solution(mesh):
    size_x = mesh.shape["gx"]
    size_y = mesh.shape["gy"]
    struct = jax.ShapeDtypeStruct
    sems = lambda n: pltpu.SemaphoreType.DMA((n,))
    order = list(range(size_y - 1, -1, -1))
    quarter = max(size_y // 4, 1)
    early, middle, late = order[:quarter], order[quarter : 2 * quarter], order[2 * quarter :]

    def shards(inputs, gain, w_query, w_key, w_value, w_output, key_cache, value_cache, lengths):
        batch, depth = inputs.shape
        width = w_query.shape[1]
        rows = key_cache.shape[0]
        packed = width + 3 * HD
        block = w_output.shape[1] // size_y
        piece = pltpu.VMEM((width, block), BF16)
        piece_bytes = 2 * width * block

        sums = pl.pallas_call(
            functools.partial(project, size_x),
            out_shape=[pltpu.VMEM((rows, packed), F32)] * size_x,
            in_specs=[ANY] * 5,
            out_specs=[VMEM] * size_x,
            scratch_shapes=[
                pltpu.VMEM(inputs.shape, BF16),
                pltpu.VMEM((1, depth), F32),
                pltpu.VMEM(w_query.shape, BF16),
                pltpu.VMEM(w_key.shape, BF16),
                pltpu.VMEM(w_value.shape, BF16),
                pltpu.VMEM(inputs.shape, BF16),
                pltpu.VMEM((batch, packed), F32),
                sems(depth // CHUNK + 4),
            ],
            compiler_params=params(28),
            cost_estimate=cost(2 * batch * depth * packed, 2 * depth * packed),
            name="project",
        )(*[in_hbm(a) for a in (inputs, gain.reshape(1, depth), w_query, w_key, w_value)])
        arrived = [sums[0]] + [swap(sums[m], "gx", size_x, m) for m in range(1, size_x)]

        fetched = pl.pallas_call(
            functools.partial(fetch_caches, early),
            out_shape=[pltpu.VMEM(key_cache.shape, BF16), pltpu.VMEM(value_cache.shape, BF16)]
            + [piece] * len(early),
            in_specs=[ANY] * 4,
            out_specs=[VMEM] * (2 + len(early)),
            scratch_shapes=[sems(2 + len(early))],
            compiler_params=params(4),
            cost_estimate=cost(0, 4 * key_cache.size + piece_bytes * len(early)),
            name="fetch_caches",
        )(sums[0], in_hbm(key_cache), in_hbm(value_cache), in_hbm(w_output))
        keys, values, *pieces = fetched

        half = HD // 2
        inverse = ROPE_BASE ** (-(jnp.arange(half, dtype=F32) * 2.0 / HD))
        angles = lengths.astype(F32)[:, None] * inverse[None, :]
        cosine, sine = jnp.cos(angles), jnp.sin(angles)
        heads, *more = pl.pallas_call(
            functools.partial(attention, size_x, depth * size_x, middle),
            out_shape=[pltpu.VMEM((rows, width), BF16)] + [piece] * len(middle),
            in_specs=[SMEM, VMEM, VMEM, VMEM, VMEM, ANY] + [VMEM] * size_x,
            out_specs=[VMEM] * (1 + len(middle)),
            scratch_shapes=[
                pltpu.VMEM((width // HD, rows, HD), F32),
                pltpu.VMEM((width // HD, rows, HD), F32),
                sems(max(len(middle), 1)),
            ],
            compiler_params=params(8),
            cost_estimate=cost(4 * key_cache.size * (width // HD), piece_bytes * len(middle)),
            name="attention",
        )(
            lengths,
            jnp.concatenate([cosine, cosine], 1),
            jnp.concatenate([-sine, sine], 1),
            in_vmem(keys),
            in_vmem(values),
            in_hbm(w_output),
            *[in_vmem(a) for a in arrived],
        )
        pieces += more
        gathered = [heads] + [swap(heads, "gx", size_x, m) for m in range(1, size_x)]

        residual, *more = pl.pallas_call(
            functools.partial(fetch_weights, late),
            out_shape=[pltpu.VMEM((batch, block), BF16)] + [piece] * len(late),
            in_specs=[ANY] * 3,
            out_specs=[VMEM] * (1 + len(late)),
            scratch_shapes=[sems(1 + len(late))],
            compiler_params=params(4),
            cost_estimate=cost(0, piece_bytes * len(late)),
            name="fetch_weights",
        )(heads, in_hbm(inputs), in_hbm(w_output))
        pieces += more

        terms = {}
        for mask, w in zip(order, pieces):
            kind = BF16 if mask else F32
            term = pl.pallas_call(
                functools.partial(project_out, size_x),
                out_shape=pltpu.VMEM((batch, block), kind),
                in_specs=[VMEM] * (1 + size_x),
                out_specs=VMEM,
                scratch_shapes=[pltpu.VMEM((batch, width), F32)],
                compiler_params=params(8),
                cost_estimate=cost(2 * batch * width * block, piece_bytes),
                name="project_out",
            )(in_vmem(w), *[in_vmem(a) for a in gathered])
            terms[mask] = swap(term, "gy", size_y, mask) if mask else term
        done = pl.pallas_call(
            finish,
            out_shape=pltpu.VMEM((batch, block), BF16),
            in_specs=[VMEM] * (1 + size_y),
            out_specs=VMEM,
            compiler_params=params(4),
            name="finish",
        )(in_vmem(residual), *[in_vmem(terms[m]) for m in range(size_y)])
        blocks = [done] + [swap(done, "gy", size_y, m) for m in range(1, size_y)]
        return pl.pallas_call(
            functools.partial(assemble, size_y),
            out_shape=struct((batch, block * size_y), BF16),
            in_specs=[VMEM] * size_y,
            out_specs=ANY,
            scratch_shapes=[sems(size_y)],
            compiler_params=params(4),
            name="assemble",
        )(*[in_vmem(b) for b in blocks])

    placed = (
        P("groups", "gx"),
        P("gx"),
        P("gx", "gy"),
        P("gx", "gy"),
        P("gx", "gy"),
        P("gy", "gx"),
        P(("groups", "gx"), None, "gy"),
        P(("groups", "gx"), None, "gy"),
        P(("groups", "gx")),
    )
    return jax.shard_map(
        shards, mesh=mesh, in_specs=placed, out_specs=P("groups", "gx"), check_vma=False
    )
```

```python
import functools
import math

import jax
import jax.numpy as jnp
from jax import lax
from jax.experimental import pallas as pl
from jax.experimental.pallas import tpu as pltpu
from jax.sharding import PartitionSpec as P

HD = 128
EPS = 1e-05
ROPE_BASE = 500000.0
CHUNK = 256
F32 = jnp.float32
BF16 = jnp.bfloat16

ANY = pl.BlockSpec(memory_space=pl.ANY)
VMEM = pl.BlockSpec(memory_space=pltpu.VMEM)
SMEM = pl.BlockSpec(memory_space=pltpu.SMEM)
MIB = 1 << 20


def columns(index, width):
    return pl.ds(pl.multiple_of(index * width, HD), width)


def params(mib):
    return pltpu.CompilerParams(vmem_limit_bytes=mib * MIB)


def cost(flops, nbytes):
    return pl.CostEstimate(flops=flops, bytes_accessed=nbytes, transcendentals=0)


def in_vmem(value):
    return pltpu.with_memory_space_constraint(value, pltpu.VMEM)


def in_hbm(value):
    return pltpu.with_memory_space_constraint(value, pltpu.HBM)


def project(size, x_hbm, gain_hbm, wq_hbm, wk_hbm, wv_hbm, *refs):
    outs = refs[:size]
    x, gain, wq, wk, wv, scaled, total, sems = refs[size:]
    depth = x.shape[1]
    steps = depth // CHUNK
    pairs = [(x_hbm, x), (gain_hbm, gain), (wk_hbm, wk), (wv_hbm, wv)]
    small = [pltpu.make_async_copy(a, b, sems.at[steps + i]) for i, (a, b) in enumerate(pairs)]
    large = []
    for step in range(steps):
        part = pl.ds(step * CHUNK, CHUNK)
        large.append(pltpu.make_async_copy(wq_hbm.at[part], wq.at[part], sems.at[step]))
    small[0].start()
    small[1].start()
    for copy in large[:2]:
        copy.start()
    small[2].start()
    small[3].start()
    for copy in large[2:]:
        copy.start()
    small[0].wait()
    small[1].wait()
    wide = x[...].astype(F32)
    scaled[...] = (wide * gain[...]).astype(BF16)
    squares = jnp.sum(wide * wide, 1, keepdims=True)
    width = wq.shape[1]
    dot = functools.partial(jnp.dot, preferred_element_type=F32)
    for step, copy in enumerate(large):
        copy.wait()
        part = slice(step * CHUNK, (step + 1) * CHUNK)
        term = dot(scaled[:, part], wq[part])
        if step == 0:
            total[:, :width] = term
        else:
            total[:, :width] += term
        if step == 1:
            small[2].wait()
            total[:, width : width + HD] = dot(scaled[...], wk[...])
            small[3].wait()
            total[:, width + HD : width + 2 * HD] = dot(scaled[...], wv[...])
            total[:, width + 2 * HD :] = jnp.broadcast_to(squares, (squares.shape[0], HD))
    rows = outs[0].shape[0]
    me = lax.axis_index("gx")
    for mask in range(size):
        start = pl.multiple_of((me ^ mask) * rows, 8)
        outs[mask][...] = total[pl.ds(start, rows), :].astype(outs[mask].dtype)


def fetch_pieces(masks, width, w_hbm, pieces, sems, first):
    me = lax.axis_index("gy")
    copies = []
    for i, mask in enumerate(masks):
        source = w_hbm.at[:, columns(me ^ mask, width)]
        copies.append(pltpu.make_async_copy(source, pieces[i], sems.at[first + i]))
    return copies


def fetch_caches(masks, after, k_hbm, v_hbm, w_hbm, k, v, *refs):
    del after
    *pieces, sems = refs
    copies = [
        pltpu.make_async_copy(k_hbm, k, sems.at[0]),
        pltpu.make_async_copy(v_hbm, v, sems.at[1]),
    ]
    if masks:
        copies += fetch_pieces(masks, pieces[0].shape[1], w_hbm, pieces, sems, 2)
    for copy in copies:
        copy.start()
    for copy in copies:
        copy.wait()


def fetch_weights(masks, after, x_hbm, w_hbm, x, *refs):
    del after
    *pieces, sems = refs
    width = x.shape[1]
    copies = [
        pltpu.make_async_copy(x_hbm.at[:, columns(lax.axis_index("gy"), width)], x, sems.at[0])
    ]
    copies += fetch_pieces(masks, width, w_hbm, pieces, sems, 1)
    for copy in copies:
        copy.start()
    for copy in copies:
        copy.wait()


def attention(size, model, masks, lengths, cosine, sine, k, v, w_hbm, *refs):
    arrived = refs[:size]
    heads = refs[size]
    pieces = refs[size + 1 : size + 1 + len(masks)]
    q_rows, o_rows, scores, sems = refs[size + 1 + len(masks) :]
    copies = fetch_pieces(masks, pieces[0].shape[1], w_hbm, pieces, sems, 0) if masks else []
    for copy in copies:
        copy.start()
    rows, slots = k.shape[0], k.shape[1]
    group = heads.shape[1] // HD
    width = group * HD
    summed = arrived[0][...]
    for item in arrived[1:]:
        summed = summed + item[...].astype(F32)
    scale = lax.rsqrt(summed[:, width + 2 * HD :] / model + EPS)
    cosines, sines = cosine[...], sine[...]

    def turn(value):
        return value * cosines + pltpu.roll(value, HD // 2, 1) * sines

    for head in range(group):
        part = summed[:, head * HD : (head + 1) * HD] * scale
        q_rows[head] = turn(part).astype(BF16).astype(F32)
    new_keys = turn(summed[:, width : width + HD] * scale).astype(BF16).astype(F32)
    new_values = (summed[:, width + HD : width + 2 * HD] * scale).astype(BF16).astype(F32)
    rate = HD ** (-0.5) * math.log2(math.e)
    half = slots // 2
    slot = lax.broadcasted_iota(jnp.int32, (group, half), 1) + half
    own, top = [], []
    for row in range(rows):
        queries = q_rows[:, row, :]
        mine = slice(row * group, (row + 1) * group)
        raw = lax.dot_general(
            queries.astype(BF16), k[row], (((1,), (1,)), ((), ())), preferred_element_type=F32
        )
        low = raw[:, :half]
        high = jnp.where(slot < lengths[row], raw[:, half:], -jnp.inf)
        scores[mine, :half] = low
        scores[mine, half:] = high
        own.append(jnp.sum(queries * new_keys[row : row + 1], 1, keepdims=True))
        top.append(jnp.maximum(jnp.max(jnp.maximum(low, high), 1, keepdims=True), own[row]))

    def soften(row):
        probs = jnp.exp2((scores[row * group : (row + 1) * group] - top[row]) * rate)
        own_prob = jnp.exp2((own[row] - top[row]) * rate)
        share = 1.0 / (jnp.sum(probs, 1, keepdims=True) + own_prob)
        return probs.astype(BF16), own_prob, share

    ready = soften(0)
    for row in range(rows):
        probs, own_prob, share = ready
        if row + 1 < rows:
            ready = soften(row + 1)
        mixed = jnp.dot(probs, v[row], preferred_element_type=F32)
        o_rows[:, row, :] = (mixed + own_prob * new_values[row : row + 1]) * share
    for head in range(group):
        heads[:, head * HD : (head + 1) * HD] = o_rows[head].astype(BF16)
    for copy in copies:
        copy.wait()


def project_out(size, w, *refs):
    blocks, out, gathered = refs[:size], refs[size], refs[size + 1]
    me = lax.axis_index("gx")
    rows = blocks[0].shape[0]
    for mask in range(size):
        gathered[pl.ds(pl.multiple_of((me ^ mask) * rows, 8), rows), :] = blocks[mask][...].astype(F32)
    out[...] = jnp.dot(
        gathered[...].astype(BF16), w[...], preferred_element_type=F32
    ).astype(out.dtype)


def finish(x, own, *refs):
    *arrived, out = refs
    total = own[...]
    for item in arrived:
        total = total + item[...].astype(F32)
    out[...] = (x[...].astype(F32) + total).astype(BF16)


def assemble(size, *refs):
    blocks, out, sems = refs[:size], refs[size], refs[size + 1]
    me = lax.axis_index("gy")
    width = blocks[0].shape[1]
    copies = []
    for mask in range(size):
        target = out.at[:, columns(me ^ mask, width)]
        copies.append(pltpu.make_async_copy(blocks[mask], target, sems.at[mask]))
    for copy in copies:
        copy.start()
    for copy in copies:
        copy.wait()


def swap(value, axis, size, mask):
    return lax.ppermute(value, axis, [(i, i ^ mask) for i in range(size)])


def solution(mesh):
    size_x = mesh.shape["gx"]
    size_y = mesh.shape["gy"]
    struct = jax.ShapeDtypeStruct
    sems = lambda n: pltpu.SemaphoreType.DMA((n,))
    order = list(range(size_y - 1, -1, -1))
    quarter = max(size_y // 4, 1)
    early, middle, late = [], order[: 2 * quarter], order[2 * quarter :]

    def shards(inputs, gain, w_query, w_key, w_value, w_output, key_cache, value_cache, lengths):
        batch, depth = inputs.shape
        width = w_query.shape[1]
        rows = key_cache.shape[0]
        packed = width + 3 * HD
        block = w_output.shape[1] // size_y
        piece = pltpu.VMEM((width, block), BF16)
        piece_bytes = 2 * width * block

        sums = pl.pallas_call(
            functools.partial(project, size_x),
            out_shape=[pltpu.VMEM((rows, packed), F32)] * size_x,
            in_specs=[ANY] * 5,
            out_specs=[VMEM] * size_x,
            scratch_shapes=[
                pltpu.VMEM(inputs.shape, BF16),
                pltpu.VMEM((1, depth), F32),
                pltpu.VMEM(w_query.shape, BF16),
                pltpu.VMEM(w_key.shape, BF16),
                pltpu.VMEM(w_value.shape, BF16),
                pltpu.VMEM(inputs.shape, BF16),
                pltpu.VMEM((batch, packed), F32),
                sems(depth // CHUNK + 4),
            ],
            compiler_params=params(28),
            cost_estimate=cost(2 * batch * depth * packed, 2 * depth * packed),
            name="project",
        )(*[in_hbm(a) for a in (inputs, gain.reshape(1, depth), w_query, w_key, w_value)])
        arrived = [sums[0]] + [swap(sums[m], "gx", size_x, m) for m in range(1, size_x)]

        fetched = pl.pallas_call(
            functools.partial(fetch_caches, early),
            out_shape=[pltpu.VMEM(key_cache.shape, BF16), pltpu.VMEM(value_cache.shape, BF16)]
            + [piece] * len(early),
            in_specs=[ANY] * 4,
            out_specs=[VMEM] * (2 + len(early)),
            scratch_shapes=[sems(2 + len(early))],
            compiler_params=params(4),
            cost_estimate=cost(0, 4 * key_cache.size + piece_bytes * len(early)),
            name="fetch_caches",
        )(sums[0], in_hbm(key_cache), in_hbm(value_cache), in_hbm(w_output))
        keys, values, *pieces = fetched

        half = HD // 2
        inverse = ROPE_BASE ** (-(jnp.arange(half, dtype=F32) * 2.0 / HD))
        angles = lengths.astype(F32)[:, None] * inverse[None, :]
        cosine, sine = jnp.cos(angles), jnp.sin(angles)
        heads, *more = pl.pallas_call(
            functools.partial(attention, size_x, depth * size_x, middle),
            out_shape=[pltpu.VMEM((rows, width), BF16)] + [piece] * len(middle),
            in_specs=[SMEM, VMEM, VMEM, VMEM, VMEM, ANY] + [VMEM] * size_x,
            out_specs=[VMEM] * (1 + len(middle)),
            scratch_shapes=[
                pltpu.VMEM((width // HD, rows, HD), F32),
                pltpu.VMEM((width // HD, rows, HD), F32),
                pltpu.VMEM((rows * (width // HD), key_cache.shape[1]), F32),
                sems(max(len(middle), 1)),
            ],
            compiler_params=params(8),
            cost_estimate=cost(4 * key_cache.size * (width // HD), piece_bytes * len(middle)),
            name="attention",
        )(
            lengths,
            jnp.concatenate([cosine, cosine], 1),
            jnp.concatenate([-sine, sine], 1),
            in_vmem(keys),
            in_vmem(values),
            in_hbm(w_output),
            *[in_vmem(a) for a in arrived],
        )
        pieces += more
        gathered = [heads] + [swap(heads, "gx", size_x, m) for m in range(1, size_x)]

        residual, *more = pl.pallas_call(
            functools.partial(fetch_weights, late),
            out_shape=[pltpu.VMEM((batch, block), BF16)] + [piece] * len(late),
            in_specs=[ANY] * 3,
            out_specs=[VMEM] * (1 + len(late)),
            scratch_shapes=[sems(1 + len(late))],
            compiler_params=params(4),
            cost_estimate=cost(0, piece_bytes * len(late)),
            name="fetch_weights",
        )(heads, in_hbm(inputs), in_hbm(w_output))
        pieces += more

        terms = {}
        for mask, w in zip(order, pieces):
            kind = BF16 if mask else F32
            term = pl.pallas_call(
                functools.partial(project_out, size_x),
                out_shape=pltpu.VMEM((batch, block), kind),
                in_specs=[VMEM] * (1 + size_x),
                out_specs=VMEM,
                scratch_shapes=[pltpu.VMEM((batch, width), F32)],
                compiler_params=params(8),
                cost_estimate=cost(2 * batch * width * block, piece_bytes),
                name="project_out",
            )(in_vmem(w), *[in_vmem(a) for a in gathered])
            terms[mask] = swap(term, "gy", size_y, mask) if mask else term
        done = pl.pallas_call(
            finish,
            out_shape=pltpu.VMEM((batch, block), BF16),
            in_specs=[VMEM] * (1 + size_y),
            out_specs=VMEM,
            compiler_params=params(4),
            name="finish",
        )(in_vmem(residual), *[in_vmem(terms[m]) for m in range(size_y)])
        blocks = [done] + [swap(done, "gy", size_y, m) for m in range(1, size_y)]
        return pl.pallas_call(
            functools.partial(assemble, size_y),
            out_shape=struct((batch, block * size_y), BF16),
            in_specs=[VMEM] * size_y,
            out_specs=ANY,
            scratch_shapes=[sems(size_y)],
            compiler_params=params(4),
            name="assemble",
        )(*[in_vmem(b) for b in blocks])

    placed = (
        P("groups", "gx"),
        P("gx"),
        P("gx", "gy"),
        P("gx", "gy"),
        P("gx", "gy"),
        P("gy", "gx"),
        P(("groups", "gx"), None, "gy"),
        P(("groups", "gx"), None, "gy"),
        P(("groups", "gx")),
    )
    return jax.shard_map(
        shards, mesh=mesh, in_specs=placed, out_specs=P("groups", "gx"), check_vma=False
    )
```

```python
import functools
import math

import jax
import jax.numpy as jnp
from jax import lax
from jax.experimental import pallas as pl
from jax.experimental.pallas import tpu as pltpu
from jax.sharding import PartitionSpec as P

HD = 128
EPS = 1e-05
ROPE_BASE = 500000.0
CHUNK = 256
F32 = jnp.float32
BF16 = jnp.bfloat16

ANY = pl.BlockSpec(memory_space=pl.ANY)
VMEM = pl.BlockSpec(memory_space=pltpu.VMEM)
SMEM = pl.BlockSpec(memory_space=pltpu.SMEM)
MIB = 1 << 20


def columns(index, width):
    return pl.ds(pl.multiple_of(index * width, HD), width)


def params(mib):
    return pltpu.CompilerParams(vmem_limit_bytes=mib * MIB)


def cost(flops, nbytes):
    return pl.CostEstimate(flops=flops, bytes_accessed=nbytes, transcendentals=0)


def in_vmem(value):
    return pltpu.with_memory_space_constraint(value, pltpu.VMEM)


def in_hbm(value):
    return pltpu.with_memory_space_constraint(value, pltpu.HBM)


def project(size, x_hbm, gain_hbm, wq_hbm, wk_hbm, wv_hbm, *refs):
    outs = refs[:size]
    x, gain, wq, wk, wv, scaled, total, sems = refs[size:]
    depth = x.shape[1]
    steps = depth // CHUNK
    pairs = [(x_hbm, x), (gain_hbm, gain), (wk_hbm, wk), (wv_hbm, wv)]
    small = [pltpu.make_async_copy(a, b, sems.at[steps + i]) for i, (a, b) in enumerate(pairs)]
    large = []
    for step in range(steps):
        part = pl.ds(step * CHUNK, CHUNK)
        large.append(pltpu.make_async_copy(wq_hbm.at[part], wq.at[part], sems.at[step]))
    small[0].start()
    small[1].start()
    for copy in large[:2]:
        copy.start()
    small[2].start()
    small[3].start()
    for copy in large[2:]:
        copy.start()
    small[0].wait()
    small[1].wait()
    wide = x[...].astype(F32)
    scaled[...] = (wide * gain[...]).astype(BF16)
    squares = jnp.sum(wide * wide, 1, keepdims=True)
    width = wq.shape[1]
    dot = functools.partial(jnp.dot, preferred_element_type=F32)
    for step, copy in enumerate(large):
        copy.wait()
        part = slice(step * CHUNK, (step + 1) * CHUNK)
        term = dot(scaled[:, part], wq[part])
        if step == 0:
            total[:, :width] = term
        else:
            total[:, :width] += term
        if step == 1:
            small[2].wait()
            total[:, width : width + HD] = dot(scaled[...], wk[...])
            small[3].wait()
            total[:, width + HD : width + 2 * HD] = dot(scaled[...], wv[...])
            total[:, width + 2 * HD :] = jnp.broadcast_to(squares, (squares.shape[0], HD))
    rows = outs[0].shape[0]
    me = lax.axis_index("gx")
    for mask in range(size):
        start = pl.multiple_of((me ^ mask) * rows, 8)
        outs[mask][...] = total[pl.ds(start, rows), :].astype(outs[mask].dtype)


def fetch_pieces(masks, width, w_hbm, pieces, sems, first):
    me = lax.axis_index("gy")
    copies = []
    for i, mask in enumerate(masks):
        source = w_hbm.at[:, columns(me ^ mask, width)]
        copies.append(pltpu.make_async_copy(source, pieces[i], sems.at[first + i]))
    return copies


def fetch_caches(masks, after, k_hbm, v_hbm, w_hbm, k, v, *refs):
    del after
    *pieces, sems = refs
    copies = [
        pltpu.make_async_copy(k_hbm, k, sems.at[0]),
        pltpu.make_async_copy(v_hbm, v, sems.at[1]),
    ]
    if masks:
        copies += fetch_pieces(masks, pieces[0].shape[1], w_hbm, pieces, sems, 2)
    for copy in copies:
        copy.start()
    for copy in copies:
        copy.wait()


def fetch_weights(masks, after, x_hbm, w_hbm, x, *refs):
    del after
    *pieces, sems = refs
    width = x.shape[1]
    copies = [
        pltpu.make_async_copy(x_hbm.at[:, columns(lax.axis_index("gy"), width)], x, sems.at[0])
    ]
    copies += fetch_pieces(masks, width, w_hbm, pieces, sems, 1)
    for copy in copies:
        copy.start()
    for copy in copies:
        copy.wait()


def attention(size, model, masks, lengths, cosine, sine, k, v, w_hbm, *refs):
    arrived = refs[:size]
    heads = refs[size]
    pieces = refs[size + 1 : size + 1 + len(masks)]
    q_rows, o_rows, blocks, scores, weights, sems = refs[size + 1 + len(masks) :]
    copies = fetch_pieces(masks, pieces[0].shape[1], w_hbm, pieces, sems, 0) if masks else []
    for copy in copies:
        copy.start()
    rows, slots = k.shape[0], k.shape[1]
    group = heads.shape[1] // HD
    width = group * HD
    lanes = rows * group
    summed = arrived[0][...]
    for item in arrived[1:]:
        summed = summed + item[...].astype(F32)
    scale = lax.rsqrt(summed[:, width + 2 * HD :] / model + EPS)
    cosines, sines = cosine[...], sine[...]

    def turn(value):
        return value * cosines + pltpu.roll(value, HD // 2, 1) * sines

    for head in range(group):
        part = summed[:, head * HD : (head + 1) * HD] * scale
        q_rows[head] = turn(part)
    new_keys = turn(summed[:, width : width + HD] * scale).astype(BF16)
    new_values = (summed[:, width + HD : width + 2 * HD] * scale).astype(BF16).astype(F32)
    queries = jnp.concatenate([q_rows[:, row, :] for row in range(rows)], 0).T.astype(BF16)

    owner = lax.broadcasted_iota(jnp.int32, (1, lanes), 1) // group
    limits = jnp.zeros((1, lanes), jnp.int32)
    for row in range(rows):
        limits = jnp.where(owner == row, lengths[row], limits)
        blocks[row * HD : (row + 1) * HD] = jnp.where(owner == row, queries, 0).astype(BF16)
    flat = jnp.concatenate([new_keys[row : row + 1] for row in range(rows)], 1)
    own = jnp.dot(
        jnp.broadcast_to(flat.astype(F32), (16, rows * HD)).astype(BF16),
        blocks[...],
        preferred_element_type=F32,
    )[:1]

    rate = HD ** (-0.5) * math.log2(math.e)
    top = jnp.full((8, lanes), -jnp.inf, F32)
    slot = lax.broadcasted_iota(jnp.int32, (CHUNK, lanes), 0)
    for start in range(0, slots, CHUNK):
        part = slice(start, start + CHUNK)
        keys = jnp.concatenate([k[row, part] for row in range(rows)], 1)
        raw = jnp.dot(keys, blocks[...], preferred_element_type=F32)
        if start + CHUNK > slots // 2:
            raw = jnp.where(slot + start < limits, raw, -jnp.inf)
        scores[part] = raw
        top = jnp.maximum(top, jnp.max(raw.reshape(CHUNK // 8, 8, lanes), 0))
    top = jnp.maximum(jnp.max(top, 0, keepdims=True), own)
    total = jnp.zeros((8, lanes), F32)
    for start in range(0, slots, CHUNK):
        part = slice(start, start + CHUNK)
        probs = jnp.exp2((scores[part] - top) * rate)
        total = total + jnp.sum(probs.reshape(CHUNK // 8, 8, lanes), 0)
        weights[:, part] = probs.T.astype(BF16)
    own_prob = jnp.exp2((own - top) * rate)
    share = 1.0 / (jnp.sum(total, 0, keepdims=True) + own_prob)
    tall = jnp.concatenate([share, own_prob * share, jnp.zeros((6, lanes), F32)], 0).T
    for row in range(0, rows, 2):
        pair = slice(row * group, (row + 2) * group)
        both = jnp.concatenate([v[row], v[row + 1]], 1)
        mixed = jnp.dot(weights[pair], both, preferred_element_type=F32)
        for side in range(2):
            mine = slice((row + side) * group, (row + side + 1) * group)
            value = mixed[side * group : (side + 1) * group, side * HD : (side + 1) * HD]
            extra = tall[mine, 1:2] * new_values[row + side : row + side + 1]
            o_rows[:, row + side, :] = value * tall[mine, :1] + extra
    for head in range(group):
        heads[:, head * HD : (head + 1) * HD] = o_rows[head].astype(BF16)
    for copy in copies:
        copy.wait()


def project_out(size, w, *refs):
    blocks, out, gathered = refs[:size], refs[size], refs[size + 1]
    me = lax.axis_index("gx")
    rows = blocks[0].shape[0]
    for mask in range(size):
        gathered[pl.ds(pl.multiple_of((me ^ mask) * rows, 8), rows), :] = blocks[mask][...].astype(F32)
    out[...] = jnp.dot(
        gathered[...].astype(BF16), w[...], preferred_element_type=F32
    ).astype(out.dtype)


def finish(x, own, *refs):
    *arrived, out = refs
    total = own[...]
    for item in arrived:
        total = total + item[...].astype(F32)
    out[...] = (x[...].astype(F32) + total).astype(BF16)


def assemble(size, *refs):
    blocks, out, sems = refs[:size], refs[size], refs[size + 1]
    me = lax.axis_index("gy")
    width = blocks[0].shape[1]
    copies = []
    for mask in range(size):
        target = out.at[:, columns(me ^ mask, width)]
        copies.append(pltpu.make_async_copy(blocks[mask], target, sems.at[mask]))
    for copy in copies:
        copy.start()
    for copy in copies:
        copy.wait()


def swap(value, axis, size, mask):
    return lax.ppermute(value, axis, [(i, i ^ mask) for i in range(size)])


def solution(mesh):
    size_x = mesh.shape["gx"]
    size_y = mesh.shape["gy"]
    struct = jax.ShapeDtypeStruct
    sems = lambda n: pltpu.SemaphoreType.DMA((n,))
    order = list(range(size_y - 1, -1, -1))
    quarter = max(size_y // 4, 1)
    early, middle, late = [], order[: 2 * quarter], order[2 * quarter :]

    def shards(inputs, gain, w_query, w_key, w_value, w_output, key_cache, value_cache, lengths):
        batch, depth = inputs.shape
        width = w_query.shape[1]
        rows = key_cache.shape[0]
        lanes = rows * (width // HD)
        packed = width + 3 * HD
        block = w_output.shape[1] // size_y
        piece = pltpu.VMEM((width, block), BF16)
        piece_bytes = 2 * width * block

        sums = pl.pallas_call(
            functools.partial(project, size_x),
            out_shape=[pltpu.VMEM((rows, packed), F32)] * size_x,
            in_specs=[ANY] * 5,
            out_specs=[VMEM] * size_x,
            scratch_shapes=[
                pltpu.VMEM(inputs.shape, BF16),
                pltpu.VMEM((1, depth), F32),
                pltpu.VMEM(w_query.shape, BF16),
                pltpu.VMEM(w_key.shape, BF16),
                pltpu.VMEM(w_value.shape, BF16),
                pltpu.VMEM(inputs.shape, BF16),
                pltpu.VMEM((batch, packed), F32),
                sems(depth // CHUNK + 4),
            ],
            compiler_params=params(28),
            cost_estimate=cost(2 * batch * depth * packed, 2 * depth * packed),
            name="project",
        )(*[in_hbm(a) for a in (inputs, gain.reshape(1, depth), w_query, w_key, w_value)])
        arrived = [sums[0]] + [swap(sums[m], "gx", size_x, m) for m in range(1, size_x)]

        fetched = pl.pallas_call(
            functools.partial(fetch_caches, early),
            out_shape=[pltpu.VMEM(key_cache.shape, BF16), pltpu.VMEM(value_cache.shape, BF16)]
            + [piece] * len(early),
            in_specs=[ANY] * 4,
            out_specs=[VMEM] * (2 + len(early)),
            scratch_shapes=[sems(2 + len(early))],
            compiler_params=params(4),
            cost_estimate=cost(0, 4 * key_cache.size + piece_bytes * len(early)),
            name="fetch_caches",
        )(sums[0], in_hbm(key_cache), in_hbm(value_cache), in_hbm(w_output))
        keys, values, *pieces = fetched

        half = HD // 2
        inverse = ROPE_BASE ** (-(jnp.arange(half, dtype=F32) * 2.0 / HD))
        angles = lengths.astype(F32)[:, None] * inverse[None, :]
        cosine, sine = jnp.cos(angles), jnp.sin(angles)
        heads, *more = pl.pallas_call(
            functools.partial(attention, size_x, depth * size_x, middle),
            out_shape=[pltpu.VMEM((rows, width), BF16)] + [piece] * len(middle),
            in_specs=[SMEM, VMEM, VMEM, VMEM, VMEM, ANY] + [VMEM] * size_x,
            out_specs=[VMEM] * (1 + len(middle)),
            scratch_shapes=[
                pltpu.VMEM((width // HD, rows, HD), F32),
                pltpu.VMEM((width // HD, rows, HD), F32),
                pltpu.VMEM((rows * HD, lanes), BF16),
                pltpu.VMEM((key_cache.shape[1], lanes), F32),
                pltpu.VMEM((lanes, key_cache.shape[1]), BF16),
                sems(max(len(middle), 1)),
            ],
            compiler_params=params(8),
            cost_estimate=cost(4 * key_cache.size * (width // HD), piece_bytes * len(middle)),
            name="attention",
        )(
            lengths,
            jnp.concatenate([cosine, cosine], 1),
            jnp.concatenate([-sine, sine], 1),
            in_vmem(keys),
            in_vmem(values),
            in_hbm(w_output),
            *[in_vmem(a) for a in arrived],
        )
        pieces += more
        gathered = [heads] + [swap(heads, "gx", size_x, m) for m in range(1, size_x)]

        residual, *more = pl.pallas_call(
            functools.partial(fetch_weights, late),
            out_shape=[pltpu.VMEM((batch, block), BF16)] + [piece] * len(late),
            in_specs=[ANY] * 3,
            out_specs=[VMEM] * (1 + len(late)),
            scratch_shapes=[sems(1 + len(late))],
            compiler_params=params(4),
            cost_estimate=cost(0, piece_bytes * len(late)),
            name="fetch_weights",
        )(heads, in_hbm(inputs), in_hbm(w_output))
        pieces += more

        terms = {}
        for mask, w in zip(order, pieces):
            kind = BF16 if mask else F32
            term = pl.pallas_call(
                functools.partial(project_out, size_x),
                out_shape=pltpu.VMEM((batch, block), kind),
                in_specs=[VMEM] * (1 + size_x),
                out_specs=VMEM,
                scratch_shapes=[pltpu.VMEM((batch, width), F32)],
                compiler_params=params(8),
                cost_estimate=cost(2 * batch * width * block, piece_bytes),
                name="project_out",
            )(in_vmem(w), *[in_vmem(a) for a in gathered])
            terms[mask] = swap(term, "gy", size_y, mask) if mask else term
        done = pl.pallas_call(
            finish,
            out_shape=pltpu.VMEM((batch, block), BF16),
            in_specs=[VMEM] * (1 + size_y),
            out_specs=VMEM,
            compiler_params=params(4),
            name="finish",
        )(in_vmem(residual), *[in_vmem(terms[m]) for m in range(size_y)])
        blocks = [done] + [swap(done, "gy", size_y, m) for m in range(1, size_y)]
        return pl.pallas_call(
            functools.partial(assemble, size_y),
            out_shape=struct((batch, block * size_y), BF16),
            in_specs=[VMEM] * size_y,
            out_specs=ANY,
            scratch_shapes=[sems(size_y)],
            compiler_params=params(4),
            name="assemble",
        )(*[in_vmem(b) for b in blocks])

    placed = (
        P("groups", "gx"),
        P("gx"),
        P("gx", "gy"),
        P("gx", "gy"),
        P("gx", "gy"),
        P("gy", "gx"),
        P(("groups", "gx"), None, "gy"),
        P(("groups", "gx"), None, "gy"),
        P(("groups", "gx")),
    )
    return jax.shard_map(
        shards, mesh=mesh, in_specs=placed, out_specs=P("groups", "gx"), check_vma=False
    )
```

```python
import functools
import math

import jax
import jax.numpy as jnp
from jax import lax
from jax.experimental import pallas as pl
from jax.experimental.pallas import tpu as pltpu
from jax.sharding import PartitionSpec as P

HD = 128
EPS = 1e-05
ROPE_BASE = 500000.0
CHUNK = 256
F32 = jnp.float32
BF16 = jnp.bfloat16

ANY = pl.BlockSpec(memory_space=pl.ANY)
VMEM = pl.BlockSpec(memory_space=pltpu.VMEM)
SMEM = pl.BlockSpec(memory_space=pltpu.SMEM)
MIB = 1 << 20


def columns(index, width):
    return pl.ds(pl.multiple_of(index * width, HD), width)


def params(mib):
    return pltpu.CompilerParams(vmem_limit_bytes=mib * MIB)


def cost(flops, nbytes):
    return pl.CostEstimate(flops=flops, bytes_accessed=nbytes, transcendentals=0)


def in_vmem(value):
    return pltpu.with_memory_space_constraint(value, pltpu.VMEM)


def in_hbm(value):
    return pltpu.with_memory_space_constraint(value, pltpu.HBM)


def project(size, x_hbm, gain_hbm, wq_hbm, wk_hbm, wv_hbm, *refs):
    kept, given, x, gain, wq, wk, wv, scaled, total, sems = refs
    depth = x.shape[1]
    steps = depth // CHUNK
    pairs = [(x_hbm, x), (gain_hbm, gain), (wk_hbm, wk), (wv_hbm, wv)]
    small = [pltpu.make_async_copy(a, b, sems.at[steps + i]) for i, (a, b) in enumerate(pairs)]
    large = []
    for step in range(steps):
        part = pl.ds(step * CHUNK, CHUNK)
        large.append(pltpu.make_async_copy(wq_hbm.at[part], wq.at[part], sems.at[step]))
    small[0].start()
    small[1].start()
    for copy in large[:2]:
        copy.start()
    small[2].start()
    small[3].start()
    for copy in large[2:]:
        copy.start()
    small[0].wait()
    small[1].wait()
    wide = x[...].astype(F32)
    scaled[...] = (wide * gain[...]).astype(BF16)
    squares = jnp.sum(wide * wide, 1, keepdims=True)
    width = wq.shape[1]
    dot = functools.partial(jnp.dot, preferred_element_type=F32)
    for step, copy in enumerate(large):
        copy.wait()
        part = slice(step * CHUNK, (step + 1) * CHUNK)
        term = dot(scaled[:, part], wq[part])
        if step == 0:
            total[:, :width] = term
        else:
            total[:, :width] += term
        if step == 1:
            small[2].wait()
            total[:, width : width + HD] = dot(scaled[...], wk[...])
            small[3].wait()
            total[:, width + HD : width + 2 * HD] = dot(scaled[...], wv[...])
            total[:, width + 2 * HD :] = jnp.broadcast_to(squares, (squares.shape[0], HD))
    rows = kept.shape[1]
    me = lax.axis_index("gx")
    for mask in range(size):
        out = given if mask % 2 else kept
        start = pl.multiple_of((me ^ mask) * rows, 8)
        out[mask // 2] = total[pl.ds(start, rows), :]


def merge(kept, arrived, *outs):
    for index, out in enumerate(outs):
        out[...] = kept[index] + arrived[index]


def fetch_pieces(masks, width, w_hbm, pieces, sems, first):
    me = lax.axis_index("gy")
    copies = []
    for i, mask in enumerate(masks):
        source = w_hbm.at[:, columns(me ^ mask, width)]
        copies.append(pltpu.make_async_copy(source, pieces[i], sems.at[first + i]))
    return copies


def fetch_caches(masks, after, k_hbm, v_hbm, w_hbm, k, v, *refs):
    del after
    *pieces, sems = refs
    copies = [
        pltpu.make_async_copy(k_hbm, k, sems.at[0]),
        pltpu.make_async_copy(v_hbm, v, sems.at[1]),
    ]
    if masks:
        copies += fetch_pieces(masks, pieces[0].shape[1], w_hbm, pieces, sems, 2)
    for copy in copies:
        copy.start()
    for copy in copies:
        copy.wait()


def fetch_weights(masks, after, w_hbm, *refs):
    del after
    *pieces, sems = refs
    copies = fetch_pieces(masks, pieces[0].shape[1], w_hbm, pieces, sems, 0)
    for copy in copies:
        copy.start()
    for copy in copies:
        copy.wait()


def attention(size, model, masks, lengths, cosine, sine, k, v, w_hbm, *refs):
    arrived = refs[:size]
    heads = refs[size]
    pieces = refs[size + 1 : size + 1 + len(masks)]
    q_rows, o_rows, scores, sems = refs[size + 1 + len(masks) :]
    copies = fetch_pieces(masks, pieces[0].shape[1], w_hbm, pieces, sems, 0) if masks else []
    for copy in copies:
        copy.start()
    rows, slots = k.shape[0], k.shape[1]
    group = heads.shape[1] // HD
    width = group * HD
    summed = arrived[0][...]
    for item in arrived[1:]:
        summed = summed + item[...].astype(F32)
    scale = lax.rsqrt(summed[:, width + 2 * HD :] / model + EPS)
    cosines, sines = cosine[...], sine[...]

    def turn(value):
        return value * cosines + pltpu.roll(value, HD // 2, 1) * sines

    for head in range(group):
        part = summed[:, head * HD : (head + 1) * HD] * scale
        q_rows[head] = turn(part).astype(BF16).astype(F32)
    new_keys = turn(summed[:, width : width + HD] * scale).astype(BF16).astype(F32)
    new_values = (summed[:, width + HD : width + 2 * HD] * scale).astype(BF16).astype(F32)
    rate = HD ** (-0.5) * math.log2(math.e)
    half = slots // 2
    slot = lax.broadcasted_iota(jnp.int32, (2 * group, half), 1) + half
    second = lax.broadcasted_iota(jnp.int32, (2 * group, 1), 0) >= group
    empty = jnp.zeros((group, HD), F32)
    own, top = [], []
    for row in range(0, rows, 2):
        first, other = q_rows[:, row, :], q_rows[:, row + 1, :]
        queries = jnp.concatenate(
            [jnp.concatenate([first, empty], 1), jnp.concatenate([empty, other], 1)], 0
        )
        keys = jnp.concatenate([k[row], k[row + 1]], 1)
        raw = lax.dot_general(
            queries.astype(BF16), keys, (((1,), (1,)), ((), ())), preferred_element_type=F32
        )
        low = raw[:, :half]
        limit = jnp.where(second, lengths[row + 1], lengths[row])
        high = jnp.where(slot < limit, raw[:, half:], -jnp.inf)
        mine = slice(row * group, (row + 2) * group)
        scores[mine, :half] = low
        scores[mine, half:] = high
        both = jnp.concatenate(
            [first * new_keys[row : row + 1], other * new_keys[row + 1 : row + 2]], 0
        )
        own.append(jnp.sum(both, 1, keepdims=True))
        top.append(jnp.maximum(jnp.max(jnp.maximum(low, high), 1, keepdims=True), own[-1]))

    def soften(pair):
        mine = slice(2 * pair * group, (2 * pair + 2) * group)
        probs = jnp.exp2((scores[mine] - top[pair]) * rate)
        own_prob = jnp.exp2((own[pair] - top[pair]) * rate)
        share = 1.0 / (jnp.sum(probs, 1, keepdims=True) + own_prob)
        return probs.astype(BF16), own_prob, share

    ready = soften(0)
    for pair in range(rows // 2):
        probs, own_prob, share = ready
        if pair + 1 < rows // 2:
            ready = soften(pair + 1)
        sides = jnp.concatenate([v[2 * pair], v[2 * pair + 1]], 1)
        mixed = jnp.dot(probs, sides, preferred_element_type=F32)
        for side in range(2):
            row = 2 * pair + side
            mine = slice(side * group, (side + 1) * group)
            value = mixed[mine, side * HD : (side + 1) * HD]
            extra = own_prob[mine] * new_values[row : row + 1]
            o_rows[:, row, :] = (value + extra) * share[mine]
    for head in range(group):
        heads[:, head * HD : (head + 1) * HD] = o_rows[head].astype(BF16)
    for copy in copies:
        copy.wait()


def gather_rows(blocks, gathered):
    me = lax.axis_index("gx")
    rows = blocks[0].shape[0]
    for mask, block in enumerate(blocks):
        start = pl.multiple_of((me ^ mask) * rows, 8)
        gathered[pl.ds(start, rows), :] = block[...].astype(F32)
    return gathered[...].astype(BF16)


def project_out(size, w, *refs):
    blocks, out, gathered = refs[:size], refs[-2], refs[-1]
    heads = gather_rows(blocks, gathered)
    out[...] = jnp.dot(heads, w[...], preferred_element_type=F32).astype(out.dtype)


def stream_out(size, mask, w_hbm, x_hbm, *refs):
    blocks = refs[:size]
    out, gathered, w, x, sems = refs[-5:]
    width = out.shape[1]
    me = lax.axis_index("gy")
    steps = w.shape[0] // (2 * CHUNK)
    copies = []
    for step in range(steps):
        part = pl.ds(step * 2 * CHUNK, 2 * CHUNK)
        source = w_hbm.at[part, columns(me ^ mask, width)]
        copies.append(pltpu.make_async_copy(source, w.at[part], sems.at[step]))
    if not mask:
        source = x_hbm.at[:, columns(me, width)]
        copies.append(pltpu.make_async_copy(source, x, sems.at[steps]))
    for copy in copies:
        copy.start()
    heads = gather_rows(blocks, gathered)
    total = None
    for step in range(steps):
        copies[step].wait()
        part = slice(step * 2 * CHUNK, (step + 1) * 2 * CHUNK)
        term = jnp.dot(heads[:, part], w[part], preferred_element_type=F32)
        total = term if total is None else total + term
    if not mask:
        copies[steps].wait()
        total = total + x[...].astype(F32)
    out[...] = total.astype(out.dtype)


def finish(own, *refs):
    *arrived, out = refs
    total = own[...]
    for item in arrived:
        total = total + item[...].astype(F32)
    out[...] = total.astype(BF16)


def assemble(size, *refs):
    blocks, out, sems = refs[:size], refs[size], refs[size + 1]
    me = lax.axis_index("gy")
    width = blocks[0].shape[1]
    copies = []
    for mask in range(size):
        target = out.at[:, columns(me ^ mask, width)]
        copies.append(pltpu.make_async_copy(blocks[mask], target, sems.at[mask]))
    for copy in copies:
        copy.start()
    for copy in copies:
        copy.wait()


def swap(value, axis, size, mask):
    return lax.ppermute(value, axis, [(i, i ^ mask) for i in range(size)])


def solution(mesh):
    size_x = mesh.shape["gx"]
    size_y = mesh.shape["gy"]
    struct = jax.ShapeDtypeStruct
    sems = lambda n: pltpu.SemaphoreType.DMA((n,))
    order = list(range(size_y - 1, -1, -1))
    quarter = max(size_y // 4, 1)
    early, middle, late = [], order[: 2 * quarter], order[2 * quarter : -1]

    def shards(inputs, gain, w_query, w_key, w_value, w_output, key_cache, value_cache, lengths):
        batch, depth = inputs.shape
        width = w_query.shape[1]
        rows = key_cache.shape[0]
        packed = width + 3 * HD
        block = w_output.shape[1] // size_y
        piece = pltpu.VMEM((width, block), BF16)
        piece_bytes = 2 * width * block

        levels = size_x // 2
        kept, given = pl.pallas_call(
            functools.partial(project, size_x),
            out_shape=[pltpu.VMEM((levels, rows, packed), F32)] * 2,
            in_specs=[ANY] * 5,
            out_specs=[VMEM] * 2,
            scratch_shapes=[
                pltpu.VMEM(inputs.shape, BF16),
                pltpu.VMEM((1, depth), F32),
                pltpu.VMEM(w_query.shape, BF16),
                pltpu.VMEM(w_key.shape, BF16),
                pltpu.VMEM(w_value.shape, BF16),
                pltpu.VMEM(inputs.shape, BF16),
                pltpu.VMEM((batch, packed), F32),
                sems(depth // CHUNK + 4),
            ],
            compiler_params=params(28),
            cost_estimate=cost(2 * batch * depth * packed, 2 * depth * packed),
            name="project",
        )(*[in_hbm(a) for a in (inputs, gain.reshape(1, depth), w_query, w_key, w_value)])
        sums = pl.pallas_call(
            merge,
            out_shape=[pltpu.VMEM((rows, packed), F32)] * levels,
            in_specs=[VMEM] * 2,
            out_specs=[VMEM] * levels,
            compiler_params=params(4),
            name="merge",
        )(in_vmem(kept), in_vmem(swap(given, "gx", size_x, 1)))
        arrived = [sums[0]] + [swap(sums[j], "gx", size_x, 2 * j) for j in range(1, levels)]

        fetched = pl.pallas_call(
            functools.partial(fetch_caches, early),
            out_shape=[pltpu.VMEM(key_cache.shape, BF16), pltpu.VMEM(value_cache.shape, BF16)]
            + [piece] * len(early),
            in_specs=[ANY] * 4,
            out_specs=[VMEM] * (2 + len(early)),
            scratch_shapes=[sems(2 + len(early))],
            compiler_params=params(4),
            cost_estimate=cost(0, 4 * key_cache.size + piece_bytes * len(early)),
            name="fetch_caches",
        )(sums[0], in_hbm(key_cache), in_hbm(value_cache), in_hbm(w_output))
        keys, values, *pieces = fetched

        half = HD // 2
        inverse = ROPE_BASE ** (-(jnp.arange(half, dtype=F32) * 2.0 / HD))
        angles = lengths.astype(F32)[:, None] * inverse[None, :]
        cosine, sine = jnp.cos(angles), jnp.sin(angles)
        heads, *more = pl.pallas_call(
            functools.partial(attention, levels, depth * size_x, middle),
            out_shape=[pltpu.VMEM((rows, width), BF16)] + [piece] * len(middle),
            in_specs=[SMEM, VMEM, VMEM, VMEM, VMEM, ANY] + [VMEM] * levels,
            out_specs=[VMEM] * (1 + len(middle)),
            scratch_shapes=[
                pltpu.VMEM((width // HD, rows, HD), F32),
                pltpu.VMEM((width // HD, rows, HD), F32),
                pltpu.VMEM((rows * (width // HD), key_cache.shape[1]), F32),
                sems(max(len(middle), 1)),
            ],
            compiler_params=params(8),
            cost_estimate=cost(4 * key_cache.size * (width // HD), piece_bytes * len(middle)),
            name="attention",
        )(
            lengths,
            jnp.concatenate([cosine, cosine], 1),
            jnp.concatenate([-sine, sine], 1),
            in_vmem(keys),
            in_vmem(values),
            in_hbm(w_output),
            *[in_vmem(a) for a in arrived],
        )
        pieces += more
        gathered = [heads] + [swap(heads, "gx", size_x, m) for m in range(1, size_x)]

        pieces += pl.pallas_call(
            functools.partial(fetch_weights, late),
            out_shape=[piece] * len(late),
            in_specs=[ANY] * 2,
            out_specs=[VMEM] * len(late),
            scratch_shapes=[sems(len(late))],
            compiler_params=params(4),
            cost_estimate=cost(0, piece_bytes * len(late)),
            name="fetch_weights",
        )(heads, in_hbm(w_output))

        terms = {}
        for index, mask in enumerate(order):
            kind = BF16 if mask else F32
            ready = index < len(pieces)
            shared = dict(
                out_shape=pltpu.VMEM((batch, block), kind),
                out_specs=VMEM,
                compiler_params=params(12),
                cost_estimate=cost(2 * batch * width * block, piece_bytes),
            )
            rows_in = [in_vmem(a) for a in gathered]
            scratch = [pltpu.VMEM((batch, width), F32)]
            if ready:
                term = pl.pallas_call(
                    functools.partial(project_out, size_x),
                    in_specs=[VMEM] * (1 + size_x),
                    scratch_shapes=scratch,
                    name="project_out",
                    **shared,
                )(in_vmem(pieces[index]), *rows_in)
            else:
                scratch += [
                    pltpu.VMEM((width, block), BF16),
                    pltpu.VMEM((batch, block), BF16),
                    sems(width // (2 * CHUNK) + 1),
                ]
                term = pl.pallas_call(
                    functools.partial(stream_out, size_x, mask),
                    in_specs=[ANY] * 2 + [VMEM] * size_x,
                    scratch_shapes=scratch,
                    name="stream_out",
                    **shared,
                )(in_hbm(w_output), in_hbm(inputs), *rows_in)
            terms[mask] = swap(term, "gy", size_y, mask) if mask else term
        done = pl.pallas_call(
            finish,
            out_shape=pltpu.VMEM((batch, block), BF16),
            in_specs=[VMEM] * size_y,
            out_specs=VMEM,
            compiler_params=params(4),
            name="finish",
        )(*[in_vmem(terms[m]) for m in range(size_y)])
        blocks = [done] + [swap(done, "gy", size_y, m) for m in range(1, size_y)]
        return pl.pallas_call(
            functools.partial(assemble, size_y),
            out_shape=struct((batch, block * size_y), BF16),
            in_specs=[VMEM] * size_y,
            out_specs=ANY,
            scratch_shapes=[sems(size_y)],
            compiler_params=params(4),
            name="assemble",
        )(*[in_vmem(b) for b in blocks])

    placed = (
        P("groups", "gx"),
        P("gx"),
        P("gx", "gy"),
        P("gx", "gy"),
        P("gx", "gy"),
        P("gy", "gx"),
        P(("groups", "gx"), None, "gy"),
        P(("groups", "gx"), None, "gy"),
        P(("groups", "gx")),
    )
    return jax.shard_map(
        shards, mesh=mesh, in_specs=placed, out_specs=P("groups", "gx"), check_vma=False
    )
```

```python
import functools
import math

import jax
import jax.numpy as jnp
from jax import lax
from jax.experimental import pallas as pl
from jax.experimental.pallas import tpu as pltpu
from jax.sharding import PartitionSpec as P

HD = 128
EPS = 1e-05
ROPE_BASE = 500000.0
CHUNK = 256
F32 = jnp.float32
BF16 = jnp.bfloat16

ANY = pl.BlockSpec(memory_space=pl.ANY)
VMEM = pl.BlockSpec(memory_space=pltpu.VMEM)
SMEM = pl.BlockSpec(memory_space=pltpu.SMEM)
MIB = 1 << 20


def columns(index, width):
    return pl.ds(pl.multiple_of(index * width, HD), width)


def params(mib):
    return pltpu.CompilerParams(vmem_limit_bytes=mib * MIB)


def cost(flops, nbytes):
    return pl.CostEstimate(flops=flops, bytes_accessed=nbytes, transcendentals=0)


def in_vmem(value):
    return pltpu.with_memory_space_constraint(value, pltpu.VMEM)


def in_hbm(value):
    return pltpu.with_memory_space_constraint(value, pltpu.HBM)


def project(size, x_hbm, gain_hbm, wq_hbm, wk_hbm, wv_hbm, *refs):
    kept, given, x, gain, wq, wk, wv, scaled, total, sems = refs
    depth = x.shape[1]
    steps = depth // CHUNK
    pairs = [(x_hbm, x), (gain_hbm, gain), (wk_hbm, wk), (wv_hbm, wv)]
    small = [pltpu.make_async_copy(a, b, sems.at[steps + i]) for i, (a, b) in enumerate(pairs)]
    large = []
    for step in range(steps):
        part = pl.ds(step * CHUNK, CHUNK)
        large.append(pltpu.make_async_copy(wq_hbm.at[part], wq.at[part], sems.at[step]))
    small[0].start()
    small[1].start()
    for copy in large[:2]:
        copy.start()
    small[2].start()
    small[3].start()
    for copy in large[2:]:
        copy.start()
    small[0].wait()
    small[1].wait()
    wide = x[...].astype(F32)
    scaled[...] = (wide * gain[...]).astype(BF16)
    squares = jnp.sum(wide * wide, 1, keepdims=True)
    width = wq.shape[1]
    dot = functools.partial(jnp.dot, preferred_element_type=F32)
    for step, copy in enumerate(large):
        copy.wait()
        part = slice(step * CHUNK, (step + 1) * CHUNK)
        term = dot(scaled[:, part], wq[part])
        if step == 0:
            total[:, :width] = term
        else:
            total[:, :width] += term
        if step == 1:
            small[2].wait()
            total[:, width : width + HD] = dot(scaled[...], wk[...])
            small[3].wait()
            total[:, width + HD : width + 2 * HD] = dot(scaled[...], wv[...])
            total[:, width + 2 * HD :] = jnp.broadcast_to(squares, (squares.shape[0], HD))
    rows = kept.shape[1]
    me = lax.axis_index("gx")
    for mask in range(size):
        out = given if mask % 2 else kept
        start = pl.multiple_of((me ^ mask) * rows, 8)
        out[mask // 2] = total[pl.ds(start, rows), :]


def merge(kept, arrived, *outs):
    for index, out in enumerate(outs):
        out[...] = kept[index] + arrived[index]


def fetch_pieces(masks, width, w_hbm, pieces, sems, first):
    me = lax.axis_index("gy")
    copies = []
    for i, mask in enumerate(masks):
        source = w_hbm.at[:, columns(me ^ mask, width)]
        copies.append(pltpu.make_async_copy(source, pieces[i], sems.at[first + i]))
    return copies


def fetch(after, source, target, sem):
    del after
    copy = pltpu.make_async_copy(source, target, sem)
    copy.start()
    copy.wait()


def weigh(size, model, masks, lengths, cosine, sine, k, v_hbm, w_hbm, *refs):
    arrived = refs[:size]
    probs_out, own_out, share_out, new_out, v = refs[size : size + 5]
    pieces = refs[size + 5 : size + 5 + len(masks)]
    q_rows, scores, sems = refs[size + 5 + len(masks) :]
    copies = [pltpu.make_async_copy(v_hbm, v, sems.at[0])]
    if masks:
        copies += fetch_pieces(masks, pieces[0].shape[1], w_hbm, pieces, sems, 1)
    for copy in copies:
        copy.start()
    rows, slots = k.shape[0], k.shape[1]
    group = probs_out.shape[0] // rows
    width = group * HD
    summed = arrived[0][...]
    for item in arrived[1:]:
        summed = summed + item[...].astype(F32)
    scale = lax.rsqrt(summed[:, width + 2 * HD :] / model + EPS)
    cosines, sines = cosine[...], sine[...]

    def turn(value):
        return value * cosines + pltpu.roll(value, HD // 2, 1) * sines

    for head in range(group):
        part = summed[:, head * HD : (head + 1) * HD] * scale
        q_rows[head] = turn(part).astype(BF16).astype(F32)
    new_keys = turn(summed[:, width : width + HD] * scale).astype(BF16).astype(F32)
    new_out[...] = (summed[:, width + HD : width + 2 * HD] * scale).astype(BF16).astype(F32)
    rate = HD ** (-0.5) * math.log2(math.e)
    half = slots // 2
    slot = lax.broadcasted_iota(jnp.int32, (2 * group, half), 1) + half
    second = lax.broadcasted_iota(jnp.int32, (2 * group, 1), 0) >= group
    empty = jnp.zeros((group, HD), F32)
    own, top = [], []
    for row in range(0, rows, 2):
        first, other = q_rows[:, row, :], q_rows[:, row + 1, :]
        queries = jnp.concatenate(
            [jnp.concatenate([first, empty], 1), jnp.concatenate([empty, other], 1)], 0
        )
        keys = jnp.concatenate([k[row], k[row + 1]], 1)
        raw = lax.dot_general(
            queries.astype(BF16), keys, (((1,), (1,)), ((), ())), preferred_element_type=F32
        )
        low = raw[:, :half]
        limit = jnp.where(second, lengths[row + 1], lengths[row])
        high = jnp.where(slot < limit, raw[:, half:], -jnp.inf)
        mine = slice(row * group, (row + 2) * group)
        scores[mine, :half] = low
        scores[mine, half:] = high
        both = jnp.concatenate(
            [first * new_keys[row : row + 1], other * new_keys[row + 1 : row + 2]], 0
        )
        own.append(jnp.sum(both, 1, keepdims=True))
        top.append(jnp.maximum(jnp.max(jnp.maximum(low, high), 1, keepdims=True), own[-1]))
    for pair in range(rows // 2):
        mine = slice(2 * pair * group, (2 * pair + 2) * group)
        probs = jnp.exp2((scores[mine] - top[pair]) * rate)
        own_prob = jnp.exp2((own[pair] - top[pair]) * rate)
        share = 1.0 / (jnp.sum(probs, 1, keepdims=True) + own_prob)
        probs_out[mine] = probs.astype(BF16)
        own_out[mine] = jnp.broadcast_to(own_prob, (2 * group, HD))
        share_out[mine] = jnp.broadcast_to(share, (2 * group, HD))
    for copy in copies:
        copy.wait()


def mix(masks, probs, own, share, new, v, w_hbm, heads, *refs):
    *pieces, o_rows, sems = refs
    copies = fetch_pieces(masks, pieces[0].shape[1], w_hbm, pieces, sems, 0) if masks else []
    for copy in copies:
        copy.start()
    rows = v.shape[0]
    group = probs.shape[0] // rows
    for row in range(0, rows, 2):
        sides = jnp.concatenate([v[row], v[row + 1]], 1)
        pair = slice(row * group, (row + 2) * group)
        mixed = jnp.dot(probs[pair], sides, preferred_element_type=F32)
        for side in range(2):
            part = slice(side * group, (side + 1) * group)
            mine = slice((row + side) * group, (row + side + 1) * group)
            value = mixed[part, side * HD : (side + 1) * HD]
            extra = own[mine] * new[row + side : row + side + 1]
            o_rows[:, row + side, :] = (value + extra) * share[mine]
    for head in range(group):
        heads[:, head * HD : (head + 1) * HD] = o_rows[head].astype(BF16)
    for copy in copies:
        copy.wait()


def gather_rows(blocks, gathered):
    me = lax.axis_index("gx")
    rows = blocks[0].shape[0]
    for mask, block in enumerate(blocks):
        start = pl.multiple_of((me ^ mask) * rows, 8)
        gathered[pl.ds(start, rows), :] = block[...].astype(F32)
    return gathered[...].astype(BF16)


def project_out(size, w, *refs):
    blocks, out, gathered = refs[:size], refs[-2], refs[-1]
    heads = gather_rows(blocks, gathered)
    out[...] = jnp.dot(heads, w[...], preferred_element_type=F32).astype(out.dtype)


def stream_out(size, mask, w_hbm, x_hbm, *refs):
    blocks = refs[:size]
    out, gathered, w, x, sems = refs[-5:]
    width = out.shape[1]
    me = lax.axis_index("gy")
    steps = w.shape[0] // (2 * CHUNK)
    copies = []
    for step in range(steps):
        part = pl.ds(step * 2 * CHUNK, 2 * CHUNK)
        source = w_hbm.at[part, columns(me ^ mask, width)]
        copies.append(pltpu.make_async_copy(source, w.at[part], sems.at[step]))
    if not mask:
        source = x_hbm.at[:, columns(me, width)]
        copies.append(pltpu.make_async_copy(source, x, sems.at[steps]))
    for copy in copies:
        copy.start()
    heads = gather_rows(blocks, gathered)
    total = None
    for step in range(steps):
        copies[step].wait()
        part = slice(step * 2 * CHUNK, (step + 1) * 2 * CHUNK)
        term = jnp.dot(heads[:, part], w[part], preferred_element_type=F32)
        total = term if total is None else total + term
    if not mask:
        copies[steps].wait()
        total = total + x[...].astype(F32)
    out[...] = total.astype(out.dtype)


def finish(own, *refs):
    *arrived, out = refs
    total = own[...]
    for item in arrived:
        total = total + item[...].astype(F32)
    out[...] = total.astype(BF16)


def assemble(size, *refs):
    blocks, out, sems = refs[:size], refs[size], refs[size + 1]
    me = lax.axis_index("gy")
    width = blocks[0].shape[1]
    copies = []
    for mask in range(size):
        target = out.at[:, columns(me ^ mask, width)]
        copies.append(pltpu.make_async_copy(blocks[mask], target, sems.at[mask]))
    for copy in copies:
        copy.start()
    for copy in copies:
        copy.wait()


def swap(value, axis, size, mask):
    return lax.ppermute(value, axis, [(i, i ^ mask) for i in range(size)])


def solution(mesh):
    size_x = mesh.shape["gx"]
    size_y = mesh.shape["gy"]
    struct = jax.ShapeDtypeStruct
    sems = lambda n: pltpu.SemaphoreType.DMA((n,))
    order = list(range(size_y - 1, -1, -1))
    quarter = max(size_y // 4, 1)
    early, middle = order[:quarter], order[quarter:-1]

    def shards(inputs, gain, w_query, w_key, w_value, w_output, key_cache, value_cache, lengths):
        batch, depth = inputs.shape
        width = w_query.shape[1]
        rows = key_cache.shape[0]
        packed = width + 3 * HD
        block = w_output.shape[1] // size_y
        piece = pltpu.VMEM((width, block), BF16)
        piece_bytes = 2 * width * block

        levels = size_x // 2
        kept, given = pl.pallas_call(
            functools.partial(project, size_x),
            out_shape=[pltpu.VMEM((levels, rows, packed), F32)] * 2,
            in_specs=[ANY] * 5,
            out_specs=[VMEM] * 2,
            scratch_shapes=[
                pltpu.VMEM(inputs.shape, BF16),
                pltpu.VMEM((1, depth), F32),
                pltpu.VMEM(w_query.shape, BF16),
                pltpu.VMEM(w_key.shape, BF16),
                pltpu.VMEM(w_value.shape, BF16),
                pltpu.VMEM(inputs.shape, BF16),
                pltpu.VMEM((batch, packed), F32),
                sems(depth // CHUNK + 4),
            ],
            compiler_params=params(28),
            cost_estimate=cost(2 * batch * depth * packed, 2 * depth * packed),
            name="project",
        )(*[in_hbm(a) for a in (inputs, gain.reshape(1, depth), w_query, w_key, w_value)])
        sums = pl.pallas_call(
            merge,
            out_shape=[pltpu.VMEM((rows, packed), F32)] * levels,
            in_specs=[VMEM] * 2,
            out_specs=[VMEM] * levels,
            compiler_params=params(4),
            name="merge",
        )(in_vmem(kept), in_vmem(swap(given, "gx", size_x, 1)))
        arrived = [sums[0]] + [swap(sums[j], "gx", size_x, 2 * j) for j in range(1, levels)]

        keys = pl.pallas_call(
            fetch,
            out_shape=pltpu.VMEM(key_cache.shape, BF16),
            in_specs=[ANY] * 2,
            out_specs=VMEM,
            scratch_shapes=[pltpu.SemaphoreType.DMA],
            compiler_params=params(4),
            cost_estimate=cost(0, 2 * key_cache.size),
            name="fetch",
        )(sums[0], in_hbm(key_cache))

        half = HD // 2
        inverse = ROPE_BASE ** (-(jnp.arange(half, dtype=F32) * 2.0 / HD))
        angles = lengths.astype(F32)[:, None] * inverse[None, :]
        cosine, sine = jnp.cos(angles), jnp.sin(angles)
        lanes = rows * (width // HD)
        stat = pltpu.VMEM((lanes, HD), F32)
        probs, own, share, new_values, values, *pieces = pl.pallas_call(
            functools.partial(weigh, levels, depth * size_x, early),
            out_shape=[
                pltpu.VMEM((lanes, key_cache.shape[1]), BF16),
                stat,
                stat,
                pltpu.VMEM((rows, HD), F32),
                pltpu.VMEM(value_cache.shape, BF16),
            ]
            + [piece] * len(early),
            in_specs=[SMEM, VMEM, VMEM, VMEM, ANY, ANY] + [VMEM] * levels,
            out_specs=[VMEM] * (5 + len(early)),
            scratch_shapes=[
                pltpu.VMEM((width // HD, rows, HD), F32),
                pltpu.VMEM((lanes, key_cache.shape[1]), F32),
                sems(1 + len(early)),
            ],
            compiler_params=params(8),
            cost_estimate=cost(2 * key_cache.size * (width // HD), 2 * value_cache.size),
            name="weigh",
        )(
            lengths,
            jnp.concatenate([cosine, cosine], 1),
            jnp.concatenate([-sine, sine], 1),
            in_vmem(keys),
            in_hbm(value_cache),
            in_hbm(w_output),
            *[in_vmem(a) for a in arrived],
        )
        heads, *more = pl.pallas_call(
            functools.partial(mix, middle),
            out_shape=[pltpu.VMEM((rows, width), BF16)] + [piece] * len(middle),
            in_specs=[VMEM] * 5 + [ANY],
            out_specs=[VMEM] * (1 + len(middle)),
            scratch_shapes=[
                pltpu.VMEM((width // HD, rows, HD), F32),
                sems(max(len(middle), 1)),
            ],
            compiler_params=params(8),
            cost_estimate=cost(2 * key_cache.size * (width // HD), piece_bytes * len(middle)),
            name="mix",
        )(*[in_vmem(a) for a in (probs, own, share, new_values, values)], in_hbm(w_output))
        pieces += more
        gathered = [heads]
        for mask in range(2, size_x, 2):
            gathered.append(swap(heads, "gx", size_x, mask))
        gathered = [g for even in gathered for g in (even, swap(even, "gx", size_x, 1))]

        terms = {}
        for index, mask in enumerate(order):
            kind = BF16 if mask else F32
            ready = index < len(pieces)
            shared = dict(
                out_shape=pltpu.VMEM((batch, block), kind),
                out_specs=VMEM,
                compiler_params=params(12),
                cost_estimate=cost(2 * batch * width * block, piece_bytes),
            )
            rows_in = [in_vmem(a) for a in gathered]
            scratch = [pltpu.VMEM((batch, width), F32)]
            if ready:
                term = pl.pallas_call(
                    functools.partial(project_out, size_x),
                    in_specs=[VMEM] * (1 + size_x),
                    scratch_shapes=scratch,
                    name="project_out",
                    **shared,
                )(in_vmem(pieces[index]), *rows_in)
            else:
                scratch += [
                    pltpu.VMEM((width, block), BF16),
                    pltpu.VMEM((batch, block), BF16),
                    sems(width // (2 * CHUNK) + 1),
                ]
                term = pl.pallas_call(
                    functools.partial(stream_out, size_x, mask),
                    in_specs=[ANY] * 2 + [VMEM] * size_x,
                    scratch_shapes=scratch,
                    name="stream_out",
                    **shared,
                )(in_hbm(w_output), in_hbm(inputs), *rows_in)
            terms[mask] = swap(term, "gy", size_y, mask) if mask else term
        done = pl.pallas_call(
            finish,
            out_shape=pltpu.VMEM((batch, block), BF16),
            in_specs=[VMEM] * size_y,
            out_specs=VMEM,
            compiler_params=params(4),
            name="finish",
        )(*[in_vmem(terms[m]) for m in range(size_y)])
        blocks = [done] + [swap(done, "gy", size_y, m) for m in range(1, size_y)]
        return pl.pallas_call(
            functools.partial(assemble, size_y),
            out_shape=struct((batch, block * size_y), BF16),
            in_specs=[VMEM] * size_y,
            out_specs=ANY,
            scratch_shapes=[sems(size_y)],
            compiler_params=params(4),
            name="assemble",
        )(*[in_vmem(b) for b in blocks])

    placed = (
        P("groups", "gx"),
        P("gx"),
        P("gx", "gy"),
        P("gx", "gy"),
        P("gx", "gy"),
        P("gy", "gx"),
        P(("groups", "gx"), None, "gy"),
        P(("groups", "gx"), None, "gy"),
        P(("groups", "gx")),
    )
    return jax.shard_map(
        shards, mesh=mesh, in_specs=placed, out_specs=P("groups", "gx"), check_vma=False
    )
```

```python
import functools
import math

import jax
import jax.numpy as jnp
from jax import lax
from jax.experimental import pallas as pl
from jax.experimental.pallas import tpu as pltpu
from jax.sharding import PartitionSpec as P

HD = 128
EPS = 1e-05
ROPE_BASE = 500000.0
CHUNK = 256
F32 = jnp.float32
BF16 = jnp.bfloat16

ANY = pl.BlockSpec(memory_space=pl.ANY)
VMEM = pl.BlockSpec(memory_space=pltpu.VMEM)
MIB = 1 << 20


def columns(index, width):
    return pl.ds(pl.multiple_of(index * width, HD), width)


def params(mib):
    return pltpu.CompilerParams(vmem_limit_bytes=mib * MIB)


def cost(flops, nbytes):
    return pl.CostEstimate(flops=flops, bytes_accessed=nbytes, transcendentals=0)


def in_vmem(value):
    return pltpu.with_memory_space_constraint(value, pltpu.VMEM)


def in_hbm(value):
    return pltpu.with_memory_space_constraint(value, pltpu.HBM)


def project(size, x_hbm, gain_hbm, wq_hbm, wk_hbm, wv_hbm, *refs):
    kept, given, x, gain, wq, wk, wv, scaled, total, sems = refs
    depth = x.shape[1]
    steps = depth // CHUNK
    pairs = [(x_hbm, x), (gain_hbm, gain), (wk_hbm, wk), (wv_hbm, wv)]
    small = [pltpu.make_async_copy(a, b, sems.at[steps + i]) for i, (a, b) in enumerate(pairs)]
    large = []
    for step in range(steps):
        part = pl.ds(step * CHUNK, CHUNK)
        large.append(pltpu.make_async_copy(wq_hbm.at[part], wq.at[part], sems.at[step]))
    small[0].start()
    small[1].start()
    for copy in large[:2]:
        copy.start()
    small[2].start()
    small[3].start()
    for copy in large[2:]:
        copy.start()
    small[0].wait()
    small[1].wait()
    wide = x[...].astype(F32)
    scaled[...] = (wide * gain[...]).astype(BF16)
    squares = jnp.sum(wide * wide, 1, keepdims=True)
    width = wq.shape[1]
    dot = functools.partial(jnp.dot, preferred_element_type=F32)
    for step, copy in enumerate(large):
        copy.wait()
        part = slice(step * CHUNK, (step + 1) * CHUNK)
        term = dot(scaled[:, part], wq[part])
        if step == 0:
            total[:, :width] = term
        else:
            total[:, :width] += term
        if step == 1:
            small[2].wait()
            total[:, width : width + HD] = dot(scaled[...], wk[...])
            small[3].wait()
            total[:, width + HD : width + 2 * HD] = dot(scaled[...], wv[...])
            total[:, width + 2 * HD :] = jnp.broadcast_to(squares, (squares.shape[0], HD))
    rows = kept.shape[1]
    me = lax.axis_index("gx")
    for mask in range(size):
        out = given if mask % 2 else kept
        start = pl.multiple_of((me ^ mask) * rows, 8)
        out[mask // 2] = total[pl.ds(start, rows), :]


def merge(kept, arrived, *outs):
    for index, out in enumerate(outs):
        out[...] = kept[index] + arrived[index]


def fetch_pieces(masks, width, w_hbm, pieces, sems, first):
    me = lax.axis_index("gy")
    copies = []
    for i, mask in enumerate(masks):
        source = w_hbm.at[:, columns(me ^ mask, width)]
        copies.append(pltpu.make_async_copy(source, pieces[i], sems.at[first + i]))
    return copies


def fetch_caches(after, k_hbm, v_hbm, k_turned, v, k, sems):
    del after
    rows, slots = k.shape[0], k.shape[1]
    copies = [pltpu.make_async_copy(k_hbm.at[r], k.at[r], sems.at[r]) for r in range(rows)]
    copies.append(pltpu.make_async_copy(v_hbm, v, sems.at[rows]))
    for copy in copies:
        copy.start()
    for row in range(rows):
        copies[row].wait()
        for start in range(0, slots, CHUNK):
            part = slice(start, start + CHUNK)
            k_turned[row, :, part] = k[row, part, :].T
    copies[rows].wait()


def fetch_weights(masks, after, w_hbm, *refs):
    del after
    *pieces, sems = refs
    copies = fetch_pieces(masks, pieces[0].shape[1], w_hbm, pieces, sems, 0)
    for copy in copies:
        copy.start()
    for copy in copies:
        copy.wait()


def attention(size, model, masks, lengths, cosine, sine, k, v, w_hbm, *refs):
    arrived = refs[:size]
    heads = refs[size]
    pieces = refs[size + 1 : size + 1 + len(masks)]
    q_rows, o_rows, scores, sems = refs[size + 1 + len(masks) :]
    copies = fetch_pieces(masks, pieces[0].shape[1], w_hbm, pieces, sems, 0) if masks else []
    for copy in copies:
        copy.start()
    rows, slots = k.shape[0], k.shape[2]
    group = heads.shape[1] // HD
    width = group * HD
    summed = arrived[0][...]
    for item in arrived[1:]:
        summed = summed + item[...].astype(F32)
    scale = lax.rsqrt(summed[:, width + 2 * HD :] / model + EPS)
    cosines, sines = cosine[...], sine[...]

    def turn(value):
        return value * cosines + pltpu.roll(value, HD // 2, 1) * sines

    for head in range(group):
        part = summed[:, head * HD : (head + 1) * HD] * scale
        q_rows[head] = turn(part).astype(BF16).astype(F32)
    new_keys = turn(summed[:, width : width + HD] * scale).astype(BF16).astype(F32)
    new_values = (summed[:, width + HD : width + 2 * HD] * scale).astype(BF16).astype(F32)
    rate = HD ** (-0.5) * math.log2(math.e)
    half = slots // 2
    slot = lax.broadcasted_iota(jnp.int32, (2 * group, half), 1) + half
    second = lax.broadcasted_iota(jnp.int32, (2 * group, 1), 0) >= group
    empty = jnp.zeros((group, HD), F32)
    own, top = [], []
    for row in range(0, rows, 2):
        first, other = q_rows[:, row, :], q_rows[:, row + 1, :]
        queries = jnp.concatenate(
            [jnp.concatenate([first, empty], 1), jnp.concatenate([empty, other], 1)], 0
        )
        keys = jnp.concatenate([k[row], k[row + 1]], 0)
        raw = jnp.dot(queries.astype(BF16), keys, preferred_element_type=F32)
        low = raw[:, :half]
        limit = jnp.where(second, lengths[row + 1 : row + 2, :1], lengths[row : row + 1, :1])
        high = jnp.where(slot < limit, raw[:, half:], -jnp.inf)
        mine = slice(row * group, (row + 2) * group)
        scores[mine, :half] = low
        scores[mine, half:] = high
        both = jnp.concatenate(
            [first * new_keys[row : row + 1], other * new_keys[row + 1 : row + 2]], 0
        )
        own.append(jnp.sum(both, 1, keepdims=True))
        top.append(jnp.maximum(jnp.max(jnp.maximum(low, high), 1, keepdims=True), own[-1]))

    def soften(pair):
        mine = slice(2 * pair * group, (2 * pair + 2) * group)
        probs = jnp.exp2((scores[mine] - top[pair]) * rate)
        own_prob = jnp.exp2((own[pair] - top[pair]) * rate)
        share = 1.0 / (jnp.sum(probs, 1, keepdims=True) + own_prob)
        return probs.astype(BF16), own_prob, share

    ready = soften(0)
    for pair in range(rows // 2):
        probs, own_prob, share = ready
        if pair + 1 < rows // 2:
            ready = soften(pair + 1)
        sides = jnp.concatenate([v[2 * pair], v[2 * pair + 1]], 1)
        mixed = jnp.dot(probs, sides, preferred_element_type=F32)
        for side in range(2):
            row = 2 * pair + side
            mine = slice(side * group, (side + 1) * group)
            value = mixed[mine, side * HD : (side + 1) * HD]
            extra = own_prob[mine] * new_values[row : row + 1]
            o_rows[:, row, :] = (value + extra) * share[mine]
    for head in range(group):
        heads[:, head * HD : (head + 1) * HD] = o_rows[head].astype(BF16)
    for copy in copies:
        copy.wait()


def gather_rows(blocks, gathered):
    me = lax.axis_index("gx")
    rows = blocks[0].shape[0]
    for mask, block in enumerate(blocks):
        start = pl.multiple_of((me ^ mask) * rows, 8)
        gathered[pl.ds(start, rows), :] = block[...].astype(F32)
    return gathered[...].astype(BF16)


def project_out(size, w, *refs):
    blocks, out, gathered = refs[:size], refs[-2], refs[-1]
    heads = gather_rows(blocks, gathered)
    out[...] = jnp.dot(heads, w[...], preferred_element_type=F32).astype(out.dtype)


def stream_out(size, mask, w_hbm, x_hbm, *refs):
    blocks = refs[:size]
    out, gathered, w, x, sems = refs[-5:]
    width = out.shape[1]
    me = lax.axis_index("gy")
    steps = w.shape[0] // (2 * CHUNK)
    copies = []
    for step in range(steps):
        part = pl.ds(step * 2 * CHUNK, 2 * CHUNK)
        source = w_hbm.at[part, columns(me ^ mask, width)]
        copies.append(pltpu.make_async_copy(source, w.at[part], sems.at[step]))
    if not mask:
        source = x_hbm.at[:, columns(me, width)]
        copies.append(pltpu.make_async_copy(source, x, sems.at[steps]))
    for copy in copies:
        copy.start()
    heads = gather_rows(blocks, gathered)
    total = None
    for step in range(steps):
        copies[step].wait()
        part = slice(step * 2 * CHUNK, (step + 1) * 2 * CHUNK)
        term = jnp.dot(heads[:, part], w[part], preferred_element_type=F32)
        total = term if total is None else total + term
    if not mask:
        copies[steps].wait()
        total = total + x[...].astype(F32)
    out[...] = total.astype(out.dtype)


def finish(own, *refs):
    *arrived, out = refs
    total = own[...]
    for item in arrived:
        total = total + item[...].astype(F32)
    out[...] = total.astype(BF16)


def assemble(size, *refs):
    blocks, out, sems = refs[:size], refs[size], refs[size + 1]
    me = lax.axis_index("gy")
    width = blocks[0].shape[1]
    copies = []
    for mask in range(size):
        target = out.at[:, columns(me ^ mask, width)]
        copies.append(pltpu.make_async_copy(blocks[mask], target, sems.at[mask]))
    for copy in copies:
        copy.start()
    for copy in copies:
        copy.wait()


def swap(value, axis, size, mask):
    return lax.ppermute(value, axis, [(i, i ^ mask) for i in range(size)])


def solution(mesh):
    size_x = mesh.shape["gx"]
    size_y = mesh.shape["gy"]
    struct = jax.ShapeDtypeStruct
    sems = lambda n: pltpu.SemaphoreType.DMA((n,))
    order = list(range(size_y - 1, -1, -1))
    quarter = max(size_y // 4, 1)
    middle, late = order[: 2 * quarter], order[2 * quarter : -1]

    def shards(inputs, gain, w_query, w_key, w_value, w_output, key_cache, value_cache, lengths):
        batch, depth = inputs.shape
        width = w_query.shape[1]
        rows = key_cache.shape[0]
        packed = width + 3 * HD
        block = w_output.shape[1] // size_y
        piece = pltpu.VMEM((width, block), BF16)
        piece_bytes = 2 * width * block

        levels = size_x // 2
        kept, given = pl.pallas_call(
            functools.partial(project, size_x),
            out_shape=[pltpu.VMEM((levels, rows, packed), F32)] * 2,
            in_specs=[ANY] * 5,
            out_specs=[VMEM] * 2,
            scratch_shapes=[
                pltpu.VMEM(inputs.shape, BF16),
                pltpu.VMEM((1, depth), F32),
                pltpu.VMEM(w_query.shape, BF16),
                pltpu.VMEM(w_key.shape, BF16),
                pltpu.VMEM(w_value.shape, BF16),
                pltpu.VMEM(inputs.shape, BF16),
                pltpu.VMEM((batch, packed), F32),
                sems(depth // CHUNK + 4),
            ],
            compiler_params=params(28),
            cost_estimate=cost(2 * batch * depth * packed, 2 * depth * packed),
            name="project",
        )(*[in_hbm(a) for a in (inputs, gain.reshape(1, depth), w_query, w_key, w_value)])
        sums = pl.pallas_call(
            merge,
            out_shape=[pltpu.VMEM((rows, packed), F32)] * levels,
            in_specs=[VMEM] * 2,
            out_specs=[VMEM] * levels,
            compiler_params=params(4),
            name="merge",
        )(in_vmem(kept), in_vmem(swap(given, "gx", size_x, 1)))
        arrived = [sums[0]] + [swap(sums[j], "gx", size_x, 2 * j) for j in range(1, levels)]

        keys, values = pl.pallas_call(
            fetch_caches,
            out_shape=[
                pltpu.VMEM((rows, HD, key_cache.shape[1]), BF16),
                pltpu.VMEM(value_cache.shape, BF16),
            ],
            in_specs=[ANY] * 3,
            out_specs=[VMEM] * 2,
            scratch_shapes=[pltpu.VMEM(key_cache.shape, BF16), sems(rows + 1)],
            compiler_params=params(12),
            cost_estimate=cost(0, 4 * key_cache.size),
            name="fetch_caches",
        )(sums[0], in_hbm(key_cache), in_hbm(value_cache))
        pieces = []

        half = HD // 2
        inverse = ROPE_BASE ** (-(jnp.arange(half, dtype=F32) * 2.0 / HD))
        angles = lengths.astype(F32)[:, None] * inverse[None, :]
        cosine, sine = jnp.cos(angles), jnp.sin(angles)
        heads, *more = pl.pallas_call(
            functools.partial(attention, levels, depth * size_x, middle),
            out_shape=[pltpu.VMEM((rows, width), BF16)] + [piece] * len(middle),
            in_specs=[VMEM, VMEM, VMEM, VMEM, VMEM, ANY] + [VMEM] * levels,
            out_specs=[VMEM] * (1 + len(middle)),
            scratch_shapes=[
                pltpu.VMEM((width // HD, rows, HD), F32),
                pltpu.VMEM((width // HD, rows, HD), F32),
                pltpu.VMEM((rows * (width // HD), key_cache.shape[1]), F32),
                sems(max(len(middle), 1)),
            ],
            compiler_params=params(8),
            cost_estimate=cost(4 * key_cache.size * (width // HD), piece_bytes * len(middle)),
            name="attention",
        )(
            jnp.broadcast_to(lengths[:, None], (rows, HD)),
            jnp.concatenate([cosine, cosine], 1),
            jnp.concatenate([-sine, sine], 1),
            in_vmem(keys),
            in_vmem(values),
            in_hbm(w_output),
            *[in_vmem(a) for a in arrived],
        )
        pieces += more
        gathered = [heads] + [swap(heads, "gx", size_x, m) for m in range(1, size_x)]

        pieces += pl.pallas_call(
            functools.partial(fetch_weights, late),
            out_shape=[piece] * len(late),
            in_specs=[ANY] * 2,
            out_specs=[VMEM] * len(late),
            scratch_shapes=[sems(len(late))],
            compiler_params=params(4),
            cost_estimate=cost(0, piece_bytes * len(late)),
            name="fetch_weights",
        )(heads, in_hbm(w_output))

        terms = {}
        for index, mask in enumerate(order):
            kind = BF16 if mask else F32
            ready = index < len(pieces)
            shared = dict(
                out_shape=pltpu.VMEM((batch, block), kind),
                out_specs=VMEM,
                compiler_params=params(12),
                cost_estimate=cost(2 * batch * width * block, piece_bytes),
            )
            rows_in = [in_vmem(a) for a in gathered]
            scratch = [pltpu.VMEM((batch, width), F32)]
            if ready:
                term = pl.pallas_call(
                    functools.partial(project_out, size_x),
                    in_specs=[VMEM] * (1 + size_x),
                    scratch_shapes=scratch,
                    name="project_out",
                    **shared,
                )(in_vmem(pieces[index]), *rows_in)
            else:
                scratch += [
                    pltpu.VMEM((width, block), BF16),
                    pltpu.VMEM((batch, block), BF16),
                    sems(width // (2 * CHUNK) + 1),
                ]
                term = pl.pallas_call(
                    functools.partial(stream_out, size_x, mask),
                    in_specs=[ANY] * 2 + [VMEM] * size_x,
                    scratch_shapes=scratch,
                    name="stream_out",
                    **shared,
                )(in_hbm(w_output), in_hbm(inputs), *rows_in)
            terms[mask] = swap(term, "gy", size_y, mask) if mask else term
        done = pl.pallas_call(
            finish,
            out_shape=pltpu.VMEM((batch, block), BF16),
            in_specs=[VMEM] * size_y,
            out_specs=VMEM,
            compiler_params=params(4),
            name="finish",
        )(*[in_vmem(terms[m]) for m in range(size_y)])
        blocks = [done] + [swap(done, "gy", size_y, m) for m in range(1, size_y)]
        return pl.pallas_call(
            functools.partial(assemble, size_y),
            out_shape=struct((batch, block * size_y), BF16),
            in_specs=[VMEM] * size_y,
            out_specs=ANY,
            scratch_shapes=[sems(size_y)],
            compiler_params=params(4),
            name="assemble",
        )(*[in_vmem(b) for b in blocks])

    placed = (
        P("groups", "gx"),
        P("gx"),
        P("gx", "gy"),
        P("gx", "gy"),
        P("gx", "gy"),
        P("gy", "gx"),
        P(("groups", "gx"), None, "gy"),
        P(("groups", "gx"), None, "gy"),
        P(("groups", "gx")),
    )
    return jax.shard_map(
        shards, mesh=mesh, in_specs=placed, out_specs=P("groups", "gx"), check_vma=False
    )
```

```python
import functools
import math

import jax
import jax.numpy as jnp
from jax import lax
from jax.experimental import pallas as pl
from jax.experimental.pallas import tpu as pltpu
from jax.sharding import PartitionSpec as P

HD = 128
EPS = 1e-05
ROPE_BASE = 500000.0
CHUNK = 256
F32 = jnp.float32
BF16 = jnp.bfloat16
F16 = jnp.float16
SQUARES = 2.0**-8

ANY = pl.BlockSpec(memory_space=pl.ANY)
VMEM = pl.BlockSpec(memory_space=pltpu.VMEM)
MIB = 1 << 20


def columns(index, width):
    return pl.ds(pl.multiple_of(index * width, HD), width)


def params(mib):
    return pltpu.CompilerParams(vmem_limit_bytes=mib * MIB)


def cost(flops, nbytes):
    return pl.CostEstimate(flops=flops, bytes_accessed=nbytes, transcendentals=0)


def in_vmem(value):
    return pltpu.with_memory_space_constraint(value, pltpu.VMEM)


def in_hbm(value):
    return pltpu.with_memory_space_constraint(value, pltpu.HBM)


def project(size, x_hbm, gain_hbm, wq_hbm, wk_hbm, wv_hbm, *refs):
    outs = refs[:size]
    x, gain, wq, wk, wv, scaled, total, sems = refs[size:]
    depth = x.shape[1]
    steps = depth // CHUNK
    pairs = [(x_hbm, x), (gain_hbm, gain), (wk_hbm, wk), (wv_hbm, wv)]
    small = [pltpu.make_async_copy(a, b, sems.at[steps + i]) for i, (a, b) in enumerate(pairs)]
    large = []
    for step in range(steps):
        part = pl.ds(step * CHUNK, CHUNK)
        large.append(pltpu.make_async_copy(wq_hbm.at[part], wq.at[part], sems.at[step]))
    small[0].start()
    small[1].start()
    for copy in large[:2]:
        copy.start()
    small[2].start()
    small[3].start()
    for copy in large[2:]:
        copy.start()
    small[0].wait()
    small[1].wait()
    wide = x[...].astype(F32)
    scaled[...] = (wide * gain[...]).astype(BF16)
    squares = jnp.sum(wide * wide, 1, keepdims=True)
    width = wq.shape[1]
    dot = functools.partial(jnp.dot, preferred_element_type=F32)
    for step, copy in enumerate(large):
        copy.wait()
        part = slice(step * CHUNK, (step + 1) * CHUNK)
        term = dot(scaled[:, part], wq[part])
        if step == 0:
            total[:, :width] = term
        else:
            total[:, :width] += term
        if step == 1:
            small[2].wait()
            total[:, width : width + HD] = dot(scaled[...], wk[...])
            small[3].wait()
            total[:, width + HD : width + 2 * HD] = dot(scaled[...], wv[...])
            total[:, width + 2 * HD :] = jnp.broadcast_to(squares, (squares.shape[0], HD))
    rows = outs[0].shape[0]
    me = lax.axis_index("gx")
    first = lax.broadcasted_iota(jnp.int32, (rows, HD), 1) < HD // 2
    for mask, out in enumerate(outs):
        start = pl.multiple_of((me ^ mask) * rows, 8)
        part = total[pl.ds(start, rows), :]
        if mask:
            whole = part[:, width + 2 * HD :] * SQUARES
            high = whole.astype(BF16).astype(F32)
            out[:, : width + 2 * HD] = part[:, : width + 2 * HD]
            out[:, width + 2 * HD :] = jnp.where(first, high, whole - high)
        else:
            out[...] = part


def fetch_pieces(masks, width, w_hbm, pieces, sems, first):
    me = lax.axis_index("gy")
    copies = []
    for i, mask in enumerate(masks):
        source = w_hbm.at[:, columns(me ^ mask, width)]
        copies.append(pltpu.make_async_copy(source, pieces[i], sems.at[first + i]))
    return copies


def fetch_keys(after, k_hbm, k_turned, k, sems):
    del after
    rows, slots = k.shape[0], k.shape[1]
    copies = [pltpu.make_async_copy(k_hbm.at[r], k.at[r], sems.at[r]) for r in range(rows)]
    for copy in copies:
        copy.start()
    for row in range(rows):
        copies[row].wait()
        for start in range(0, slots, CHUNK):
            part = slice(start, start + CHUNK)
            k_turned[row, :, part] = k[row, part, :].T


def fetch_weights(masks, after, w_hbm, *refs):
    del after
    *pieces, sems = refs
    copies = fetch_pieces(masks, pieces[0].shape[1], w_hbm, pieces, sems, 0)
    for copy in copies:
        copy.start()
    for copy in copies:
        copy.wait()


def attention(size, model, masks, lengths, cosine, sine, k, v_hbm, w_hbm, *refs):
    arrived = refs[:size]
    heads = refs[size]
    pieces = refs[size + 1 : size + 1 + len(masks)]
    q_rows, o_rows, scores, v, sems = refs[size + 1 + len(masks) :]
    copies = [pltpu.make_async_copy(v_hbm, v, sems.at[0])]
    if masks:
        copies += fetch_pieces(masks, pieces[0].shape[1], w_hbm, pieces, sems, 1)
    for copy in copies:
        copy.start()
    rows, slots = k.shape[0], k.shape[2]
    group = heads.shape[1] // HD
    width = group * HD
    summed = arrived[0][:, : width + 2 * HD]
    squares = arrived[0][:, width + 2 * HD :]
    for item in arrived[1:]:
        summed = summed + item[:, : width + 2 * HD].astype(F32)
        parts = item[:, width + 2 * HD :].astype(F32)
        squares = squares + (parts + pltpu.roll(parts, HD // 2, 1)) * (1.0 / SQUARES)
    scale = lax.rsqrt(squares / model + EPS)
    cosines, sines = cosine[...], sine[...]

    def turn(value):
        return value * cosines + pltpu.roll(value, HD // 2, 1) * sines

    for head in range(group):
        part = summed[:, head * HD : (head + 1) * HD] * scale
        q_rows[head * rows : (head + 1) * rows] = turn(part).astype(BF16).astype(F32)
    new_keys = turn(summed[:, width : width + HD] * scale).astype(BF16).astype(F32)
    new_values = (summed[:, width + HD : width + 2 * HD] * scale).astype(BF16).astype(F32)
    rate = HD ** (-0.5) * math.log2(math.e)
    half = slots // 2
    slot = lax.broadcasted_iota(jnp.int32, (2 * group, half), 1) + half
    second = lax.broadcasted_iota(jnp.int32, (2 * group, 1), 0) >= group
    empty = jnp.zeros((group, HD), F32)
    own, top = [], []
    for row in range(0, rows, 2):
        first = q_rows[pl.ds(row, group, stride=rows), :]
        other = q_rows[pl.ds(row + 1, group, stride=rows), :]
        queries = jnp.concatenate(
            [jnp.concatenate([first, empty], 1), jnp.concatenate([empty, other], 1)], 0
        )
        keys = jnp.concatenate([k[row], k[row + 1]], 0)
        raw = jnp.dot(queries.astype(BF16), keys, preferred_element_type=F32)
        low = raw[:, :half]
        limit = jnp.where(second, lengths[row + 1 : row + 2, :1], lengths[row : row + 1, :1])
        high = jnp.where(slot < limit, raw[:, half:], -jnp.inf)
        mine = slice(row * group, (row + 2) * group)
        scores[mine, :half] = low
        scores[mine, half:] = high
        both = jnp.concatenate(
            [first * new_keys[row : row + 1], other * new_keys[row + 1 : row + 2]], 0
        )
        own.append(jnp.sum(both, 1, keepdims=True))
        top.append(jnp.maximum(jnp.max(jnp.maximum(low, high), 1, keepdims=True), own[-1]))

    def soften(pair):
        mine = slice(2 * pair * group, (2 * pair + 2) * group)
        probs = jnp.exp2((scores[mine] - top[pair]) * rate)
        own_prob = jnp.exp2((own[pair] - top[pair]) * rate)
        share = 1.0 / (jnp.sum(probs, 1, keepdims=True) + own_prob)
        return (probs * share).astype(BF16), (own_prob * share).astype(BF16).astype(F32)

    ready = soften(0)
    for pair in range(rows // 2):
        weights, own_weight = ready
        if pair + 1 < rows // 2:
            ready = soften(pair + 1)
        if not pair:
            copies[0].wait()
        sides = jnp.concatenate([v[2 * pair], v[2 * pair + 1]], 1)
        mixed = jnp.dot(weights, sides, preferred_element_type=F32)
        for side in range(2):
            row = 2 * pair + side
            mine = slice(side * group, (side + 1) * group)
            value = mixed[mine, side * HD : (side + 1) * HD]
            extra = own_weight[mine] * new_values[row : row + 1]
            o_rows[pl.ds(row, group, stride=rows), :] = value + extra
    for head in range(group):
        heads[:, head * HD : (head + 1) * HD] = o_rows[head * rows : (head + 1) * rows].astype(BF16)
    for copy in copies[1:]:
        copy.wait()


def gather_rows(blocks, gathered):
    me = lax.axis_index("gx")
    rows = blocks[0].shape[0]
    for mask, block in enumerate(blocks):
        start = pl.multiple_of((me ^ mask) * rows, 8)
        gathered[pl.ds(start, rows), :] = block[...].astype(F32)
    return gathered[...].astype(BF16)


def project_out(size, w, *refs):
    blocks, out, gathered = refs[:size], refs[-2], refs[-1]
    heads = gather_rows(blocks, gathered)
    out[...] = jnp.dot(heads, w[...], preferred_element_type=F32).astype(out.dtype)


def stream_out(size, mask, w_hbm, x_hbm, *refs):
    blocks = refs[:size]
    out, gathered, w, x, sems = refs[-5:]
    width = out.shape[1]
    me = lax.axis_index("gy")
    steps = w.shape[0] // (2 * CHUNK)
    copies = []
    for step in range(steps):
        part = pl.ds(step * 2 * CHUNK, 2 * CHUNK)
        source = w_hbm.at[part, columns(me ^ mask, width)]
        copies.append(pltpu.make_async_copy(source, w.at[part], sems.at[step]))
    if not mask:
        source = x_hbm.at[:, columns(me, width)]
        copies.append(pltpu.make_async_copy(source, x, sems.at[steps]))
    for copy in copies:
        copy.start()
    heads = gather_rows(blocks, gathered)
    total = None
    for step in range(steps):
        copies[step].wait()
        part = slice(step * 2 * CHUNK, (step + 1) * 2 * CHUNK)
        term = jnp.dot(heads[:, part], w[part], preferred_element_type=F32)
        total = term if total is None else total + term
    if not mask:
        copies[steps].wait()
        total = total + x[...].astype(F32)
    out[...] = total.astype(out.dtype)


def finish(own, *refs):
    *arrived, out = refs
    total = own[...]
    for item in arrived:
        total = total + item[...].astype(F32)
    out[...] = total.astype(BF16)


def assemble(size, *refs):
    blocks, out, sems = refs[:size], refs[size], refs[size + 1]
    me = lax.axis_index("gy")
    width = blocks[0].shape[1]
    copies = []
    for mask in range(size):
        target = out.at[:, columns(me ^ mask, width)]
        copies.append(pltpu.make_async_copy(blocks[mask], target, sems.at[mask]))
    for copy in copies:
        copy.start()
    for copy in copies:
        copy.wait()


def swap(value, axis, size, mask):
    return lax.ppermute(value, axis, [(i, i ^ mask) for i in range(size)])


def solution(mesh):
    size_x = mesh.shape["gx"]
    size_y = mesh.shape["gy"]
    struct = jax.ShapeDtypeStruct
    sems = lambda n: pltpu.SemaphoreType.DMA((n,))
    order = list(range(size_y - 1, -1, -1))
    quarter = max(size_y // 4, 1)
    middle, late = order[: 2 * quarter], order[2 * quarter : -1]

    def shards(inputs, gain, w_query, w_key, w_value, w_output, key_cache, value_cache, lengths):
        batch, depth = inputs.shape
        width = w_query.shape[1]
        rows = key_cache.shape[0]
        packed = width + 3 * HD
        block = w_output.shape[1] // size_y
        piece = pltpu.VMEM((width, block), BF16)
        piece_bytes = 2 * width * block

        sums = pl.pallas_call(
            functools.partial(project, size_x),
            out_shape=[pltpu.VMEM((rows, packed), F32)] * size_x,
            in_specs=[ANY] * 5,
            out_specs=[VMEM] * size_x,
            scratch_shapes=[
                pltpu.VMEM(inputs.shape, BF16),
                pltpu.VMEM((1, depth), F32),
                pltpu.VMEM(w_query.shape, BF16),
                pltpu.VMEM(w_key.shape, BF16),
                pltpu.VMEM(w_value.shape, BF16),
                pltpu.VMEM(inputs.shape, BF16),
                pltpu.VMEM((batch, packed), F32),
                sems(depth // CHUNK + 4),
            ],
            compiler_params=params(28),
            cost_estimate=cost(2 * batch * depth * packed, 2 * depth * packed),
            name="project",
        )(*[in_hbm(a) for a in (inputs, gain.reshape(1, depth), w_query, w_key, w_value)])
        arrived = [sums[0]]
        for mask in range(1, size_x):
            arrived.append(swap(sums[mask].astype(F16), "gx", size_x, mask).astype(F32))
        keys = pl.pallas_call(
            fetch_keys,
            out_shape=pltpu.VMEM((rows, HD, key_cache.shape[1]), BF16),
            in_specs=[ANY] * 2,
            out_specs=VMEM,
            scratch_shapes=[pltpu.VMEM(key_cache.shape, BF16), sems(rows)],
            compiler_params=params(12),
            cost_estimate=cost(0, 2 * key_cache.size),
            name="fetch_keys",
        )(sums[0], in_hbm(key_cache))
        pieces = []

        half = HD // 2
        inverse = ROPE_BASE ** (-(jnp.arange(half, dtype=F32) * 2.0 / HD))
        angles = lengths.astype(F32)[:, None] * inverse[None, :]
        cosine, sine = jnp.cos(angles), jnp.sin(angles)
        heads, *more = pl.pallas_call(
            functools.partial(attention, size_x, depth * size_x, middle),
            out_shape=[pltpu.VMEM((rows, width), BF16)] + [piece] * len(middle),
            in_specs=[VMEM, VMEM, VMEM, VMEM, ANY, ANY] + [VMEM] * size_x,
            out_specs=[VMEM] * (1 + len(middle)),
            scratch_shapes=[
                pltpu.VMEM((rows * (width // HD), HD), F32),
                pltpu.VMEM((rows * (width // HD), HD), F32),
                pltpu.VMEM((rows * (width // HD), key_cache.shape[1]), F32),
                pltpu.VMEM(value_cache.shape, BF16),
                sems(1 + len(middle)),
            ],
            compiler_params=params(12),
            cost_estimate=cost(4 * key_cache.size * (width // HD), piece_bytes * len(middle)),
            name="attention",
        )(
            jnp.broadcast_to(lengths[:, None], (rows, HD)),
            jnp.concatenate([cosine, cosine], 1),
            jnp.concatenate([-sine, sine], 1),
            in_vmem(keys),
            in_hbm(value_cache),
            in_hbm(w_output),
            *[in_vmem(a) for a in arrived],
        )
        pieces += more
        gathered = [heads] + [swap(heads, "gx", size_x, m) for m in range(1, size_x)]

        pieces += pl.pallas_call(
            functools.partial(fetch_weights, late),
            out_shape=[piece] * len(late),
            in_specs=[ANY] * 2,
            out_specs=[VMEM] * len(late),
            scratch_shapes=[sems(len(late))],
            compiler_params=params(4),
            cost_estimate=cost(0, piece_bytes * len(late)),
            name="fetch_weights",
        )(heads, in_hbm(w_output))

        terms = {}
        for index, mask in enumerate(order):
            kind = BF16 if mask else F32
            ready = index < len(pieces)
            shared = dict(
                out_shape=pltpu.VMEM((batch, block), kind),
                out_specs=VMEM,
                compiler_params=params(12),
                cost_estimate=cost(2 * batch * width * block, piece_bytes),
            )
            rows_in = [in_vmem(a) for a in gathered]
            scratch = [pltpu.VMEM((batch, width), F32)]
            if ready:
                term = pl.pallas_call(
                    functools.partial(project_out, size_x),
                    in_specs=[VMEM] * (1 + size_x),
                    scratch_shapes=scratch,
                    name="project_out",
                    **shared,
                )(in_vmem(pieces[index]), *rows_in)
            else:
                scratch += [
                    pltpu.VMEM((width, block), BF16),
                    pltpu.VMEM((batch, block), BF16),
                    sems(width // (2 * CHUNK) + 1),
                ]
                term = pl.pallas_call(
                    functools.partial(stream_out, size_x, mask),
                    in_specs=[ANY] * 2 + [VMEM] * size_x,
                    scratch_shapes=scratch,
                    name="stream_out",
                    **shared,
                )(in_hbm(w_output), in_hbm(inputs), *rows_in)
            terms[mask] = swap(term, "gy", size_y, mask) if mask else term
        done = pl.pallas_call(
            finish,
            out_shape=pltpu.VMEM((batch, block), BF16),
            in_specs=[VMEM] * size_y,
            out_specs=VMEM,
            compiler_params=params(4),
            name="finish",
        )(*[in_vmem(terms[m]) for m in range(size_y)])
        blocks = [done] + [swap(done, "gy", size_y, m) for m in range(1, size_y)]
        return pl.pallas_call(
            functools.partial(assemble, size_y),
            out_shape=struct((batch, block * size_y), BF16),
            in_specs=[VMEM] * size_y,
            out_specs=ANY,
            scratch_shapes=[sems(size_y)],
            compiler_params=params(4),
            name="assemble",
        )(*[in_vmem(b) for b in blocks])

    placed = (
        P("groups", "gx"),
        P("gx"),
        P("gx", "gy"),
        P("gx", "gy"),
        P("gx", "gy"),
        P("gy", "gx"),
        P(("groups", "gx"), None, "gy"),
        P(("groups", "gx"), None, "gy"),
        P(("groups", "gx")),
    )
    return jax.shard_map(
        shards, mesh=mesh, in_specs=placed, out_specs=P("groups", "gx"), check_vma=False
    )
```

```python
import functools
import math

import jax
import jax.numpy as jnp
from jax import lax
from jax.experimental import pallas as pl
from jax.experimental.pallas import tpu as pltpu
from jax.sharding import PartitionSpec as P

HD = 128
EPS = 1e-05
ROPE_BASE = 500000.0
CHUNK = 256
F32 = jnp.float32
BF16 = jnp.bfloat16
F16 = jnp.float16
SQUARES = 2.0**-8

ANY = pl.BlockSpec(memory_space=pl.ANY)
VMEM = pl.BlockSpec(memory_space=pltpu.VMEM)
MIB = 1 << 20


def columns(index, width):
    return pl.ds(pl.multiple_of(index * width, HD), width)


def params(mib):
    return pltpu.CompilerParams(vmem_limit_bytes=mib * MIB)


def cost(flops, nbytes):
    return pl.CostEstimate(flops=flops, bytes_accessed=nbytes, transcendentals=0)


def in_vmem(value):
    return pltpu.with_memory_space_constraint(value, pltpu.VMEM)


def in_hbm(value):
    return pltpu.with_memory_space_constraint(value, pltpu.HBM)


def project(x_hbm, gain_hbm, wq_hbm, wk_hbm, wv_hbm, *refs):
    total, x, gain, wq, wk, wv, scaled, sems = refs
    depth = x.shape[1]
    steps = depth // CHUNK
    pairs = [(x_hbm, x), (gain_hbm, gain), (wk_hbm, wk), (wv_hbm, wv)]
    small = [pltpu.make_async_copy(a, b, sems.at[steps + i]) for i, (a, b) in enumerate(pairs)]
    large = []
    for step in range(steps):
        part = pl.ds(step * CHUNK, CHUNK)
        large.append(pltpu.make_async_copy(wq_hbm.at[part], wq.at[part], sems.at[step]))
    small[0].start()
    small[1].start()
    for copy in large[:2]:
        copy.start()
    small[2].start()
    small[3].start()
    for copy in large[2:]:
        copy.start()
    small[0].wait()
    small[1].wait()
    wide = x[...].astype(F32)
    scaled[...] = (wide * gain[...]).astype(BF16)
    squares = jnp.sum(wide * wide, 1, keepdims=True)
    width = wq.shape[1]
    dot = functools.partial(jnp.dot, preferred_element_type=F32)
    for step, copy in enumerate(large):
        copy.wait()
        part = slice(step * CHUNK, (step + 1) * CHUNK)
        term = dot(scaled[:, part], wq[part])
        if step == 0:
            total[:, :width] = term
        else:
            total[:, :width] += term
        if step == 1:
            small[2].wait()
            total[:, width : width + HD] = dot(scaled[...], wk[...])
            small[3].wait()
            total[:, width + HD : width + 2 * HD] = dot(scaled[...], wv[...])
            total[:, width + 2 * HD :] = jnp.broadcast_to(squares, (squares.shape[0], HD))


def split(total, weights, *outs):
    del weights
    width = total.shape[1] - 3 * HD
    rows = outs[0].shape[0]
    me = lax.axis_index("gx")
    first = lax.broadcasted_iota(jnp.int32, (rows, HD), 1) < HD // 2
    for mask, out in enumerate(outs):
        start = pl.multiple_of((me ^ mask) * rows, 8)
        part = total[pl.ds(start, rows), :]
        if mask:
            whole = part[:, width + 2 * HD :] * SQUARES
            high = whole.astype(BF16).astype(F32)
            out[:, : width + 2 * HD] = part[:, : width + 2 * HD]
            out[:, width + 2 * HD :] = jnp.where(first, high, whole - high)
        else:
            out[...] = part


def turn_keys(after, k, v, k_turned):
    del after, v
    rows, slots = k.shape[0], k.shape[1]
    for row in range(rows):
        for start in range(0, slots, CHUNK):
            part = slice(start, start + CHUNK)
            k_turned[row, :, part] = k[row, part, :].T


def attention(size, model, weights, lengths, cosine, sine, k, v, *refs):
    del weights
    arrived = refs[:size]
    heads, q_rows, o_rows, scores = refs[size:]
    rows, slots = k.shape[0], k.shape[2]
    group = heads.shape[1] // HD
    width = group * HD
    summed = arrived[0][:, : width + 2 * HD]
    squares = arrived[0][:, width + 2 * HD :]
    for item in arrived[1:]:
        summed = summed + item[:, : width + 2 * HD].astype(F32)
        parts = item[:, width + 2 * HD :].astype(F32)
        squares = squares + (parts + pltpu.roll(parts, HD // 2, 1)) * (1.0 / SQUARES)
    scale = lax.rsqrt(squares / model + EPS)
    cosines, sines = cosine[...], sine[...]

    def turn(value):
        return value * cosines + pltpu.roll(value, HD // 2, 1) * sines

    for head in range(group):
        part = summed[:, head * HD : (head + 1) * HD] * scale
        q_rows[head * rows : (head + 1) * rows] = turn(part).astype(BF16).astype(F32)
    new_keys = turn(summed[:, width : width + HD] * scale).astype(BF16).astype(F32)
    new_values = (summed[:, width + HD : width + 2 * HD] * scale).astype(BF16).astype(F32)
    rate = HD ** (-0.5) * math.log2(math.e)
    half = slots // 2
    slot = lax.broadcasted_iota(jnp.int32, (2 * group, half), 1) + half
    second = lax.broadcasted_iota(jnp.int32, (2 * group, 1), 0) >= group
    empty = jnp.zeros((group, HD), F32)
    own, top = [], []
    for row in range(0, rows, 2):
        first = q_rows[pl.ds(row, group, stride=rows), :]
        other = q_rows[pl.ds(row + 1, group, stride=rows), :]
        queries = jnp.concatenate(
            [jnp.concatenate([first, empty], 1), jnp.concatenate([empty, other], 1)], 0
        )
        keys = jnp.concatenate([k[row], k[row + 1]], 0)
        raw = jnp.dot(queries.astype(BF16), keys, preferred_element_type=F32)
        low = raw[:, :half]
        limit = jnp.where(second, lengths[row + 1 : row + 2, :1], lengths[row : row + 1, :1])
        high = jnp.where(slot < limit, raw[:, half:], -jnp.inf)
        mine = slice(row * group, (row + 2) * group)
        scores[mine, :half] = low
        scores[mine, half:] = high
        both = jnp.concatenate(
            [first * new_keys[row : row + 1], other * new_keys[row + 1 : row + 2]], 0
        )
        own.append(jnp.sum(both, 1, keepdims=True))
        top.append(jnp.maximum(jnp.max(jnp.maximum(low, high), 1, keepdims=True), own[-1]))

    def soften(pair):
        mine = slice(2 * pair * group, (2 * pair + 2) * group)
        probs = jnp.exp2((scores[mine] - top[pair]) * rate)
        own_prob = jnp.exp2((own[pair] - top[pair]) * rate)
        share = 1.0 / (jnp.sum(probs, 1, keepdims=True) + own_prob)
        return (probs * share).astype(BF16), (own_prob * share).astype(BF16).astype(F32)

    ready = soften(0)
    for pair in range(rows // 2):
        weights, own_weight = ready
        if pair + 1 < rows // 2:
            ready = soften(pair + 1)
        sides = jnp.concatenate([v[2 * pair], v[2 * pair + 1]], 1)
        mixed = jnp.dot(weights, sides, preferred_element_type=F32)
        for side in range(2):
            row = 2 * pair + side
            mine = slice(side * group, (side + 1) * group)
            value = mixed[mine, side * HD : (side + 1) * HD]
            extra = own_weight[mine] * new_values[row : row + 1]
            o_rows[pl.ds(row, group, stride=rows), :] = value + extra
    for head in range(group):
        heads[:, head * HD : (head + 1) * HD] = o_rows[head * rows : (head + 1) * rows].astype(BF16)


def gather_rows(blocks, gathered):
    me = lax.axis_index("gx")
    rows = blocks[0].shape[0]
    for mask, block in enumerate(blocks):
        start = pl.multiple_of((me ^ mask) * rows, 8)
        gathered[pl.ds(start, rows), :] = block[...].astype(F32)
    return gathered[...].astype(BF16)


def project_out(size, mask, w, x, *refs):
    blocks, out, gathered = refs[:size], refs[-2], refs[-1]
    part = columns(lax.axis_index("gy") ^ mask, out.shape[1])
    heads = gather_rows(blocks, gathered)
    total = jnp.dot(heads, w[:, part], preferred_element_type=F32)
    if not mask:
        total = total + x[:, part].astype(F32)
    out[...] = total.astype(out.dtype)


def finish(own, *refs):
    *arrived, out = refs
    total = own[...]
    for item in arrived:
        total = total + item[...].astype(F32)
    out[...] = total.astype(BF16)


def assemble(size, *refs):
    blocks, out, sems = refs[:size], refs[size], refs[size + 1]
    me = lax.axis_index("gy")
    width = blocks[0].shape[1]
    copies = []
    for mask in range(size):
        target = out.at[:, columns(me ^ mask, width)]
        copies.append(pltpu.make_async_copy(blocks[mask], target, sems.at[mask]))
    for copy in copies:
        copy.start()
    for copy in copies:
        copy.wait()


def swap(value, axis, size, mask):
    return lax.ppermute(value, axis, [(i, i ^ mask) for i in range(size)])


def solution(mesh):
    size_x = mesh.shape["gx"]
    size_y = mesh.shape["gy"]
    struct = jax.ShapeDtypeStruct
    sems = lambda n: pltpu.SemaphoreType.DMA((n,))
    order = list(range(size_y - 1, -1, -1))

    def shards(inputs, gain, w_query, w_key, w_value, w_output, key_cache, value_cache, lengths):
        batch, depth = inputs.shape
        width = w_query.shape[1]
        rows = key_cache.shape[0]
        packed = width + 3 * HD
        block = w_output.shape[1] // size_y

        total = pl.pallas_call(
            project,
            out_shape=pltpu.VMEM((batch, packed), F32),
            in_specs=[ANY] * 5,
            out_specs=VMEM,
            scratch_shapes=[
                pltpu.VMEM(inputs.shape, BF16),
                pltpu.VMEM((1, depth), F32),
                pltpu.VMEM(w_query.shape, BF16),
                pltpu.VMEM(w_key.shape, BF16),
                pltpu.VMEM(w_value.shape, BF16),
                pltpu.VMEM(inputs.shape, BF16),
                sems(depth // CHUNK + 4),
            ],
            compiler_params=params(28),
            cost_estimate=cost(2 * batch * depth * packed, 2 * depth * packed),
            name="project",
        )(*[in_hbm(a) for a in (inputs, gain.reshape(1, depth), w_query, w_key, w_value)])
        sums = pl.pallas_call(
            split,
            out_shape=[pltpu.VMEM((rows, packed), F32)] * size_x,
            in_specs=[VMEM, ANY],
            out_specs=[VMEM] * size_x,
            compiler_params=params(4),
            name="split",
        )(in_vmem(total), in_hbm(w_query))
        arrived = [sums[0]]
        for mask in range(1, size_x):
            arrived.append(swap(sums[mask].astype(F16), "gx", size_x, mask).astype(F32))

        values = in_vmem(value_cache)
        keys = pl.pallas_call(
            turn_keys,
            out_shape=pltpu.VMEM((rows, HD, key_cache.shape[1]), BF16),
            in_specs=[ANY, VMEM, ANY],
            out_specs=VMEM,
            compiler_params=params(4),
            cost_estimate=cost(0, 2 * key_cache.size),
            name="turn_keys",
        )(sums[0], in_vmem(key_cache), values)

        half = HD // 2
        inverse = ROPE_BASE ** (-(jnp.arange(half, dtype=F32) * 2.0 / HD))
        angles = lengths.astype(F32)[:, None] * inverse[None, :]
        cosine, sine = jnp.cos(angles), jnp.sin(angles)
        lanes = rows * (width // HD)
        heads = pl.pallas_call(
            functools.partial(attention, size_x, depth * size_x),
            out_shape=pltpu.VMEM((rows, width), BF16),
            in_specs=[ANY] + [VMEM] * (5 + size_x),
            out_specs=VMEM,
            scratch_shapes=[
                pltpu.VMEM((lanes, HD), F32),
                pltpu.VMEM((lanes, HD), F32),
                pltpu.VMEM((lanes, key_cache.shape[1]), F32),
            ],
            compiler_params=params(8),
            cost_estimate=cost(4 * key_cache.size * (width // HD), 4 * key_cache.size),
            name="attention",
        )(
            in_hbm(w_query),
            jnp.broadcast_to(lengths[:, None], (rows, HD)),
            jnp.concatenate([cosine, cosine], 1),
            jnp.concatenate([-sine, sine], 1),
            in_vmem(keys),
            values,
            *[in_vmem(a) for a in arrived],
        )
        gathered = [heads] + [swap(heads, "gx", size_x, m) for m in range(1, size_x)]

        terms = {}
        for mask in order:
            term = pl.pallas_call(
                functools.partial(project_out, size_x, mask),
                out_shape=pltpu.VMEM((batch, block), BF16 if mask else F32),
                in_specs=[VMEM] * (2 + size_x),
                out_specs=VMEM,
                scratch_shapes=[pltpu.VMEM((batch, width), F32)],
                compiler_params=params(8),
                cost_estimate=cost(2 * batch * width * block, 2 * width * block),
                name="project_out",
            )(in_vmem(w_output), in_vmem(inputs), *[in_vmem(a) for a in gathered])
            terms[mask] = swap(term, "gy", size_y, mask) if mask else term
        done = pl.pallas_call(
            finish,
            out_shape=pltpu.VMEM((batch, block), BF16),
            in_specs=[VMEM] * size_y,
            out_specs=VMEM,
            compiler_params=params(4),
            name="finish",
        )(*[in_vmem(terms[m]) for m in range(size_y)])
        blocks = [done] + [swap(done, "gy", size_y, m) for m in range(1, size_y)]
        return pl.pallas_call(
            functools.partial(assemble, size_y),
            out_shape=struct((batch, block * size_y), BF16),
            in_specs=[VMEM] * size_y,
            out_specs=ANY,
            scratch_shapes=[sems(size_y)],
            compiler_params=params(4),
            name="assemble",
        )(*[in_vmem(b) for b in blocks])

    placed = (
        P("groups", "gx"),
        P("gx"),
        P("gx", "gy"),
        P("gx", "gy"),
        P("gx", "gy"),
        P("gy", "gx"),
        P(("groups", "gx"), None, "gy"),
        P(("groups", "gx"), None, "gy"),
        P(("groups", "gx")),
    )
    return jax.shard_map(
        shards, mesh=mesh, in_specs=placed, out_specs=P("groups", "gx"), check_vma=False
    )
```

```python
import functools
import math

import jax
import jax.numpy as jnp
from jax import lax
from jax.experimental import pallas as pl
from jax.experimental.pallas import tpu as pltpu
from jax.sharding import PartitionSpec as P

HD = 128
EPS = 1e-05
ROPE_BASE = 500000.0
CHUNK = 256
F32 = jnp.float32
BF16 = jnp.bfloat16
F16 = jnp.float16
SQUARES = 2.0**-8

ANY = pl.BlockSpec(memory_space=pl.ANY)
VMEM = pl.BlockSpec(memory_space=pltpu.VMEM)
MIB = 1 << 20


def columns(index, width):
    return pl.ds(pl.multiple_of(index * width, HD), width)


def params(mib):
    return pltpu.CompilerParams(vmem_limit_bytes=mib * MIB)


def cost(flops, nbytes):
    return pl.CostEstimate(flops=flops, bytes_accessed=nbytes, transcendentals=0)


def in_vmem(value):
    return pltpu.with_memory_space_constraint(value, pltpu.VMEM)


def in_hbm(value):
    return pltpu.with_memory_space_constraint(value, pltpu.HBM)


def project(x_hbm, gain_hbm, wq_hbm, wk_hbm, wv_hbm, *refs):
    total, x, gain, wq, wk, wv, scaled, sems = refs
    depth = x.shape[1]
    steps = depth // CHUNK
    pairs = [(x_hbm, x), (gain_hbm, gain), (wk_hbm, wk), (wv_hbm, wv)]
    small = [pltpu.make_async_copy(a, b, sems.at[steps + i]) for i, (a, b) in enumerate(pairs)]
    large = []
    for step in range(steps):
        part = pl.ds(step * CHUNK, CHUNK)
        large.append(pltpu.make_async_copy(wq_hbm.at[part], wq.at[part], sems.at[step]))
    small[0].start()
    small[1].start()
    for copy in large[:2]:
        copy.start()
    small[2].start()
    small[3].start()
    for copy in large[2:]:
        copy.start()
    small[0].wait()
    small[1].wait()
    wide = x[...].astype(F32)
    scaled[...] = (wide * gain[...]).astype(BF16)
    squares = jnp.sum(wide * wide, 1, keepdims=True)
    width = wq.shape[1]
    dot = functools.partial(jnp.dot, preferred_element_type=F32)
    for step, copy in enumerate(large):
        copy.wait()
        part = slice(step * CHUNK, (step + 1) * CHUNK)
        term = dot(scaled[:, part], wq[part])
        if step == 0:
            total[:, :width] = term
        else:
            total[:, :width] += term
        if step == 1:
            small[2].wait()
            total[:, width : width + HD] = dot(scaled[...], wk[...])
            small[3].wait()
            total[:, width + HD : width + 2 * HD] = dot(scaled[...], wv[...])
            total[:, width + 2 * HD :] = jnp.broadcast_to(squares, (squares.shape[0], HD))


def split(total, weights, *outs):
    del weights
    width = total.shape[1] - 3 * HD
    rows = outs[0].shape[0]
    me = lax.axis_index("gx")
    first = lax.broadcasted_iota(jnp.int32, (rows, HD), 1) < HD // 2
    for mask, out in enumerate(outs):
        start = pl.multiple_of((me ^ mask) * rows, 8)
        part = total[pl.ds(start, rows), :]
        if mask:
            whole = part[:, width + 2 * HD :] * SQUARES
            high = whole.astype(BF16).astype(F32)
            out[:, : width + 2 * HD] = part[:, : width + 2 * HD]
            out[:, width + 2 * HD :] = jnp.where(first, high, whole - high)
        else:
            out[...] = part


def turn_keys(after, k, v, k_turned):
    del after, v
    rows, slots = k.shape[0], k.shape[1]
    for row in range(rows):
        for start in range(0, slots, CHUNK):
            part = slice(start, start + CHUNK)
            k_turned[row, :, part] = k[row, part, :].T


def attention(size, model, weights, lengths, cosine, sine, k, v, *refs):
    del weights
    arrived = refs[:size]
    heads, q_rows, o_rows, scores = refs[size:]
    rows, slots = k.shape[0], k.shape[2]
    group = heads.shape[1] // HD
    width = group * HD
    summed = arrived[0][:, : width + 2 * HD]
    squares = arrived[0][:, width + 2 * HD :]
    for item in arrived[1:]:
        summed = summed + item[:, : width + 2 * HD].astype(F32)
        parts = item[:, width + 2 * HD :].astype(F32)
        squares = squares + (parts + pltpu.roll(parts, HD // 2, 1)) * (1.0 / SQUARES)
    scale = lax.rsqrt(squares / model + EPS)
    cosines, sines = cosine[...], sine[...]

    def turn(value):
        return value * cosines + pltpu.roll(value, HD // 2, 1) * sines

    for head in range(group):
        part = summed[:, head * HD : (head + 1) * HD] * scale
        q_rows[head * rows : (head + 1) * rows] = turn(part).astype(BF16).astype(F32)
    new_keys = turn(summed[:, width : width + HD] * scale).astype(BF16).astype(F32)
    new_values = (summed[:, width + HD : width + 2 * HD] * scale).astype(BF16).astype(F32)
    rate = HD ** (-0.5) * math.log2(math.e)
    half = slots // 2
    slot = lax.broadcasted_iota(jnp.int32, (2 * group, half), 1) + half
    second = lax.broadcasted_iota(jnp.int32, (2 * group, 1), 0) >= group
    empty = jnp.zeros((group, HD), F32)
    own, top = [], []
    for row in range(0, rows, 2):
        first = q_rows[pl.ds(row, group, stride=rows), :]
        other = q_rows[pl.ds(row + 1, group, stride=rows), :]
        queries = jnp.concatenate(
            [jnp.concatenate([first, empty], 1), jnp.concatenate([empty, other], 1)], 0
        )
        keys = jnp.concatenate([k[row], k[row + 1]], 0)
        raw = jnp.dot(queries.astype(BF16), keys, preferred_element_type=F32)
        low = raw[:, :half]
        limit = jnp.where(second, lengths[row + 1 : row + 2, :1], lengths[row : row + 1, :1])
        high = jnp.where(slot < limit, raw[:, half:], -jnp.inf)
        mine = slice(row * group, (row + 2) * group)
        scores[mine, :half] = low
        scores[mine, half:] = high
        both = jnp.concatenate(
            [first * new_keys[row : row + 1], other * new_keys[row + 1 : row + 2]], 0
        )
        own.append(jnp.sum(both, 1, keepdims=True))
        top.append(jnp.maximum(jnp.max(jnp.maximum(low, high), 1, keepdims=True), own[-1]))

    def soften(pair):
        mine = slice(2 * pair * group, (2 * pair + 2) * group)
        probs = jnp.exp2((scores[mine] - top[pair]) * rate)
        own_prob = jnp.exp2((own[pair] - top[pair]) * rate)
        share = 1.0 / (jnp.sum(probs, 1, keepdims=True) + own_prob)
        return (probs * share).astype(BF16), (own_prob * share).astype(BF16).astype(F32)

    ready = soften(0)
    for pair in range(rows // 2):
        weights, own_weight = ready
        if pair + 1 < rows // 2:
            ready = soften(pair + 1)
        sides = jnp.concatenate([v[2 * pair], v[2 * pair + 1]], 1)
        mixed = jnp.dot(weights, sides, preferred_element_type=F32)
        for side in range(2):
            row = 2 * pair + side
            mine = slice(side * group, (side + 1) * group)
            value = mixed[mine, side * HD : (side + 1) * HD]
            extra = own_weight[mine] * new_values[row : row + 1]
            o_rows[pl.ds(row, group, stride=rows), :] = value + extra
    for head in range(group):
        heads[:, head * HD : (head + 1) * HD] = o_rows[head * rows : (head + 1) * rows].astype(BF16)


def gather_rows(blocks, gathered):
    me = lax.axis_index("gx")
    rows = blocks[0].shape[0]
    for mask, block in enumerate(blocks):
        start = pl.multiple_of((me ^ mask) * rows, 8)
        gathered[pl.ds(start, rows), :] = block[...].astype(F32)
    return gathered[...].astype(BF16)


def project_out(size_x, size_y, w, x, *refs):
    blocks, outs, gathered = refs[:size_x], refs[size_x : size_x + size_y], refs[-1]
    heads = gather_rows(blocks, gathered)
    for mask in reversed(range(size_y)):
        out = outs[mask]
        part = columns(lax.axis_index("gy") ^ mask, out.shape[1])
        total = jnp.dot(heads, w[:, part], preferred_element_type=F32)
        if not mask:
            total = total + x[:, part].astype(F32)
        out[...] = total.astype(out.dtype)


def finish(own, *refs):
    *arrived, out = refs
    total = own[...]
    for item in arrived:
        total = total + item[...].astype(F32)
    out[...] = total.astype(BF16)


def assemble(size, *refs):
    blocks, out, sems = refs[:size], refs[size], refs[size + 1]
    me = lax.axis_index("gy")
    width = blocks[0].shape[1]
    copies = []
    for mask in range(size):
        target = out.at[:, columns(me ^ mask, width)]
        copies.append(pltpu.make_async_copy(blocks[mask], target, sems.at[mask]))
    for copy in copies:
        copy.start()
    for copy in copies:
        copy.wait()


def swap(value, axis, size, mask):
    return lax.ppermute(value, axis, [(i, i ^ mask) for i in range(size)])


def solution(mesh):
    size_x = mesh.shape["gx"]
    size_y = mesh.shape["gy"]
    struct = jax.ShapeDtypeStruct
    sems = lambda n: pltpu.SemaphoreType.DMA((n,))
    order = [*range(size_y // 2, size_y), *range(1, size_y // 2)]

    def shards(inputs, gain, w_query, w_key, w_value, w_output, key_cache, value_cache, lengths):
        batch, depth = inputs.shape
        width = w_query.shape[1]
        rows = key_cache.shape[0]
        packed = width + 3 * HD
        block = w_output.shape[1] // size_y

        total = pl.pallas_call(
            project,
            out_shape=pltpu.VMEM((batch, packed), F32),
            in_specs=[ANY] * 5,
            out_specs=VMEM,
            scratch_shapes=[
                pltpu.VMEM(inputs.shape, BF16),
                pltpu.VMEM((1, depth), F32),
                pltpu.VMEM(w_query.shape, BF16),
                pltpu.VMEM(w_key.shape, BF16),
                pltpu.VMEM(w_value.shape, BF16),
                pltpu.VMEM(inputs.shape, BF16),
                sems(depth // CHUNK + 4),
            ],
            compiler_params=params(28),
            cost_estimate=cost(2 * batch * depth * packed, 2 * depth * packed),
            name="project",
        )(*[in_hbm(a) for a in (inputs, gain.reshape(1, depth), w_query, w_key, w_value)])
        sums = pl.pallas_call(
            split,
            out_shape=[pltpu.VMEM((rows, packed), F32)] * size_x,
            in_specs=[VMEM, ANY],
            out_specs=[VMEM] * size_x,
            compiler_params=params(4),
            name="split",
        )(in_vmem(total), in_hbm(w_query))
        arrived = [sums[0]]
        for mask in range(1, size_x):
            arrived.append(swap(sums[mask].astype(F16), "gx", size_x, mask).astype(F32))

        values = in_vmem(value_cache)
        keys = pl.pallas_call(
            turn_keys,
            out_shape=pltpu.VMEM((rows, HD, key_cache.shape[1]), BF16),
            in_specs=[ANY, VMEM, ANY],
            out_specs=VMEM,
            compiler_params=params(4),
            cost_estimate=cost(0, 2 * key_cache.size),
            name="turn_keys",
        )(sums[0], in_vmem(key_cache), values)

        half = HD // 2
        inverse = ROPE_BASE ** (-(jnp.arange(half, dtype=F32) * 2.0 / HD))
        angles = lengths.astype(F32)[:, None] * inverse[None, :]
        cosine, sine = jnp.cos(angles), jnp.sin(angles)
        lanes = rows * (width // HD)
        heads = pl.pallas_call(
            functools.partial(attention, size_x, depth * size_x),
            out_shape=pltpu.VMEM((rows, width), BF16),
            in_specs=[ANY] + [VMEM] * (5 + size_x),
            out_specs=VMEM,
            scratch_shapes=[
                pltpu.VMEM((lanes, HD), F32),
                pltpu.VMEM((lanes, HD), F32),
                pltpu.VMEM((lanes, key_cache.shape[1]), F32),
            ],
            compiler_params=params(8),
            cost_estimate=cost(4 * key_cache.size * (width // HD), 4 * key_cache.size),
            name="attention",
        )(
            in_hbm(w_query),
            jnp.broadcast_to(lengths[:, None], (rows, HD)),
            jnp.concatenate([cosine, cosine], 1),
            jnp.concatenate([-sine, sine], 1),
            in_vmem(keys),
            values,
            *[in_vmem(a) for a in arrived],
        )
        gathered = [heads] + [swap(heads, "gx", size_x, m) for m in range(1, size_x)]

        terms = pl.pallas_call(
            functools.partial(project_out, size_x, size_y),
            out_shape=[pltpu.VMEM((batch, block), BF16 if m else F32) for m in range(size_y)],
            in_specs=[VMEM] * (2 + size_x),
            out_specs=[VMEM] * size_y,
            scratch_shapes=[pltpu.VMEM((batch, width), F32)],
            compiler_params=params(8),
            cost_estimate=cost(2 * batch * w_output.size, 2 * w_output.size),
            name="project_out",
        )(in_vmem(w_output), in_vmem(inputs), *[in_vmem(a) for a in gathered])
        landed = [swap(terms[m], "gy", size_y, m) for m in order]
        done = pl.pallas_call(
            finish,
            out_shape=pltpu.VMEM((batch, block), BF16),
            in_specs=[VMEM] * size_y,
            out_specs=VMEM,
            compiler_params=params(4),
            name="finish",
        )(*[in_vmem(a) for a in (terms[0], *landed)])
        blocks = {0: done} | {m: swap(done, "gy", size_y, m) for m in order}
        blocks = [blocks[m] for m in range(size_y)]
        return pl.pallas_call(
            functools.partial(assemble, size_y),
            out_shape=struct((batch, block * size_y), BF16),
            in_specs=[VMEM] * size_y,
            out_specs=ANY,
            scratch_shapes=[sems(size_y)],
            compiler_params=params(4),
            name="assemble",
        )(*[in_vmem(b) for b in blocks])

    placed = (
        P("groups", "gx"),
        P("gx"),
        P("gx", "gy"),
        P("gx", "gy"),
        P("gx", "gy"),
        P("gy", "gx"),
        P(("groups", "gx"), None, "gy"),
        P(("groups", "gx"), None, "gy"),
        P(("groups", "gx")),
    )
    return jax.shard_map(
        shards, mesh=mesh, in_specs=placed, out_specs=P("groups", "gx"), check_vma=False
    )
```

```python
import functools
import math

import jax
import jax.numpy as jnp
from jax import lax
from jax.experimental import pallas as pl
from jax.experimental.pallas import tpu as pltpu
from jax.sharding import PartitionSpec as P

HD = 128
EPS = 1e-05
ROPE_BASE = 500000.0
CHUNK = 256
F32 = jnp.float32
BF16 = jnp.bfloat16
F16 = jnp.float16
SQUARES = 2.0**-8

ANY = pl.BlockSpec(memory_space=pl.ANY)
VMEM = pl.BlockSpec(memory_space=pltpu.VMEM)
MIB = 1 << 20


def columns(index, width):
    return pl.ds(pl.multiple_of(index * width, HD), width)


def params(mib):
    return pltpu.CompilerParams(vmem_limit_bytes=mib * MIB)


def cost(flops, nbytes):
    return pl.CostEstimate(flops=flops, bytes_accessed=nbytes, transcendentals=0)


def in_vmem(value):
    return pltpu.with_memory_space_constraint(value, pltpu.VMEM)


def in_hbm(value):
    return pltpu.with_memory_space_constraint(value, pltpu.HBM)


def project(x_hbm, gain_hbm, wq_hbm, wk_hbm, wv_hbm, *refs):
    total, x, gain, wq, wk, wv, scaled, sems = refs
    depth = x.shape[1]
    cuts = [*range(0, depth, 2 * CHUNK), depth - CHUNK, depth]
    spans = [slice(a, b) for a, b in zip(cuts, cuts[1:])]
    steps = len(spans)
    pairs = [(x_hbm, x), (gain_hbm, gain), (wk_hbm, wk), (wv_hbm, wv)]
    small = [pltpu.make_async_copy(a, b, sems.at[steps + i]) for i, (a, b) in enumerate(pairs)]
    large = []
    for step, span in enumerate(spans):
        part = pl.ds(span.start, span.stop - span.start)
        large.append(pltpu.make_async_copy(wq_hbm.at[part], wq.at[part], sems.at[step]))
    small[0].start()
    small[1].start()
    for copy in large[:2]:
        copy.start()
    small[2].start()
    small[3].start()
    for copy in large[2:]:
        copy.start()
    small[0].wait()
    small[1].wait()
    wide = x[...].astype(F32)
    scaled[...] = (wide * gain[...]).astype(BF16)
    squares = jnp.sum(wide * wide, 1, keepdims=True)
    width = wq.shape[1]
    dot = functools.partial(jnp.dot, preferred_element_type=F32)
    for step, copy in enumerate(large):
        copy.wait()
        part = spans[step]
        term = dot(scaled[:, part], wq[part])
        if step == 0:
            total[:, :width] = term
        else:
            total[:, :width] += term
        if step == 1:
            small[2].wait()
            total[:, width : width + HD] = dot(scaled[...], wk[...])
            small[3].wait()
            total[:, width + HD : width + 2 * HD] = dot(scaled[...], wv[...])
            total[:, width + 2 * HD :] = jnp.broadcast_to(squares, (squares.shape[0], HD))


def split(total, weights, *outs):
    del weights
    width = total.shape[1] - 3 * HD
    rows = outs[0].shape[0]
    me = lax.axis_index("gx")
    first = lax.broadcasted_iota(jnp.int32, (rows, HD), 1) < HD // 2
    for mask, out in enumerate(outs):
        start = pl.multiple_of((me ^ mask) * rows, 8)
        part = total[pl.ds(start, rows), :]
        if mask:
            whole = part[:, width + 2 * HD :] * SQUARES
            high = whole.astype(BF16).astype(F32)
            out[:, : width + 2 * HD] = part[:, : width + 2 * HD]
            out[:, width + 2 * HD :] = jnp.where(first, high, whole - high)
        else:
            out[...] = part


def turn_keys(after, k, v, k_turned):
    del after, v
    rows, slots = k.shape[0], k.shape[1]
    for row in range(rows):
        for start in range(0, slots, CHUNK):
            part = slice(start, start + CHUNK)
            k_turned[row, :, part] = k[row, part, :].T


def attention(size, model, weights, lengths, cosine, sine, k, v, *refs):
    del weights
    arrived = refs[:size]
    heads, q_rows, o_rows, scores = refs[size:]
    rows, slots = k.shape[0], k.shape[2]
    group = heads.shape[1] // HD
    width = group * HD
    summed = arrived[0][:, : width + 2 * HD]
    squares = arrived[0][:, width + 2 * HD :]
    for item in arrived[1:]:
        summed = summed + item[:, : width + 2 * HD].astype(F32)
        parts = item[:, width + 2 * HD :].astype(F32)
        squares = squares + (parts + pltpu.roll(parts, HD // 2, 1)) * (1.0 / SQUARES)
    scale = lax.rsqrt(squares / model + EPS)
    cosines, sines = cosine[...], sine[...]

    def turn(value):
        return value * cosines + pltpu.roll(value, HD // 2, 1) * sines

    for head in range(group):
        part = summed[:, head * HD : (head + 1) * HD] * scale
        q_rows[head * rows : (head + 1) * rows] = turn(part).astype(BF16).astype(F32)
    new_keys = turn(summed[:, width : width + HD] * scale).astype(BF16).astype(F32)
    new_values = (summed[:, width + HD : width + 2 * HD] * scale).astype(BF16).astype(F32)
    rate = HD ** (-0.5) * math.log2(math.e)
    half = slots // 2
    slot = lax.broadcasted_iota(jnp.int32, (2 * group, half), 1) + half
    second = lax.broadcasted_iota(jnp.int32, (2 * group, 1), 0) >= group
    empty = jnp.zeros((group, HD), F32)
    own, top = [], []
    for row in range(0, rows, 2):
        first = q_rows[pl.ds(row, group, stride=rows), :]
        other = q_rows[pl.ds(row + 1, group, stride=rows), :]
        queries = jnp.concatenate(
            [jnp.concatenate([first, empty], 1), jnp.concatenate([empty, other], 1)], 0
        )
        keys = jnp.concatenate([k[row], k[row + 1]], 0)
        raw = jnp.dot(queries.astype(BF16), keys, preferred_element_type=F32)
        low = raw[:, :half]
        limit = jnp.where(second, lengths[row + 1 : row + 2, :1], lengths[row : row + 1, :1])
        high = jnp.where(slot < limit, raw[:, half:], -jnp.inf)
        mine = slice(row * group, (row + 2) * group)
        scores[mine, :half] = low
        scores[mine, half:] = high
        both = jnp.concatenate(
            [first * new_keys[row : row + 1], other * new_keys[row + 1 : row + 2]], 0
        )
        own.append(jnp.sum(both, 1, keepdims=True))
        top.append(jnp.maximum(jnp.max(jnp.maximum(low, high), 1, keepdims=True), own[-1]))

    def soften(pair):
        mine = slice(2 * pair * group, (2 * pair + 2) * group)
        probs = jnp.exp2((scores[mine] - top[pair]) * rate)
        own_prob = jnp.exp2((own[pair] - top[pair]) * rate)
        share = 1.0 / (jnp.sum(probs, 1, keepdims=True) + own_prob)
        return (probs * share).astype(BF16), (own_prob * share).astype(BF16).astype(F32)

    ready = soften(0)
    for pair in range(rows // 2):
        weights, own_weight = ready
        if pair + 1 < rows // 2:
            ready = soften(pair + 1)
        sides = jnp.concatenate([v[2 * pair], v[2 * pair + 1]], 1)
        mixed = jnp.dot(weights, sides, preferred_element_type=F32)
        for side in range(2):
            row = 2 * pair + side
            mine = slice(side * group, (side + 1) * group)
            value = mixed[mine, side * HD : (side + 1) * HD]
            extra = own_weight[mine] * new_values[row : row + 1]
            o_rows[pl.ds(row, group, stride=rows), :] = value + extra
    for head in range(group):
        heads[:, head * HD : (head + 1) * HD] = o_rows[head * rows : (head + 1) * rows].astype(BF16)


def gather_rows(blocks, gathered):
    me = lax.axis_index("gx")
    rows = blocks[0].shape[0]
    for mask, block in enumerate(blocks):
        start = pl.multiple_of((me ^ mask) * rows, 8)
        gathered[pl.ds(start, rows), :] = block[...].astype(F32)
    return gathered[...].astype(BF16)


def project_out(size, mask, w, x, *refs):
    blocks, out, gathered = refs[:size], refs[-2], refs[-1]
    part = columns(lax.axis_index("gy") ^ mask, out.shape[1])
    heads = gather_rows(blocks, gathered)
    total = jnp.dot(heads, w[:, part], preferred_element_type=F32)
    if not mask:
        total = total + x[:, part].astype(F32)
    out[...] = total.astype(out.dtype)


def finish(own, *refs):
    *arrived, out = refs
    total = own[...]
    for item in arrived:
        total = total + item[...].astype(F32)
    out[...] = total.astype(BF16)


def assemble(size, *refs):
    blocks, out, sems = refs[:size], refs[size], refs[size + 1]
    me = lax.axis_index("gy")
    width = blocks[0].shape[1]
    copies = []
    for mask in range(size):
        target = out.at[:, columns(me ^ mask, width)]
        copies.append(pltpu.make_async_copy(blocks[mask], target, sems.at[mask]))
    for copy in copies:
        copy.start()
    for copy in copies:
        copy.wait()


def swap(value, axis, size, mask):
    return lax.ppermute(value, axis, [(i, i ^ mask) for i in range(size)])


def solution(mesh):
    size_x = mesh.shape["gx"]
    size_y = mesh.shape["gy"]
    struct = jax.ShapeDtypeStruct
    sems = lambda n: pltpu.SemaphoreType.DMA((n,))
    order = [0, *range(size_y // 2, size_y), *range(1, size_y // 2)]

    def shards(inputs, gain, w_query, w_key, w_value, w_output, key_cache, value_cache, lengths):
        batch, depth = inputs.shape
        width = w_query.shape[1]
        rows = key_cache.shape[0]
        packed = width + 3 * HD
        block = w_output.shape[1] // size_y

        total = pl.pallas_call(
            project,
            out_shape=pltpu.VMEM((batch, packed), F32),
            in_specs=[ANY] * 5,
            out_specs=VMEM,
            scratch_shapes=[
                pltpu.VMEM(inputs.shape, BF16),
                pltpu.VMEM((1, depth), F32),
                pltpu.VMEM(w_query.shape, BF16),
                pltpu.VMEM(w_key.shape, BF16),
                pltpu.VMEM(w_value.shape, BF16),
                pltpu.VMEM(inputs.shape, BF16),
                sems(depth // (2 * CHUNK) + 5),
            ],
            compiler_params=params(28),
            cost_estimate=cost(2 * batch * depth * packed, 2 * depth * packed),
            name="project",
        )(*[in_hbm(a) for a in (inputs, gain.reshape(1, depth), w_query, w_key, w_value)])
        sums = pl.pallas_call(
            split,
            out_shape=[pltpu.VMEM((rows, packed), F32)] * size_x,
            in_specs=[VMEM, ANY],
            out_specs=[VMEM] * size_x,
            compiler_params=params(4),
            name="split",
        )(in_vmem(total), in_hbm(w_query))
        arrived = [sums[0]]
        for mask in range(1, size_x):
            arrived.append(swap(sums[mask].astype(F16), "gx", size_x, mask).astype(F32))

        values = in_vmem(value_cache)
        keys = pl.pallas_call(
            turn_keys,
            out_shape=pltpu.VMEM((rows, HD, key_cache.shape[1]), BF16),
            in_specs=[ANY, VMEM, ANY],
            out_specs=VMEM,
            compiler_params=params(4),
            cost_estimate=cost(0, 2 * key_cache.size),
            name="turn_keys",
        )(sums[0], in_vmem(key_cache), values)

        half = HD // 2
        inverse = ROPE_BASE ** (-(jnp.arange(half, dtype=F32) * 2.0 / HD))
        angles = lengths.astype(F32)[:, None] * inverse[None, :]
        cosine, sine = jnp.cos(angles), jnp.sin(angles)
        lanes = rows * (width // HD)
        heads = pl.pallas_call(
            functools.partial(attention, size_x, depth * size_x),
            out_shape=pltpu.VMEM((rows, width), BF16),
            in_specs=[ANY] + [VMEM] * (5 + size_x),
            out_specs=VMEM,
            scratch_shapes=[
                pltpu.VMEM((lanes, HD), F32),
                pltpu.VMEM((lanes, HD), F32),
                pltpu.VMEM((lanes, key_cache.shape[1]), F32),
            ],
            compiler_params=params(8),
            cost_estimate=cost(4 * key_cache.size * (width // HD), 4 * key_cache.size),
            name="attention",
        )(
            in_hbm(w_query),
            jnp.broadcast_to(lengths[:, None], (rows, HD)),
            jnp.concatenate([cosine, cosine], 1),
            jnp.concatenate([-sine, sine], 1),
            in_vmem(keys),
            values,
            *[in_vmem(a) for a in arrived],
        )
        gathered = [heads] + [swap(heads, "gx", size_x, m) for m in range(1, size_x)]

        terms = {}
        for mask in order:
            term = pl.pallas_call(
                functools.partial(project_out, size_x, mask),
                out_shape=pltpu.VMEM((batch, block), BF16 if mask else F32),
                in_specs=[VMEM] * (2 + size_x),
                out_specs=VMEM,
                scratch_shapes=[pltpu.VMEM((batch, width), F32)],
                compiler_params=params(8),
                cost_estimate=cost(2 * batch * width * block, 2 * width * block),
                name="project_out",
            )(in_vmem(w_output), in_vmem(inputs), *[in_vmem(a) for a in gathered])
            terms[mask] = swap(term, "gy", size_y, mask) if mask else term
        done = pl.pallas_call(
            finish,
            out_shape=pltpu.VMEM((batch, block), BF16),
            in_specs=[VMEM] * size_y,
            out_specs=VMEM,
            compiler_params=params(4),
            name="finish",
        )(*[in_vmem(terms[m]) for m in order])
        blocks = [done] + [swap(done, "gy", size_y, m) for m in range(1, size_y)]
        return pl.pallas_call(
            functools.partial(assemble, size_y),
            out_shape=struct((batch, block * size_y), BF16),
            in_specs=[VMEM] * size_y,
            out_specs=ANY,
            scratch_shapes=[sems(size_y)],
            compiler_params=params(4),
            name="assemble",
        )(*[in_vmem(b) for b in blocks])

    placed = (
        P("groups", "gx"),
        P("gx"),
        P("gx", "gy"),
        P("gx", "gy"),
        P("gx", "gy"),
        P("gy", "gx"),
        P(("groups", "gx"), None, "gy"),
        P(("groups", "gx"), None, "gy"),
        P(("groups", "gx")),
    )
    return jax.shard_map(
        shards, mesh=mesh, in_specs=placed, out_specs=P("groups", "gx"), check_vma=False
    )
```

```python
import functools
import math

import jax
import jax.numpy as jnp
from jax import lax
from jax.experimental import pallas as pl
from jax.experimental.pallas import tpu as pltpu
from jax.sharding import PartitionSpec as P

HD = 128
EPS = 1e-05
ROPE_BASE = 500000.0
CHUNK = 256
F32 = jnp.float32
BF16 = jnp.bfloat16
F16 = jnp.float16
SQUARES = 2.0**-8

ANY = pl.BlockSpec(memory_space=pl.ANY)
VMEM = pl.BlockSpec(memory_space=pltpu.VMEM)
MIB = 1 << 20


def columns(index, width):
    return pl.ds(pl.multiple_of(index * width, HD), width)


def params(mib):
    return pltpu.CompilerParams(vmem_limit_bytes=mib * MIB)


def cost(flops, nbytes):
    return pl.CostEstimate(flops=flops, bytes_accessed=nbytes, transcendentals=0)


def in_vmem(value):
    return pltpu.with_memory_space_constraint(value, pltpu.VMEM)


def in_hbm(value):
    return pltpu.with_memory_space_constraint(value, pltpu.HBM)


def project(x_hbm, gain_hbm, wq_hbm, wk_hbm, wv_hbm, *refs):
    total, x, gain, wq, wk, wv, scaled, sems = refs
    depth = x.shape[1]
    cuts = [*range(0, depth, 2 * CHUNK), depth - CHUNK, depth]
    spans = [slice(a, b) for a, b in zip(cuts, cuts[1:])]
    steps = len(spans)
    pairs = [(x_hbm, x), (gain_hbm, gain), (wk_hbm, wk), (wv_hbm, wv)]
    small = [pltpu.make_async_copy(a, b, sems.at[steps + i]) for i, (a, b) in enumerate(pairs)]
    large = []
    for step, span in enumerate(spans):
        part = pl.ds(span.start, span.stop - span.start)
        large.append(pltpu.make_async_copy(wq_hbm.at[part], wq.at[part], sems.at[step]))
    small[0].start()
    small[1].start()
    for copy in large[:2]:
        copy.start()
    small[2].start()
    small[3].start()
    for copy in large[2:]:
        copy.start()
    small[0].wait()
    small[1].wait()
    wide = x[...].astype(F32)
    scaled[...] = (wide * gain[...]).astype(BF16)
    squares = jnp.sum(wide * wide, 1, keepdims=True)
    width = wq.shape[1]
    dot = functools.partial(jnp.dot, preferred_element_type=F32)
    for step, copy in enumerate(large):
        copy.wait()
        part = spans[step]
        term = dot(scaled[:, part], wq[part])
        if step == 0:
            total[:, :width] = term
        else:
            total[:, :width] += term
        if step == 1:
            small[2].wait()
            total[:, width : width + HD] = dot(scaled[...], wk[...])
            small[3].wait()
            total[:, width + HD : width + 2 * HD] = dot(scaled[...], wv[...])
            total[:, width + 2 * HD :] = jnp.broadcast_to(squares, (squares.shape[0], HD))


def split(total, weights, *outs):
    del weights
    width = total.shape[1] - 3 * HD
    rows = outs[0].shape[0]
    me = lax.axis_index("gx")
    first = lax.broadcasted_iota(jnp.int32, (rows, HD), 1) < HD // 2
    for mask, out in enumerate(outs):
        start = pl.multiple_of((me ^ mask) * rows, 8)
        part = total[pl.ds(start, rows), :]
        if mask:
            whole = part[:, width + 2 * HD :] * SQUARES
            high = whole.astype(BF16).astype(F32)
            out[:, : width + 2 * HD] = part[:, : width + 2 * HD]
            out[:, width + 2 * HD :] = jnp.where(first, high, whole - high)
        else:
            out[...] = part


def turn_keys(after, k, v, k_turned):
    del after, v
    rows, slots = k.shape[0], k.shape[1]
    for row in range(rows):
        for start in range(0, slots, CHUNK):
            part = slice(start, start + CHUNK)
            k_turned[row, :, part] = k[row, part, :].T


def attention(size, model, weights, lengths, cosine, sine, k, v, *refs):
    del weights
    arrived = refs[:size]
    heads, q_rows, o_rows, scores = refs[size:]
    rows, slots = k.shape[0], k.shape[2]
    group = heads.shape[1] // HD
    width = group * HD
    summed = arrived[0][:, : width + 2 * HD]
    squares = arrived[0][:, width + 2 * HD :]
    for item in arrived[1:]:
        summed = summed + item[:, : width + 2 * HD].astype(F32)
        parts = item[:, width + 2 * HD :].astype(F32)
        squares = squares + (parts + pltpu.roll(parts, HD // 2, 1)) * (1.0 / SQUARES)
    scale = lax.rsqrt(squares / model + EPS)
    cosines, sines = cosine[...], sine[...]

    def turn(value):
        return value * cosines + pltpu.roll(value, HD // 2, 1) * sines

    for head in range(group):
        part = summed[:, head * HD : (head + 1) * HD] * scale
        q_rows[head * rows : (head + 1) * rows] = turn(part).astype(BF16).astype(F32)
    new_keys = turn(summed[:, width : width + HD] * scale).astype(BF16).astype(F32)
    new_values = (summed[:, width + HD : width + 2 * HD] * scale).astype(BF16).astype(F32)
    rate = HD ** (-0.5) * math.log2(math.e)
    half = slots // 2
    slot = lax.broadcasted_iota(jnp.int32, (2 * group, half), 1) + half
    second = lax.broadcasted_iota(jnp.int32, (2 * group, 1), 0) >= group
    empty = jnp.zeros((group, HD), F32)
    own, top = [], []
    for row in range(0, rows, 2):
        first = q_rows[pl.ds(row, group, stride=rows), :]
        other = q_rows[pl.ds(row + 1, group, stride=rows), :]
        queries = jnp.concatenate(
            [jnp.concatenate([first, empty], 1), jnp.concatenate([empty, other], 1)], 0
        )
        keys = jnp.concatenate([k[row], k[row + 1]], 0)
        raw = jnp.dot(queries.astype(BF16), keys, preferred_element_type=F32)
        low = raw[:, :half]
        limit = jnp.where(second, lengths[row + 1 : row + 2, :1], lengths[row : row + 1, :1])
        high = jnp.where(slot < limit, raw[:, half:], -jnp.inf)
        mine = slice(row * group, (row + 2) * group)
        scores[mine, :half] = low
        scores[mine, half:] = high
        both = jnp.concatenate(
            [first * new_keys[row : row + 1], other * new_keys[row + 1 : row + 2]], 0
        )
        own.append(jnp.sum(both, 1, keepdims=True))
        top.append(jnp.maximum(jnp.max(jnp.maximum(low, high), 1, keepdims=True), own[-1]))

    def soften(pair):
        mine = slice(2 * pair * group, (2 * pair + 2) * group)
        probs = jnp.exp2((scores[mine] - top[pair]) * rate)
        own_prob = jnp.exp2((own[pair] - top[pair]) * rate)
        share = 1.0 / (jnp.sum(probs, 1, keepdims=True) + own_prob)
        return (probs * share).astype(BF16), (own_prob * share).astype(BF16).astype(F32)

    ready = soften(0)
    for pair in range(rows // 2):
        weights, own_weight = ready
        if pair + 1 < rows // 2:
            ready = soften(pair + 1)
        sides = jnp.concatenate([v[2 * pair], v[2 * pair + 1]], 1)
        mixed = jnp.dot(weights, sides, preferred_element_type=F32)
        for side in range(2):
            row = 2 * pair + side
            mine = slice(side * group, (side + 1) * group)
            value = mixed[mine, side * HD : (side + 1) * HD]
            extra = own_weight[mine] * new_values[row : row + 1]
            o_rows[pl.ds(row, group, stride=rows), :] = value + extra
    for head in range(group):
        heads[:, head * HD : (head + 1) * HD] = o_rows[head * rows : (head + 1) * rows].astype(BF16)


def gather_rows(blocks, gathered):
    me = lax.axis_index("gx")
    rows = blocks[0].shape[0]
    for mask, block in enumerate(blocks):
        start = pl.multiple_of((me ^ mask) * rows, 8)
        gathered[pl.ds(start, rows), :] = block[...].astype(F32)
    return gathered[...].astype(BF16)


def place(chunk, given):
    return 2 * chunk + ((lax.axis_index("gy") ^ given) & 1)


def project_out(size, chunk, given, w, *refs):
    blocks, out, gathered = refs[:size], refs[-2], refs[-1]
    heads = gather_rows(blocks, gathered)
    part = columns(place(chunk, given), out.shape[1])
    out[...] = jnp.dot(heads, w[:, part], preferred_element_type=F32).astype(out.dtype)


def add_near(own, arrived, out):
    out[...] = (own[...] + arrived[...].astype(F32)).astype(BF16)


def finish(size, chunk, x, *refs):
    terms, out, ranked = refs[:size], refs[-2], refs[-1]
    rank = lax.axis_index("gy") // 2
    for mask, term in enumerate(terms):
        ranked[rank ^ mask] = term[...].astype(F32)
    total = ranked[0]
    for index in range(1, size):
        total = total + ranked[index]
    part = columns(place(chunk, 0), out.shape[1])
    out[...] = (x[:, part].astype(F32) + total).astype(BF16)


def assemble(*refs):
    *blocks, out, sems = refs
    width = blocks[0].shape[1]
    copies = []
    for index, block in enumerate(blocks):
        target = out.at[:, columns(place(index // 2, index % 2), width)]
        copies.append(pltpu.make_async_copy(block, target, sems.at[index]))
    for copy in copies:
        copy.start()
    for copy in copies:
        copy.wait()


def swap(value, axis, size, mask):
    return lax.ppermute(value, axis, [(i, i ^ mask) for i in range(size)])


def solution(mesh):
    size_x = mesh.shape["gx"]
    size_y = mesh.shape["gy"]
    sems = lambda n: pltpu.SemaphoreType.DMA((n,))

    def shards(inputs, gain, w_query, w_key, w_value, w_output, key_cache, value_cache, lengths):
        batch, depth = inputs.shape
        width = w_query.shape[1]
        rows = key_cache.shape[0]
        packed = width + 3 * HD
        block = w_output.shape[1] // 4

        total = pl.pallas_call(
            project,
            out_shape=pltpu.VMEM((batch, packed), F32),
            in_specs=[ANY] * 5,
            out_specs=VMEM,
            scratch_shapes=[
                pltpu.VMEM(inputs.shape, BF16),
                pltpu.VMEM((1, depth), F32),
                pltpu.VMEM(w_query.shape, BF16),
                pltpu.VMEM(w_key.shape, BF16),
                pltpu.VMEM(w_value.shape, BF16),
                pltpu.VMEM(inputs.shape, BF16),
                sems(depth // (2 * CHUNK) + 5),
            ],
            compiler_params=params(28),
            cost_estimate=cost(2 * batch * depth * packed, 2 * depth * packed),
            name="project",
        )(*[in_hbm(a) for a in (inputs, gain.reshape(1, depth), w_query, w_key, w_value)])
        sums = pl.pallas_call(
            split,
            out_shape=[pltpu.VMEM((rows, packed), F32)] * size_x,
            in_specs=[VMEM, ANY],
            out_specs=[VMEM] * size_x,
            compiler_params=params(4),
            name="split",
        )(in_vmem(total), in_hbm(w_query))
        arrived = [sums[0]]
        for mask in range(1, size_x):
            arrived.append(swap(sums[mask].astype(F16), "gx", size_x, mask).astype(F32))

        values = in_vmem(value_cache)
        keys = pl.pallas_call(
            turn_keys,
            out_shape=pltpu.VMEM((rows, HD, key_cache.shape[1]), BF16),
            in_specs=[ANY, VMEM, ANY],
            out_specs=VMEM,
            compiler_params=params(4),
            cost_estimate=cost(0, 2 * key_cache.size),
            name="turn_keys",
        )(sums[0], in_vmem(key_cache), values)

        half = HD // 2
        inverse = ROPE_BASE ** (-(jnp.arange(half, dtype=F32) * 2.0 / HD))
        angles = lengths.astype(F32)[:, None] * inverse[None, :]
        cosine, sine = jnp.cos(angles), jnp.sin(angles)
        lanes = rows * (width // HD)
        heads = pl.pallas_call(
            functools.partial(attention, size_x, depth * size_x),
            out_shape=pltpu.VMEM((rows, width), BF16),
            in_specs=[ANY] + [VMEM] * (5 + size_x),
            out_specs=VMEM,
            scratch_shapes=[
                pltpu.VMEM((lanes, HD), F32),
                pltpu.VMEM((lanes, HD), F32),
                pltpu.VMEM((lanes, key_cache.shape[1]), F32),
            ],
            compiler_params=params(8),
            cost_estimate=cost(4 * key_cache.size * (width // HD), 4 * key_cache.size),
            name="attention",
        )(
            in_hbm(w_query),
            jnp.broadcast_to(lengths[:, None], (rows, HD)),
            jnp.concatenate([cosine, cosine], 1),
            jnp.concatenate([-sine, sine], 1),
            in_vmem(keys),
            values,
            *[in_vmem(a) for a in arrived],
        )
        gathered = [heads] + [swap(heads, "gx", size_x, m) for m in range(1, size_x)]

        gathered = [in_vmem(a) for a in gathered]
        half = size_y // 2

        def product(chunk, given):
            return pl.pallas_call(
                functools.partial(project_out, size_x, chunk, given),
                out_shape=pltpu.VMEM((batch, block), BF16 if given else F32),
                in_specs=[VMEM] * (1 + size_x),
                out_specs=VMEM,
                scratch_shapes=[pltpu.VMEM((batch, width), F32)],
                compiler_params=params(8),
                cost_estimate=cost(2 * batch * width * block, 2 * width * block),
                name="project_out",
            )(in_vmem(w_output), *gathered)

        near = [swap(product(chunk, 1), "gy", size_y, 1) for chunk in range(2)]
        blocks = []
        for chunk in range(2):
            pair = pl.pallas_call(
                add_near,
                out_shape=pltpu.VMEM((batch, block), BF16),
                in_specs=[VMEM] * 2,
                out_specs=VMEM,
                compiler_params=params(4),
                name="add_near",
            )(in_vmem(product(chunk, 0)), in_vmem(near[chunk]))
            far = [pair] + [swap(pair, "gy", size_y, 2 * m) for m in range(1, half)]
            done = pl.pallas_call(
                functools.partial(finish, half, chunk),
                out_shape=pltpu.VMEM((batch, block), BF16),
                in_specs=[VMEM] * (1 + half),
                out_specs=VMEM,
                scratch_shapes=[pltpu.VMEM((half, batch, block), F32)],
                compiler_params=params(8),
                name="finish",
            )(in_vmem(inputs), *[in_vmem(a) for a in far])
            blocks += [done, swap(done, "gy", size_y, 1)]
        return pl.pallas_call(
            assemble,
            out_shape=jax.ShapeDtypeStruct((batch, block * 4), BF16),
            in_specs=[VMEM] * 4,
            out_specs=ANY,
            scratch_shapes=[sems(4)],
            compiler_params=params(4),
            name="assemble",
        )(*[in_vmem(b) for b in blocks])

    placed = (
        P("groups", "gx"),
        P("gx"),
        P("gx", "gy"),
        P("gx", "gy"),
        P("gx", "gy"),
        P("gy", "gx"),
        P(("groups", "gx"), None, "gy"),
        P(("groups", "gx"), None, "gy"),
        P(("groups", "gx")),
    )
    return jax.shard_map(
        shards, mesh=mesh, in_specs=placed, out_specs=P("groups", "gx"), check_vma=False
    )
```

```python
import functools
import math

import jax
import jax.numpy as jnp
from jax import lax
from jax.experimental import pallas as pl
from jax.experimental.pallas import tpu as pltpu
from jax.sharding import PartitionSpec as P

HD = 128
EPS = 1e-05
ROPE_BASE = 500000.0
CHUNK = 256
F32 = jnp.float32
BF16 = jnp.bfloat16
F16 = jnp.float16
SQUARES = 2.0**-8

ANY = pl.BlockSpec(memory_space=pl.ANY)
VMEM = pl.BlockSpec(memory_space=pltpu.VMEM)
MIB = 1 << 20


def columns(index, width):
    return pl.ds(pl.multiple_of(index * width, HD), width)


def params(mib):
    return pltpu.CompilerParams(vmem_limit_bytes=mib * MIB)


def cost(flops, nbytes):
    return pl.CostEstimate(flops=flops, bytes_accessed=nbytes, transcendentals=0)


def in_vmem(value):
    return pltpu.with_memory_space_constraint(value, pltpu.VMEM)


def in_hbm(value):
    return pltpu.with_memory_space_constraint(value, pltpu.HBM)


def project(x_hbm, gain_hbm, wq_hbm, wk_hbm, wv_hbm, *refs):
    total, x, gain, wq, wk, wv, scaled, sems = refs
    depth = x.shape[1]
    cuts = [*range(0, depth, 2 * CHUNK), depth - CHUNK, depth]
    spans = [slice(a, b) for a, b in zip(cuts, cuts[1:])]
    steps = len(spans)
    pairs = [(x_hbm, x), (gain_hbm, gain), (wk_hbm, wk), (wv_hbm, wv)]
    small = [pltpu.make_async_copy(a, b, sems.at[steps + i]) for i, (a, b) in enumerate(pairs)]
    large = []
    for step, span in enumerate(spans):
        part = pl.ds(span.start, span.stop - span.start)
        large.append(pltpu.make_async_copy(wq_hbm.at[part], wq.at[part], sems.at[step]))
    small[0].start()
    small[1].start()
    for copy in large[:2]:
        copy.start()
    small[2].start()
    small[3].start()
    for copy in large[2:]:
        copy.start()
    small[0].wait()
    small[1].wait()
    wide = x[...].astype(F32)
    scaled[...] = (wide * gain[...]).astype(BF16)
    squares = jnp.sum(wide * wide, 1, keepdims=True)
    width = wq.shape[1]
    dot = functools.partial(jnp.dot, preferred_element_type=F32)
    for step, copy in enumerate(large):
        copy.wait()
        part = spans[step]
        term = dot(scaled[:, part], wq[part])
        if step == 0:
            total[:, :width] = term
        else:
            total[:, :width] += term
        if step == 1:
            small[2].wait()
            total[:, width : width + HD] = dot(scaled[...], wk[...])
            small[3].wait()
            total[:, width + HD : width + 2 * HD] = dot(scaled[...], wv[...])
            total[:, width + 2 * HD :] = jnp.broadcast_to(squares, (squares.shape[0], HD))


def split(total, weights, *outs):
    del weights
    width = total.shape[1] - 3 * HD
    rows = outs[0].shape[0]
    me = lax.axis_index("gx")
    first = lax.broadcasted_iota(jnp.int32, (rows, HD), 1) < HD // 2
    for mask, out in enumerate(outs):
        start = pl.multiple_of((me ^ mask) * rows, 8)
        part = total[pl.ds(start, rows), :]
        if mask:
            whole = part[:, width + 2 * HD :] * SQUARES
            high = whole.astype(BF16).astype(F32)
            out[:, : width + 2 * HD] = part[:, : width + 2 * HD]
            out[:, width + 2 * HD :] = jnp.where(first, high, whole - high)
        else:
            out[...] = part


def turn_keys(after, k, v, k_turned):
    del after, v
    rows, slots = k.shape[0], k.shape[1]
    for row in range(rows):
        for start in range(0, slots, CHUNK):
            part = slice(start, start + CHUNK)
            k_turned[row, :, part] = k[row, part, :].T


def attention(size, model, weights, lengths, cosine, sine, k, v, *refs):
    del weights
    arrived = refs[:size]
    heads, q_rows, o_rows, scores = refs[size:]
    rows, slots = k.shape[0], k.shape[2]
    group = heads.shape[1] // HD
    width = group * HD
    summed = arrived[0][:, : width + 2 * HD]
    squares = arrived[0][:, width + 2 * HD :]
    for item in arrived[1:]:
        summed = summed + item[:, : width + 2 * HD].astype(F32)
        parts = item[:, width + 2 * HD :].astype(F32)
        squares = squares + (parts + pltpu.roll(parts, HD // 2, 1)) * (1.0 / SQUARES)
    scale = lax.rsqrt(squares / model + EPS)
    cosines, sines = cosine[...], sine[...]

    def turn(value):
        return value * cosines + pltpu.roll(value, HD // 2, 1) * sines

    for head in range(group):
        part = summed[:, head * HD : (head + 1) * HD] * scale
        q_rows[head * rows : (head + 1) * rows] = turn(part).astype(BF16).astype(F32)
    new_keys = turn(summed[:, width : width + HD] * scale).astype(BF16).astype(F32)
    new_values = (summed[:, width + HD : width + 2 * HD] * scale).astype(BF16).astype(F32)
    rate = HD ** (-0.5) * math.log2(math.e)
    half = slots // 2
    slot = lax.broadcasted_iota(jnp.int32, (2 * group, half), 1) + half
    second = lax.broadcasted_iota(jnp.int32, (2 * group, 1), 0) >= group
    empty = jnp.zeros((group, HD), F32)
    own, top = [], []
    for row in range(0, rows, 2):
        first = q_rows[pl.ds(row, group, stride=rows), :]
        other = q_rows[pl.ds(row + 1, group, stride=rows), :]
        queries = jnp.concatenate(
            [jnp.concatenate([first, empty], 1), jnp.concatenate([empty, other], 1)], 0
        )
        keys = jnp.concatenate([k[row], k[row + 1]], 0)
        raw = jnp.dot(queries.astype(BF16), keys, preferred_element_type=F32)
        low = raw[:, :half]
        limit = jnp.where(second, lengths[row + 1 : row + 2, :1], lengths[row : row + 1, :1])
        high = jnp.where(slot < limit, raw[:, half:], -jnp.inf)
        mine = slice(row * group, (row + 2) * group)
        scores[mine, :half] = low
        scores[mine, half:] = high
        both = jnp.concatenate(
            [first * new_keys[row : row + 1], other * new_keys[row + 1 : row + 2]], 0
        )
        own.append(jnp.sum(both, 1, keepdims=True))
        top.append(jnp.maximum(jnp.max(jnp.maximum(low, high), 1, keepdims=True), own[-1]))

    def soften(pair):
        mine = slice(2 * pair * group, (2 * pair + 2) * group)
        probs = jnp.exp2((scores[mine] - top[pair]) * rate)
        own_prob = jnp.exp2((own[pair] - top[pair]) * rate)
        share = 1.0 / (jnp.sum(probs, 1, keepdims=True) + own_prob)
        return (probs * share).astype(BF16), (own_prob * share).astype(BF16).astype(F32)

    ready = soften(0)
    for pair in range(rows // 2):
        weights, own_weight = ready
        if pair + 1 < rows // 2:
            ready = soften(pair + 1)
        sides = jnp.concatenate([v[2 * pair], v[2 * pair + 1]], 1)
        mixed = jnp.dot(weights, sides, preferred_element_type=F32)
        for side in range(2):
            row = 2 * pair + side
            mine = slice(side * group, (side + 1) * group)
            value = mixed[mine, side * HD : (side + 1) * HD]
            extra = own_weight[mine] * new_values[row : row + 1]
            o_rows[pl.ds(row, group, stride=rows), :] = value + extra
    for head in range(group):
        heads[:, head * HD : (head + 1) * HD] = o_rows[head * rows : (head + 1) * rows].astype(BF16)


def gather_rows(blocks, gathered):
    me = lax.axis_index("gx")
    rows = blocks[0].shape[0]
    for mask, block in enumerate(blocks):
        start = pl.multiple_of((me ^ mask) * rows, 8)
        gathered[pl.ds(start, rows), :] = block[...].astype(F32)
    return gathered[...].astype(BF16)


def place(chunk, given):
    return 2 * chunk + ((lax.axis_index("gy") ^ given) & 1)


def project_out(size, chunk, w, *refs):
    blocks, out, gathered = refs[:size], refs[-2], refs[-1]
    heads = gather_rows(blocks, gathered)
    part = columns(place(chunk, 1), out.shape[1])
    out[...] = jnp.dot(heads, w[:, part], preferred_element_type=F32).astype(out.dtype)


def add_near(size, chunk, w, arrived, *refs):
    blocks, out, gathered = refs[:size], refs[-2], refs[-1]
    heads = gather_rows(blocks, gathered)
    part = columns(place(chunk, 0), out.shape[1])
    total = jnp.dot(heads, w[:, part], preferred_element_type=F32)
    out[...] = (total + arrived[...].astype(F32)).astype(BF16)


def finish(size, chunk, x, *refs):
    terms, out, ranked = refs[:size], refs[-2], refs[-1]
    rank = lax.axis_index("gy") // 2
    for mask, term in enumerate(terms):
        ranked[rank ^ mask] = term[...].astype(F32)
    total = ranked[0]
    for index in range(1, size):
        total = total + ranked[index]
    part = columns(place(chunk, 0), out.shape[1])
    out[...] = (x[:, part].astype(F32) + total).astype(BF16)


def assemble(*refs):
    *blocks, out, sems = refs
    width = blocks[0].shape[1]
    copies = []
    for index, block in enumerate(blocks):
        target = out.at[:, columns(place(index // 2, index % 2), width)]
        copies.append(pltpu.make_async_copy(block, target, sems.at[index]))
    for copy in copies:
        copy.start()
    for copy in copies:
        copy.wait()


def swap(value, axis, size, mask):
    return lax.ppermute(value, axis, [(i, i ^ mask) for i in range(size)])


def solution(mesh):
    size_x = mesh.shape["gx"]
    size_y = mesh.shape["gy"]
    sems = lambda n: pltpu.SemaphoreType.DMA((n,))

    def shards(inputs, gain, w_query, w_key, w_value, w_output, key_cache, value_cache, lengths):
        batch, depth = inputs.shape
        width = w_query.shape[1]
        rows = key_cache.shape[0]
        packed = width + 3 * HD
        block = w_output.shape[1] // 4

        total = pl.pallas_call(
            project,
            out_shape=pltpu.VMEM((batch, packed), F32),
            in_specs=[ANY] * 5,
            out_specs=VMEM,
            scratch_shapes=[
                pltpu.VMEM(inputs.shape, BF16),
                pltpu.VMEM((1, depth), F32),
                pltpu.VMEM(w_query.shape, BF16),
                pltpu.VMEM(w_key.shape, BF16),
                pltpu.VMEM(w_value.shape, BF16),
                pltpu.VMEM(inputs.shape, BF16),
                sems(depth // (2 * CHUNK) + 5),
            ],
            compiler_params=params(28),
            cost_estimate=cost(2 * batch * depth * packed, 2 * depth * packed),
            name="project",
        )(*[in_hbm(a) for a in (inputs, gain.reshape(1, depth), w_query, w_key, w_value)])
        sums = pl.pallas_call(
            split,
            out_shape=[pltpu.VMEM((rows, packed), F32)] * size_x,
            in_specs=[VMEM, ANY],
            out_specs=[VMEM] * size_x,
            compiler_params=params(4),
            name="split",
        )(in_vmem(total), in_hbm(w_query))
        arrived = [sums[0]]
        for mask in range(1, size_x):
            arrived.append(swap(sums[mask].astype(F16), "gx", size_x, mask).astype(F32))

        values = in_vmem(value_cache)
        keys = pl.pallas_call(
            turn_keys,
            out_shape=pltpu.VMEM((rows, HD, key_cache.shape[1]), BF16),
            in_specs=[ANY, VMEM, ANY],
            out_specs=VMEM,
            compiler_params=params(4),
            cost_estimate=cost(0, 2 * key_cache.size),
            name="turn_keys",
        )(sums[0], in_vmem(key_cache), values)

        half = HD // 2
        inverse = ROPE_BASE ** (-(jnp.arange(half, dtype=F32) * 2.0 / HD))
        angles = lengths.astype(F32)[:, None] * inverse[None, :]
        cosine, sine = jnp.cos(angles), jnp.sin(angles)
        lanes = rows * (width // HD)
        heads = pl.pallas_call(
            functools.partial(attention, size_x, depth * size_x),
            out_shape=pltpu.VMEM((rows, width), BF16),
            in_specs=[ANY] + [VMEM] * (5 + size_x),
            out_specs=VMEM,
            scratch_shapes=[
                pltpu.VMEM((lanes, HD), F32),
                pltpu.VMEM((lanes, HD), F32),
                pltpu.VMEM((lanes, key_cache.shape[1]), F32),
            ],
            compiler_params=params(8),
            cost_estimate=cost(4 * key_cache.size * (width // HD), 4 * key_cache.size),
            name="attention",
        )(
            in_hbm(w_query),
            jnp.broadcast_to(lengths[:, None], (rows, HD)),
            jnp.concatenate([cosine, cosine], 1),
            jnp.concatenate([-sine, sine], 1),
            in_vmem(keys),
            values,
            *[in_vmem(a) for a in arrived],
        )
        gathered = [heads] + [swap(heads, "gx", size_x, m) for m in range(1, size_x)]

        gathered = [in_vmem(a) for a in gathered]
        half = size_y // 2

        def product(kernel, chunk, *operands):
            return pl.pallas_call(
                functools.partial(kernel, size_x, chunk),
                out_shape=pltpu.VMEM((batch, block), BF16),
                in_specs=[VMEM] * (1 + len(operands) + size_x),
                out_specs=VMEM,
                scratch_shapes=[pltpu.VMEM((batch, width), F32)],
                compiler_params=params(8),
                cost_estimate=cost(2 * batch * width * block, 2 * width * block),
                name=kernel.__name__,
            )(in_vmem(w_output), *[in_vmem(a) for a in operands], *gathered)

        near = [swap(product(project_out, chunk), "gy", size_y, 1) for chunk in range(2)]
        blocks = []
        for chunk in range(2):
            pair = product(add_near, chunk, near[chunk])
            far = [pair] + [swap(pair, "gy", size_y, 2 * m) for m in range(1, half)]
            done = pl.pallas_call(
                functools.partial(finish, half, chunk),
                out_shape=pltpu.VMEM((batch, block), BF16),
                in_specs=[VMEM] * (1 + half),
                out_specs=VMEM,
                scratch_shapes=[pltpu.VMEM((half, batch, block), F32)],
                compiler_params=params(8),
                name="finish",
            )(in_vmem(inputs), *[in_vmem(a) for a in far])
            blocks += [done, swap(done, "gy", size_y, 1)]
        return pl.pallas_call(
            assemble,
            out_shape=jax.ShapeDtypeStruct((batch, block * 4), BF16),
            in_specs=[VMEM] * 4,
            out_specs=ANY,
            scratch_shapes=[sems(4)],
            compiler_params=params(4),
            name="assemble",
        )(*[in_vmem(b) for b in blocks])

    placed = (
        P("groups", "gx"),
        P("gx"),
        P("gx", "gy"),
        P("gx", "gy"),
        P("gx", "gy"),
        P("gy", "gx"),
        P(("groups", "gx"), None, "gy"),
        P(("groups", "gx"), None, "gy"),
        P(("groups", "gx")),
    )
    return jax.shard_map(
        shards, mesh=mesh, in_specs=placed, out_specs=P("groups", "gx"), check_vma=False
    )
```

```python
import functools
import math

import jax
import jax.numpy as jnp
from jax import lax
from jax.experimental import pallas as pl
from jax.experimental.pallas import tpu as pltpu
from jax.sharding import PartitionSpec as P

HD = 128
EPS = 1e-05
ROPE_BASE = 500000.0
CHUNK = 256
F32 = jnp.float32
BF16 = jnp.bfloat16
F16 = jnp.float16
SQUARES = 2.0**-8

ANY = pl.BlockSpec(memory_space=pl.ANY)
VMEM = pl.BlockSpec(memory_space=pltpu.VMEM)
MIB = 1 << 20


def columns(index, width):
    return pl.ds(pl.multiple_of(index * width, HD), width)


def params(mib):
    return pltpu.CompilerParams(vmem_limit_bytes=mib * MIB)


def cost(flops, nbytes):
    return pl.CostEstimate(flops=flops, bytes_accessed=nbytes, transcendentals=0)


def in_vmem(value):
    return pltpu.with_memory_space_constraint(value, pltpu.VMEM)


def in_hbm(value):
    return pltpu.with_memory_space_constraint(value, pltpu.HBM)


def project(x_hbm, gain_hbm, wq_hbm, wk_hbm, wv_hbm, *refs):
    total, x, gain, wq, wk, wv, scaled, sems = refs
    depth = x.shape[1]
    cuts = [*range(0, depth, 2 * CHUNK), depth - CHUNK, depth]
    spans = [slice(a, b) for a, b in zip(cuts, cuts[1:])]
    steps = len(spans)
    pairs = [(x_hbm, x), (gain_hbm, gain), (wk_hbm, wk), (wv_hbm, wv)]
    small = [pltpu.make_async_copy(a, b, sems.at[steps + i]) for i, (a, b) in enumerate(pairs)]
    large = []
    for step, span in enumerate(spans):
        part = pl.ds(span.start, span.stop - span.start)
        large.append(pltpu.make_async_copy(wq_hbm.at[part], wq.at[part], sems.at[step]))
    small[0].start()
    small[1].start()
    for copy in large[:2]:
        copy.start()
    small[2].start()
    small[3].start()
    for copy in large[2:]:
        copy.start()
    small[0].wait()
    small[1].wait()
    wide = x[...].astype(F32)
    scaled[...] = (wide * gain[...]).astype(BF16)
    squares = jnp.sum(wide * wide, 1, keepdims=True)
    width = wq.shape[1]
    dot = functools.partial(jnp.dot, preferred_element_type=F32)
    for step, copy in enumerate(large):
        copy.wait()
        part = spans[step]
        term = dot(scaled[:, part], wq[part])
        if step == 0:
            total[:, :width] = term
        else:
            total[:, :width] += term
        if step == 1:
            small[2].wait()
            total[:, width : width + HD] = dot(scaled[...], wk[...])
            small[3].wait()
            total[:, width + HD : width + 2 * HD] = dot(scaled[...], wv[...])
            total[:, width + 2 * HD :] = jnp.broadcast_to(squares, (squares.shape[0], HD))


def split(total, weights, *outs):
    del weights
    width = total.shape[1] - 3 * HD
    rows = outs[0].shape[0]
    me = lax.axis_index("gx")
    first = lax.broadcasted_iota(jnp.int32, (rows, HD), 1) < HD // 2
    for mask, out in enumerate(outs):
        start = pl.multiple_of((me ^ mask) * rows, 8)
        part = total[pl.ds(start, rows), :]
        if mask:
            whole = part[:, width + 2 * HD :] * SQUARES
            high = whole.astype(BF16).astype(F32)
            out[:, : width + 2 * HD] = part[:, : width + 2 * HD]
            out[:, width + 2 * HD :] = jnp.where(first, high, whole - high)
        else:
            out[...] = part


def turn_keys(after, k, v, k_turned):
    del after, v
    rows, slots = k.shape[0], k.shape[1]
    for row in range(rows):
        for start in range(0, slots, CHUNK):
            part = slice(start, start + CHUNK)
            k_turned[row, :, part] = k[row, part, :].T


def attention(size, model, weights, lengths, cosine, sine, k, v, *refs):
    del weights
    arrived = refs[:size]
    heads, q_rows, o_rows, scores = refs[size:]
    rows, slots = k.shape[0], k.shape[2]
    group = heads.shape[1] // HD
    width = group * HD
    summed = arrived[0][:, : width + 2 * HD]
    squares = arrived[0][:, width + 2 * HD :]
    for item in arrived[1:]:
        summed = summed + item[:, : width + 2 * HD].astype(F32)
        parts = item[:, width + 2 * HD :].astype(F32)
        squares = squares + (parts + pltpu.roll(parts, HD // 2, 1)) * (1.0 / SQUARES)
    scale = lax.rsqrt(squares / model + EPS)
    cosines, sines = cosine[...], sine[...]

    def turn(value):
        return value * cosines + pltpu.roll(value, HD // 2, 1) * sines

    for head in range(group):
        part = summed[:, head * HD : (head + 1) * HD] * scale
        q_rows[head * rows : (head + 1) * rows] = turn(part).astype(BF16).astype(F32)
    new_keys = turn(summed[:, width : width + HD] * scale).astype(BF16).astype(F32)
    new_values = (summed[:, width + HD : width + 2 * HD] * scale).astype(BF16).astype(F32)
    rate = HD ** (-0.5) * math.log2(math.e)
    half = slots // 2
    slot = lax.broadcasted_iota(jnp.int32, (2 * group, half), 1) + half
    second = lax.broadcasted_iota(jnp.int32, (2 * group, 1), 0) >= group
    empty = jnp.zeros((group, HD), F32)
    own, top = [], []
    for row in range(0, rows, 2):
        first = q_rows[pl.ds(row, group, stride=rows), :]
        other = q_rows[pl.ds(row + 1, group, stride=rows), :]
        queries = jnp.concatenate(
            [jnp.concatenate([first, empty], 1), jnp.concatenate([empty, other], 1)], 0
        )
        keys = jnp.concatenate([k[row], k[row + 1]], 0)
        raw = jnp.dot(queries.astype(BF16), keys, preferred_element_type=F32)
        low = raw[:, :half]
        limit = jnp.where(second, lengths[row + 1 : row + 2, :1], lengths[row : row + 1, :1])
        high = jnp.where(slot < limit, raw[:, half:], -jnp.inf)
        mine = slice(row * group, (row + 2) * group)
        scores[mine, :half] = low
        scores[mine, half:] = high
        both = jnp.concatenate(
            [first * new_keys[row : row + 1], other * new_keys[row + 1 : row + 2]], 0
        )
        own.append(jnp.sum(both, 1, keepdims=True))
        top.append(jnp.maximum(jnp.max(jnp.maximum(low, high), 1, keepdims=True), own[-1]))

    def soften(pair):
        mine = slice(2 * pair * group, (2 * pair + 2) * group)
        probs = jnp.exp2((scores[mine] - top[pair]) * rate)
        own_prob = jnp.exp2((own[pair] - top[pair]) * rate)
        share = 1.0 / (jnp.sum(probs, 1, keepdims=True) + own_prob)
        return (probs * share).astype(BF16), (own_prob * share).astype(BF16).astype(F32)

    ready = soften(0)
    for pair in range(rows // 2):
        weights, own_weight = ready
        if pair + 1 < rows // 2:
            ready = soften(pair + 1)
        sides = jnp.concatenate([v[2 * pair], v[2 * pair + 1]], 1)
        mixed = jnp.dot(weights, sides, preferred_element_type=F32)
        for side in range(2):
            row = 2 * pair + side
            mine = slice(side * group, (side + 1) * group)
            value = mixed[mine, side * HD : (side + 1) * HD]
            extra = own_weight[mine] * new_values[row : row + 1]
            o_rows[pl.ds(row, group, stride=rows), :] = value + extra
    for head in range(group):
        heads[:, head * HD : (head + 1) * HD] = o_rows[head * rows : (head + 1) * rows].astype(BF16)


def gather_rows(masks, blocks, gathered):
    me = lax.axis_index("gx")
    rows = blocks[0].shape[0]
    for mask, block in zip(masks, blocks):
        start = pl.multiple_of((me ^ mask) * rows, 8)
        gathered[pl.ds(start, rows), :] = block[...].astype(F32)
    return gathered[...].astype(BF16)


def half_of(given, width):
    return columns((lax.axis_index("gy") ^ given) & 1, width)


def project_out(masks, pick, w, *refs):
    *blocks, out, gathered = refs
    heads = gather_rows(masks, blocks, gathered)
    total = jnp.dot(heads, w[:, pick(out.shape[1])], preferred_element_type=F32)
    out[...] = total.astype(out.dtype)


def add_near(own, arrived, out):
    out[...] = (own[...].astype(F32) + arrived[...].astype(F32)).astype(BF16)


def finish(size, pick, x, *refs):
    *terms, out, ranked = refs
    rank = lax.axis_index("gy") // 2
    for mask, term in enumerate(terms):
        ranked[rank ^ mask] = term[...].astype(F32)
    total = ranked[0]
    for index in range(1, size):
        total = total + ranked[index]
    out[...] = (x[:, pick(out.shape[1])].astype(F32) + total).astype(BF16)


def assemble(kept, swapped, rest, out, sems):
    near, far = kept.shape[1], rest.shape[1]
    targets = [half_of(0, near), half_of(1, near), pl.ds(2 * near, far)]
    copies = []
    for index, (block, target) in enumerate(zip((kept, swapped, rest), targets)):
        copies.append(pltpu.make_async_copy(block, out.at[:, target], sems.at[index]))
    for copy in copies:
        copy.start()
    for copy in copies:
        copy.wait()


def swap(value, axis, size, mask):
    return lax.ppermute(value, axis, [(i, i ^ mask) for i in range(size)])


def solution(mesh):
    size_x = mesh.shape["gx"]
    size_y = mesh.shape["gy"]
    order = [0, *range(1, size_x, 2), *range(2, size_x, 2)]
    sems = lambda n: pltpu.SemaphoreType.DMA((n,))

    def shards(inputs, gain, w_query, w_key, w_value, w_output, key_cache, value_cache, lengths):
        batch, depth = inputs.shape
        width = w_query.shape[1]
        rows = key_cache.shape[0]
        packed = width + 3 * HD

        total = pl.pallas_call(
            project,
            out_shape=pltpu.VMEM((batch, packed), F32),
            in_specs=[ANY] * 5,
            out_specs=VMEM,
            scratch_shapes=[
                pltpu.VMEM(inputs.shape, BF16),
                pltpu.VMEM((1, depth), F32),
                pltpu.VMEM(w_query.shape, BF16),
                pltpu.VMEM(w_key.shape, BF16),
                pltpu.VMEM(w_value.shape, BF16),
                pltpu.VMEM(inputs.shape, BF16),
                sems(depth // (2 * CHUNK) + 5),
            ],
            compiler_params=params(28),
            cost_estimate=cost(2 * batch * depth * packed, 2 * depth * packed),
            name="project",
        )(*[in_hbm(a) for a in (inputs, gain.reshape(1, depth), w_query, w_key, w_value)])
        sums = pl.pallas_call(
            split,
            out_shape=[pltpu.VMEM((rows, packed), F32)] * size_x,
            in_specs=[VMEM, ANY],
            out_specs=[VMEM] * size_x,
            compiler_params=params(4),
            name="split",
        )(in_vmem(total), in_hbm(w_query))
        arrived = [sums[0]]
        for mask in order[1:]:
            arrived.append(swap(sums[mask].astype(F16), "gx", size_x, mask).astype(F32))

        values = in_vmem(value_cache)
        keys = pl.pallas_call(
            turn_keys,
            out_shape=pltpu.VMEM((rows, HD, key_cache.shape[1]), BF16),
            in_specs=[ANY, VMEM, ANY],
            out_specs=VMEM,
            compiler_params=params(4),
            cost_estimate=cost(0, 2 * key_cache.size),
            name="turn_keys",
        )(sums[0], in_vmem(key_cache), values)

        half = HD // 2
        inverse = ROPE_BASE ** (-(jnp.arange(half, dtype=F32) * 2.0 / HD))
        angles = lengths.astype(F32)[:, None] * inverse[None, :]
        cosine, sine = jnp.cos(angles), jnp.sin(angles)
        lanes = rows * (width // HD)
        heads = pl.pallas_call(
            functools.partial(attention, size_x, depth * size_x),
            out_shape=pltpu.VMEM((rows, width), BF16),
            in_specs=[ANY] + [VMEM] * (5 + size_x),
            out_specs=VMEM,
            scratch_shapes=[
                pltpu.VMEM((lanes, HD), F32),
                pltpu.VMEM((lanes, HD), F32),
                pltpu.VMEM((lanes, key_cache.shape[1]), F32),
            ],
            compiler_params=params(8),
            cost_estimate=cost(4 * key_cache.size * (width // HD), 4 * key_cache.size),
            name="attention",
        )(
            in_hbm(w_query),
            jnp.broadcast_to(lengths[:, None], (rows, HD)),
            jnp.concatenate([cosine, cosine], 1),
            jnp.concatenate([-sine, sine], 1),
            in_vmem(keys),
            values,
            *[in_vmem(a) for a in arrived],
        )
        gathered = [heads] + [swap(heads, "gx", size_x, m) for m in order[1:]]

        gathered = [in_vmem(a) for a in gathered]
        model_cut = w_output.shape[1]
        near = -(-5 * model_cut // (16 * HD)) * HD
        rest = model_cut - 2 * near
        picks = {
            "kept": functools.partial(half_of, 0),
            "given": functools.partial(half_of, 1),
            "rest": lambda far: pl.ds(2 * near, far),
        }

        def product(pick, block, kind):
            return pl.pallas_call(
                functools.partial(project_out, order, picks[pick]),
                out_shape=pltpu.VMEM((batch, block), kind),
                in_specs=[VMEM] * (1 + size_x),
                out_specs=VMEM,
                scratch_shapes=[pltpu.VMEM((batch, width), F32)],
                compiler_params=params(8),
                cost_estimate=cost(2 * batch * width * block, 2 * width * block),
                name="project_out",
            )(in_vmem(w_output), *gathered)

        def near_sum(own, arrived):
            return pl.pallas_call(
                add_near,
                out_shape=pltpu.VMEM(own.shape, BF16),
                in_specs=[VMEM] * 2,
                out_specs=VMEM,
                compiler_params=params(4),
                name="add_near",
            )(in_vmem(own), in_vmem(arrived))

        def far_sum(pick, pair):
            half = size_y // 2
            terms = [pair] + [swap(pair, "gy", size_y, 2 * m) for m in range(1, half)]
            return pl.pallas_call(
                functools.partial(finish, half, picks[pick]),
                out_shape=pltpu.VMEM(pair.shape, BF16),
                in_specs=[VMEM] * (1 + half),
                out_specs=VMEM,
                scratch_shapes=[pltpu.VMEM((half, *pair.shape), F32)],
                compiler_params=params(8),
                name="finish",
            )(in_vmem(inputs), *[in_vmem(a) for a in terms])

        near_a = swap(product("given", near, BF16), "gy", size_y, 1)
        own_b = product("rest", rest, BF16)
        near_b = swap(own_b, "gy", size_y, 1)
        kept = far_sum("kept", near_sum(product("kept", near, F32), near_a))
        swapped = swap(kept, "gy", size_y, 1)
        last = far_sum("rest", near_sum(own_b, near_b))
        return pl.pallas_call(
            assemble,
            out_shape=jax.ShapeDtypeStruct((batch, model_cut), BF16),
            in_specs=[VMEM] * 3,
            out_specs=ANY,
            scratch_shapes=[sems(3)],
            compiler_params=params(4),
            name="assemble",
        )(*[in_vmem(b) for b in (kept, swapped, last)])

    placed = (
        P("groups", "gx"),
        P("gx"),
        P("gx", "gy"),
        P("gx", "gy"),
        P("gx", "gy"),
        P("gy", "gx"),
        P(("groups", "gx"), None, "gy"),
        P(("groups", "gx"), None, "gy"),
        P(("groups", "gx")),
    )
    return jax.shard_map(
        shards, mesh=mesh, in_specs=placed, out_specs=P("groups", "gx"), check_vma=False
    )
```

```python
import functools
import math

import jax
import jax.numpy as jnp
from jax import lax
from jax.experimental import pallas as pl
from jax.experimental.pallas import tpu as pltpu
from jax.sharding import PartitionSpec as P

HD = 128
EPS = 1e-05
ROPE_BASE = 500000.0
CHUNK = 256
F32 = jnp.float32
BF16 = jnp.bfloat16
F16 = jnp.float16
SQUARES = 2.0**-8

ANY = pl.BlockSpec(memory_space=pl.ANY)
VMEM = pl.BlockSpec(memory_space=pltpu.VMEM)
MIB = 1 << 20


def columns(index, width):
    return pl.ds(pl.multiple_of(index * width, HD), width)


def params(mib):
    return pltpu.CompilerParams(vmem_limit_bytes=mib * MIB)


def cost(flops, nbytes):
    return pl.CostEstimate(flops=flops, bytes_accessed=nbytes, transcendentals=0)


def in_vmem(value):
    return pltpu.with_memory_space_constraint(value, pltpu.VMEM)


def in_hbm(value):
    return pltpu.with_memory_space_constraint(value, pltpu.HBM)


def project(x_hbm, gain_hbm, wq_hbm, wk_hbm, wv_hbm, *refs):
    total, x, gain, wq, wk, wv, scaled, sems = refs
    depth = x.shape[1]
    cuts = [*range(0, depth, 2 * CHUNK), depth - CHUNK, depth]
    spans = [slice(a, b) for a, b in zip(cuts, cuts[1:])]
    steps = len(spans)
    pairs = [(x_hbm, x), (gain_hbm, gain), (wk_hbm, wk), (wv_hbm, wv)]
    small = [pltpu.make_async_copy(a, b, sems.at[steps + i]) for i, (a, b) in enumerate(pairs)]
    large = []
    for step, span in enumerate(spans):
        part = pl.ds(span.start, span.stop - span.start)
        large.append(pltpu.make_async_copy(wq_hbm.at[part], wq.at[part], sems.at[step]))
    small[0].start()
    small[1].start()
    for copy in large[:2]:
        copy.start()
    small[2].start()
    small[3].start()
    for copy in large[2:]:
        copy.start()
    small[0].wait()
    small[1].wait()
    wide = x[...].astype(F32)
    scaled[...] = (wide * gain[...]).astype(BF16)
    squares = jnp.sum(wide * wide, 1, keepdims=True)
    width = wq.shape[1]
    dot = functools.partial(jnp.dot, preferred_element_type=F32)
    for step, copy in enumerate(large):
        copy.wait()
        part = spans[step]
        term = dot(scaled[:, part], wq[part])
        if step == 0:
            total[:, :width] = term
        else:
            total[:, :width] += term
        if step == 1:
            small[2].wait()
            total[:, width : width + HD] = dot(scaled[...], wk[...])
            small[3].wait()
            total[:, width + HD : width + 2 * HD] = dot(scaled[...], wv[...])
            total[:, width + 2 * HD :] = jnp.broadcast_to(squares, (squares.shape[0], HD))


def split(total, weights, *outs):
    del weights
    width = total.shape[1] - 3 * HD
    rows = outs[0].shape[0]
    me = lax.axis_index("gx")
    first = lax.broadcasted_iota(jnp.int32, (rows, HD), 1) < HD // 2
    for mask, out in enumerate(outs):
        start = pl.multiple_of((me ^ mask) * rows, 8)
        part = total[pl.ds(start, rows), :]
        if mask:
            whole = part[:, width + 2 * HD :] * SQUARES
            high = whole.astype(BF16).astype(F32)
            out[:, : width + 2 * HD] = part[:, : width + 2 * HD]
            out[:, width + 2 * HD :] = jnp.where(first, high, whole - high)
        else:
            out[...] = part


def turn_keys(after, k, v, k_turned):
    del after, v
    rows, slots = k.shape[0], k.shape[1]
    for row in range(rows):
        for start in range(0, slots, CHUNK):
            part = slice(start, start + CHUNK)
            k_turned[row, :, part] = k[row, part, :].T


def attention(size, model, weights, lengths, cosine, sine, k, v, *refs):
    del weights
    arrived = refs[:size]
    heads, q_rows, o_rows, scores = refs[size:]
    rows, slots = k.shape[0], k.shape[2]
    group = heads.shape[1] // HD
    width = group * HD
    summed = arrived[0][:, : width + 2 * HD]
    squares = arrived[0][:, width + 2 * HD :]
    for item in arrived[1:]:
        summed = summed + item[:, : width + 2 * HD].astype(F32)
        parts = item[:, width + 2 * HD :].astype(F32)
        squares = squares + (parts + pltpu.roll(parts, HD // 2, 1)) * (1.0 / SQUARES)
    scale = lax.rsqrt(squares / model + EPS)
    cosines, sines = cosine[...], sine[...]

    def turn(value):
        return value * cosines + pltpu.roll(value, HD // 2, 1) * sines

    for head in range(group):
        part = summed[:, head * HD : (head + 1) * HD] * scale
        q_rows[head * rows : (head + 1) * rows] = turn(part).astype(BF16).astype(F32)
    new_keys = turn(summed[:, width : width + HD] * scale).astype(BF16).astype(F32)
    new_values = (summed[:, width + HD : width + 2 * HD] * scale).astype(BF16).astype(F32)
    rate = HD ** (-0.5) * math.log2(math.e)
    half = slots // 2
    slot = lax.broadcasted_iota(jnp.int32, (2 * group, half), 1) + half
    second = lax.broadcasted_iota(jnp.int32, (2 * group, 1), 0) >= group
    empty = jnp.zeros((group, HD), F32)
    own, top = [], []
    for row in range(0, rows, 2):
        first = q_rows[pl.ds(row, group, stride=rows), :]
        other = q_rows[pl.ds(row + 1, group, stride=rows), :]
        queries = jnp.concatenate(
            [jnp.concatenate([first, empty], 1), jnp.concatenate([empty, other], 1)], 0
        )
        keys = jnp.concatenate([k[row], k[row + 1]], 0)
        raw = jnp.dot(queries.astype(BF16), keys, preferred_element_type=F32)
        low = raw[:, :half]
        limit = jnp.where(second, lengths[row + 1 : row + 2, :1], lengths[row : row + 1, :1])
        high = jnp.where(slot < limit, raw[:, half:], -jnp.inf)
        mine = slice(row * group, (row + 2) * group)
        scores[mine, :half] = low
        scores[mine, half:] = high
        both = jnp.concatenate(
            [first * new_keys[row : row + 1], other * new_keys[row + 1 : row + 2]], 0
        )
        own.append(jnp.sum(both, 1, keepdims=True))
        top.append(jnp.maximum(jnp.max(jnp.maximum(low, high), 1, keepdims=True), own[-1]))

    def soften(pair):
        mine = slice(2 * pair * group, (2 * pair + 2) * group)
        probs = jnp.exp2((scores[mine] - top[pair]) * rate)
        own_prob = jnp.exp2((own[pair] - top[pair]) * rate)
        share = 1.0 / (jnp.sum(probs, 1, keepdims=True) + own_prob)
        return (probs * share).astype(BF16), (own_prob * share).astype(BF16).astype(F32)

    ready = soften(0)
    for pair in range(rows // 2):
        weights, own_weight = ready
        if pair + 1 < rows // 2:
            ready = soften(pair + 1)
        sides = jnp.concatenate([v[2 * pair], v[2 * pair + 1]], 1)
        mixed = jnp.dot(weights, sides, preferred_element_type=F32)
        for side in range(2):
            row = 2 * pair + side
            mine = slice(side * group, (side + 1) * group)
            value = mixed[mine, side * HD : (side + 1) * HD]
            extra = own_weight[mine] * new_values[row : row + 1]
            o_rows[pl.ds(row, group, stride=rows), :] = value + extra
    for head in range(group):
        heads[:, head * HD : (head + 1) * HD] = o_rows[head * rows : (head + 1) * rows].astype(BF16)


def chip_rows(distance, rows):
    chip = (lax.axis_index("gx") // 2) ^ distance
    return pl.ds(pl.multiple_of(chip * 2 * rows, 16), 2 * rows)


def half_of(given, width):
    return columns((lax.axis_index("gy") ^ given) & 1, width)


def project_out(given, arrivals, w, *refs):
    arrived, blocks = refs[:arrivals], refs[arrivals:-2]
    out, gathered = refs[-2:]
    rows = blocks[0].shape[0]
    core = lax.axis_index("gx") & 1
    for index, block in enumerate(blocks):
        start = (index // 2) * 2 * rows + ((core ^ index) & 1) * rows
        gathered[pl.ds(pl.multiple_of(start, 8), rows), :] = block[...].astype(F32)
    heads = gathered[...].astype(BF16)
    width = out.shape[1]
    total = jnp.dot(heads, w[:, half_of(given, width)], preferred_element_type=F32)
    for item in arrived:
        total = total + item[...].astype(F32)
    out[...] = total.astype(out.dtype)


def add_near(own, arrived, out):
    out[...] = (own[...] + arrived[...].astype(F32)).astype(BF16)


def finish(distances, rows, x, *refs):
    *terms, out, ranked = refs
    rank = lax.axis_index("gy") // 2
    for mask, term in enumerate(terms):
        ranked[rank ^ mask] = term[...].astype(F32)
    part = half_of(0, out.shape[1])
    for index, distance in enumerate(distances):
        mine = slice(index * 2 * rows, (index + 1) * 2 * rows)
        total = ranked[0, mine]
        for other in range(1, len(terms)):
            total = total + ranked[other, mine]
        out[mine] = (x[chip_rows(distance, rows), part].astype(F32) + total).astype(BF16)


def assemble(chunks, rows, *refs):
    *blocks, out, sems = refs
    copies = []
    for index, block in enumerate(blocks):
        part = half_of(index % 2, block.shape[1])
        for place, distance in enumerate(chunks[index // 2]):
            source = block.at[pl.ds(place * 2 * rows, 2 * rows)]
            target = out.at[chip_rows(distance, rows), part]
            copies.append(pltpu.make_async_copy(source, target, sems.at[len(copies)]))
    for copy in copies:
        copy.start()
    for copy in copies:
        copy.wait()


def swap(value, axis, size, mask):
    return lax.ppermute(value, axis, [(i, i ^ mask) for i in range(size)])


def solution(mesh):
    size_x = mesh.shape["gx"]
    size_y = mesh.shape["gy"]
    sems = lambda n: pltpu.SemaphoreType.DMA((n,))

    def shards(inputs, gain, w_query, w_key, w_value, w_output, key_cache, value_cache, lengths):
        batch, depth = inputs.shape
        width = w_query.shape[1]
        rows = key_cache.shape[0]
        packed = width + 3 * HD

        total = pl.pallas_call(
            project,
            out_shape=pltpu.VMEM((batch, packed), F32),
            in_specs=[ANY] * 5,
            out_specs=VMEM,
            scratch_shapes=[
                pltpu.VMEM(inputs.shape, BF16),
                pltpu.VMEM((1, depth), F32),
                pltpu.VMEM(w_query.shape, BF16),
                pltpu.VMEM(w_key.shape, BF16),
                pltpu.VMEM(w_value.shape, BF16),
                pltpu.VMEM(inputs.shape, BF16),
                sems(depth // (2 * CHUNK) + 5),
            ],
            compiler_params=params(28),
            cost_estimate=cost(2 * batch * depth * packed, 2 * depth * packed),
            name="project",
        )(*[in_hbm(a) for a in (inputs, gain.reshape(1, depth), w_query, w_key, w_value)])
        sums = pl.pallas_call(
            split,
            out_shape=[pltpu.VMEM((rows, packed), F32)] * size_x,
            in_specs=[VMEM, ANY],
            out_specs=[VMEM] * size_x,
            compiler_params=params(4),
            name="split",
        )(in_vmem(total), in_hbm(w_query))
        arrived = [sums[0]]
        for mask in range(1, size_x):
            arrived.append(swap(sums[mask].astype(F16), "gx", size_x, mask).astype(F32))

        values = in_vmem(value_cache)
        keys = pl.pallas_call(
            turn_keys,
            out_shape=pltpu.VMEM((rows, HD, key_cache.shape[1]), BF16),
            in_specs=[ANY, VMEM, ANY],
            out_specs=VMEM,
            compiler_params=params(4),
            cost_estimate=cost(0, 2 * key_cache.size),
            name="turn_keys",
        )(sums[0], in_vmem(key_cache), values)

        half = HD // 2
        inverse = ROPE_BASE ** (-(jnp.arange(half, dtype=F32) * 2.0 / HD))
        angles = lengths.astype(F32)[:, None] * inverse[None, :]
        cosine, sine = jnp.cos(angles), jnp.sin(angles)
        lanes = rows * (width // HD)
        heads = pl.pallas_call(
            functools.partial(attention, size_x, depth * size_x),
            out_shape=pltpu.VMEM((rows, width), BF16),
            in_specs=[ANY] + [VMEM] * (5 + size_x),
            out_specs=VMEM,
            scratch_shapes=[
                pltpu.VMEM((lanes, HD), F32),
                pltpu.VMEM((lanes, HD), F32),
                pltpu.VMEM((lanes, key_cache.shape[1]), F32),
            ],
            compiler_params=params(8),
            cost_estimate=cost(4 * key_cache.size * (width // HD), 4 * key_cache.size),
            name="attention",
        )(
            in_hbm(w_query),
            jnp.broadcast_to(lengths[:, None], (rows, HD)),
            jnp.concatenate([cosine, cosine], 1),
            jnp.concatenate([-sine, sine], 1),
            in_vmem(keys),
            values,
            *[in_vmem(a) for a in arrived],
        )
        gathered = [heads] + [swap(heads, "gx", size_x, m) for m in range(1, size_x)]

        gathered = [in_vmem(a) for a in gathered]
        half = size_y // 2
        block = w_output.shape[1] // 2
        chunks = [list(range(1, size_x // 2)), [0]]

        def product(chunk, given, kind, *arrived):
            pieces = gathered[2:] if chunk == 0 else gathered[:2]
            tall = rows * len(pieces)
            return pl.pallas_call(
                functools.partial(project_out, given, len(arrived)),
                out_shape=pltpu.VMEM((tall, block), kind),
                in_specs=[VMEM] * (1 + len(arrived) + len(pieces)),
                out_specs=VMEM,
                scratch_shapes=[pltpu.VMEM((tall, width), F32)],
                compiler_params=params(8),
                cost_estimate=cost(2 * tall * width * block, 2 * width * block),
                name="project_out",
            )(in_vmem(w_output), *[in_vmem(a) for a in arrived], *pieces)

        near = [swap(product(chunk, 1, BF16), "gy", size_y, 1) for chunk in range(2)]
        blocks = []
        for chunk, distances in enumerate(chunks):
            tall = 2 * rows * len(distances)
            if chunk == 0:
                pair = product(chunk, 0, BF16, near[chunk])
            else:
                pair = pl.pallas_call(
                    add_near,
                    out_shape=pltpu.VMEM((tall, block), BF16),
                    in_specs=[VMEM] * 2,
                    out_specs=VMEM,
                    compiler_params=params(4),
                    name="add_near",
                )(in_vmem(product(chunk, 0, F32)), in_vmem(near[chunk]))
            far = [pair] + [swap(pair, "gy", size_y, 2 * m) for m in range(1, half)]
            done = pl.pallas_call(
                functools.partial(finish, distances, rows),
                out_shape=pltpu.VMEM((tall, block), BF16),
                in_specs=[VMEM] * (1 + half),
                out_specs=VMEM,
                scratch_shapes=[pltpu.VMEM((half, tall, block), F32)],
                compiler_params=params(8),
                name="finish",
            )(in_vmem(inputs), *[in_vmem(a) for a in far])
            blocks += [done, swap(done, "gy", size_y, 1)]
        return pl.pallas_call(
            functools.partial(assemble, chunks, rows),
            out_shape=jax.ShapeDtypeStruct((batch, 2 * block), BF16),
            in_specs=[VMEM] * 4,
            out_specs=ANY,
            scratch_shapes=[sems(size_x)],
            compiler_params=params(4),
            name="assemble",
        )(*[in_vmem(b) for b in blocks])

    placed = (
        P("groups", "gx"),
        P("gx"),
        P("gx", "gy"),
        P("gx", "gy"),
        P("gx", "gy"),
        P("gy", "gx"),
        P(("groups", "gx"), None, "gy"),
        P(("groups", "gx"), None, "gy"),
        P(("groups", "gx")),
    )
    return jax.shard_map(
        shards, mesh=mesh, in_specs=placed, out_specs=P("groups", "gx"), check_vma=False
    )
```

```python
import functools
import math

import jax
import jax.numpy as jnp
from jax import lax
from jax.experimental import pallas as pl
from jax.experimental.pallas import tpu as pltpu
from jax.sharding import PartitionSpec as P

HD = 128
EPS = 1e-05
ROPE_BASE = 500000.0
CHUNK = 256
F32 = jnp.float32
BF16 = jnp.bfloat16
F16 = jnp.float16
SQUARES = 2.0**-8

ANY = pl.BlockSpec(memory_space=pl.ANY)
VMEM = pl.BlockSpec(memory_space=pltpu.VMEM)
MIB = 1 << 20


def columns(index, width):
    return pl.ds(pl.multiple_of(index * width, HD), width)


def params(mib):
    return pltpu.CompilerParams(vmem_limit_bytes=mib * MIB)


def cost(flops, nbytes):
    return pl.CostEstimate(flops=flops, bytes_accessed=nbytes, transcendentals=0)


def in_vmem(value):
    return pltpu.with_memory_space_constraint(value, pltpu.VMEM)


def in_hbm(value):
    return pltpu.with_memory_space_constraint(value, pltpu.HBM)


def project(x_hbm, gain_hbm, wq_hbm, wk_hbm, wv_hbm, *refs):
    total, x, gain, wq, wk, wv, scaled, sems = refs
    depth = x.shape[1]
    cuts = [*range(0, depth, 2 * CHUNK), depth - CHUNK, depth]
    spans = [slice(a, b) for a, b in zip(cuts, cuts[1:])]
    steps = len(spans)
    pairs = [(x_hbm, x), (gain_hbm, gain), (wk_hbm, wk), (wv_hbm, wv)]
    small = [pltpu.make_async_copy(a, b, sems.at[steps + i]) for i, (a, b) in enumerate(pairs)]
    large = []
    for step, span in enumerate(spans):
        part = pl.ds(span.start, span.stop - span.start)
        large.append(pltpu.make_async_copy(wq_hbm.at[part], wq.at[part], sems.at[step]))
    small[0].start()
    small[1].start()
    for copy in large[:2]:
        copy.start()
    small[2].start()
    small[3].start()
    for copy in large[2:]:
        copy.start()
    small[0].wait()
    small[1].wait()
    wide = x[...].astype(F32)
    scaled[...] = (wide * gain[...]).astype(BF16)
    squares = jnp.sum(wide * wide, 1, keepdims=True)
    width = wq.shape[1]
    dot = functools.partial(jnp.dot, preferred_element_type=F32)
    for step, copy in enumerate(large):
        copy.wait()
        part = spans[step]
        term = dot(scaled[:, part], wq[part])
        if step == 0:
            total[:, :width] = term
        else:
            total[:, :width] += term
        if step == 1:
            small[2].wait()
            total[:, width : width + HD] = dot(scaled[...], wk[...])
            small[3].wait()
            total[:, width + HD : width + 2 * HD] = dot(scaled[...], wv[...])
            total[:, width + 2 * HD :] = jnp.broadcast_to(squares, (squares.shape[0], HD))


def split(total, weights, *outs):
    del weights
    width = total.shape[1] - 3 * HD
    rows = outs[0].shape[0]
    me = lax.axis_index("gx")
    first = lax.broadcasted_iota(jnp.int32, (rows, HD), 1) < HD // 2
    for mask, out in enumerate(outs):
        start = pl.multiple_of((me ^ mask) * rows, 8)
        part = total[pl.ds(start, rows), :]
        if mask:
            whole = part[:, width + 2 * HD :] * SQUARES
            high = whole.astype(BF16).astype(F32)
            out[:, : width + 2 * HD] = part[:, : width + 2 * HD]
            out[:, width + 2 * HD :] = jnp.where(first, high, whole - high)
        else:
            out[...] = part


def turn_keys(after, k, v, k_turned):
    del after, v
    rows, slots = k.shape[0], k.shape[1]
    for row in range(rows):
        for start in range(0, slots, CHUNK):
            part = slice(start, start + CHUNK)
            k_turned[row, :, part] = k[row, part, :].T


def attention(size, model, weights, lengths, cosine, sine, k, v, *refs):
    del weights
    arrived = refs[:size]
    heads, q_rows, o_rows, scores = refs[size:]
    rows, slots = k.shape[0], k.shape[2]
    group = heads.shape[1] // HD
    width = group * HD
    summed = arrived[0][:, : width + 2 * HD]
    squares = arrived[0][:, width + 2 * HD :]
    for item in arrived[1:]:
        summed = summed + item[:, : width + 2 * HD].astype(F32)
        parts = item[:, width + 2 * HD :].astype(F32)
        squares = squares + (parts + pltpu.roll(parts, HD // 2, 1)) * (1.0 / SQUARES)
    scale = lax.rsqrt(squares / model + EPS)
    cosines, sines = cosine[...], sine[...]

    def turn(value):
        return value * cosines + pltpu.roll(value, HD // 2, 1) * sines

    for head in range(group):
        part = summed[:, head * HD : (head + 1) * HD] * scale
        q_rows[head * rows : (head + 1) * rows] = turn(part).astype(BF16).astype(F32)
    new_keys = turn(summed[:, width : width + HD] * scale).astype(BF16).astype(F32)
    new_values = (summed[:, width + HD : width + 2 * HD] * scale).astype(BF16).astype(F32)
    rate = HD ** (-0.5) * math.log2(math.e)
    half = slots // 2
    slot = lax.broadcasted_iota(jnp.int32, (2 * group, half), 1) + half
    second = lax.broadcasted_iota(jnp.int32, (2 * group, 1), 0) >= group
    empty = jnp.zeros((group, HD), F32)
    own, top = [], []
    for row in range(0, rows, 2):
        first = q_rows[pl.ds(row, group, stride=rows), :]
        other = q_rows[pl.ds(row + 1, group, stride=rows), :]
        queries = jnp.concatenate(
            [jnp.concatenate([first, empty], 1), jnp.concatenate([empty, other], 1)], 0
        )
        keys = jnp.concatenate([k[row], k[row + 1]], 0)
        raw = jnp.dot(queries.astype(BF16), keys, preferred_element_type=F32)
        low = raw[:, :half]
        limit = jnp.where(second, lengths[row + 1 : row + 2, :1], lengths[row : row + 1, :1])
        high = jnp.where(slot < limit, raw[:, half:], -jnp.inf)
        mine = slice(row * group, (row + 2) * group)
        scores[mine, :half] = low
        scores[mine, half:] = high
        both = jnp.concatenate(
            [first * new_keys[row : row + 1], other * new_keys[row + 1 : row + 2]], 0
        )
        own.append(jnp.sum(both, 1, keepdims=True))
        top.append(jnp.maximum(jnp.max(jnp.maximum(low, high), 1, keepdims=True), own[-1]))

    def soften(pair):
        mine = slice(2 * pair * group, (2 * pair + 2) * group)
        probs = jnp.exp2((scores[mine] - top[pair]) * rate)
        own_prob = jnp.exp2((own[pair] - top[pair]) * rate)
        share = 1.0 / (jnp.sum(probs, 1, keepdims=True) + own_prob)
        return (probs * share).astype(BF16), (own_prob * share).astype(BF16).astype(F32)

    ready = soften(0)
    for pair in range(rows // 2):
        weights, own_weight = ready
        if pair + 1 < rows // 2:
            ready = soften(pair + 1)
        sides = jnp.concatenate([v[2 * pair], v[2 * pair + 1]], 1)
        mixed = jnp.dot(weights, sides, preferred_element_type=F32)
        for side in range(2):
            row = 2 * pair + side
            mine = slice(side * group, (side + 1) * group)
            value = mixed[mine, side * HD : (side + 1) * HD]
            extra = own_weight[mine] * new_values[row : row + 1]
            o_rows[pl.ds(row, group, stride=rows), :] = value + extra
    for head in range(group):
        heads[:, head * HD : (head + 1) * HD] = o_rows[head * rows : (head + 1) * rows].astype(BF16)


def chip_rows(distance, rows):
    chip = (lax.axis_index("gx") // 2) ^ distance
    return pl.ds(pl.multiple_of(chip * 2 * rows, 16), 2 * rows)


def half_of(given, width):
    return columns((lax.axis_index("gy") ^ given) & 1, width)


def project_out(given, w, *refs):
    blocks = refs[:-2]
    out, gathered = refs[-2:]
    rows = blocks[0].shape[0]
    core = lax.axis_index("gx") & 1
    for index, block in enumerate(blocks):
        start = (index // 2) * 2 * rows + ((core ^ index) & 1) * rows
        gathered[pl.ds(pl.multiple_of(start, 8), rows), :] = block[...].astype(F32)
    heads = gathered[...].astype(BF16)
    width = out.shape[1]
    total = jnp.dot(heads, w[:, half_of(given, width)], preferred_element_type=F32)
    out[...] = total.astype(out.dtype)


def add_near(own, arrived, out):
    out[...] = (own[...] + arrived[...].astype(F32)).astype(BF16)


def finish(distances, rows, x, *refs):
    *terms, out, ranked = refs
    rank = lax.axis_index("gy") // 2
    for mask, term in enumerate(terms):
        ranked[rank ^ mask] = term[...].astype(F32)
    part = half_of(0, out.shape[1])
    for index, distance in enumerate(distances):
        mine = slice(index * 2 * rows, (index + 1) * 2 * rows)
        total = ranked[0, mine]
        for other in range(1, len(terms)):
            total = total + ranked[other, mine]
        out[mine] = (x[chip_rows(distance, rows), part].astype(F32) + total).astype(BF16)


def assemble(chunks, rows, *refs):
    *blocks, out, sems = refs
    copies = []
    for index, block in enumerate(blocks):
        part = half_of(index % 2, block.shape[1])
        for place, distance in enumerate(chunks[index // 2]):
            source = block.at[pl.ds(place * 2 * rows, 2 * rows)]
            target = out.at[chip_rows(distance, rows), part]
            copies.append(pltpu.make_async_copy(source, target, sems.at[len(copies)]))
    for copy in copies:
        copy.start()
    for copy in copies:
        copy.wait()


def swap(value, axis, size, mask):
    return lax.ppermute(value, axis, [(i, i ^ mask) for i in range(size)])


def solution(mesh):
    size_x = mesh.shape["gx"]
    size_y = mesh.shape["gy"]
    sems = lambda n: pltpu.SemaphoreType.DMA((n,))

    def shards(inputs, gain, w_query, w_key, w_value, w_output, key_cache, value_cache, lengths):
        batch, depth = inputs.shape
        width = w_query.shape[1]
        rows = key_cache.shape[0]
        packed = width + 3 * HD

        total = pl.pallas_call(
            project,
            out_shape=pltpu.VMEM((batch, packed), F32),
            in_specs=[ANY] * 5,
            out_specs=VMEM,
            scratch_shapes=[
                pltpu.VMEM(inputs.shape, BF16),
                pltpu.VMEM((1, depth), F32),
                pltpu.VMEM(w_query.shape, BF16),
                pltpu.VMEM(w_key.shape, BF16),
                pltpu.VMEM(w_value.shape, BF16),
                pltpu.VMEM(inputs.shape, BF16),
                sems(depth // (2 * CHUNK) + 5),
            ],
            compiler_params=params(28),
            cost_estimate=cost(2 * batch * depth * packed, 2 * depth * packed),
            name="project",
        )(*[in_hbm(a) for a in (inputs, gain.reshape(1, depth), w_query, w_key, w_value)])
        sums = pl.pallas_call(
            split,
            out_shape=[pltpu.VMEM((rows, packed), F32)] * size_x,
            in_specs=[VMEM, ANY],
            out_specs=[VMEM] * size_x,
            compiler_params=params(4),
            name="split",
        )(in_vmem(total), in_hbm(w_query))
        arrived = [sums[0]]
        for mask in range(1, size_x):
            arrived.append(swap(sums[mask].astype(F16), "gx", size_x, mask).astype(F32))

        values = in_vmem(value_cache)
        keys = pl.pallas_call(
            turn_keys,
            out_shape=pltpu.VMEM((rows, HD, key_cache.shape[1]), BF16),
            in_specs=[ANY, VMEM, ANY],
            out_specs=VMEM,
            compiler_params=params(4),
            cost_estimate=cost(0, 2 * key_cache.size),
            name="turn_keys",
        )(sums[0], in_vmem(key_cache), values)

        half = HD // 2
        inverse = ROPE_BASE ** (-(jnp.arange(half, dtype=F32) * 2.0 / HD))
        angles = lengths.astype(F32)[:, None] * inverse[None, :]
        cosine, sine = jnp.cos(angles), jnp.sin(angles)
        lanes = rows * (width // HD)
        heads = pl.pallas_call(
            functools.partial(attention, size_x, depth * size_x),
            out_shape=pltpu.VMEM((rows, width), BF16),
            in_specs=[ANY] + [VMEM] * (5 + size_x),
            out_specs=VMEM,
            scratch_shapes=[
                pltpu.VMEM((lanes, HD), F32),
                pltpu.VMEM((lanes, HD), F32),
                pltpu.VMEM((lanes, key_cache.shape[1]), F32),
            ],
            compiler_params=params(8),
            cost_estimate=cost(4 * key_cache.size * (width // HD), 4 * key_cache.size),
            name="attention",
        )(
            in_hbm(w_query),
            jnp.broadcast_to(lengths[:, None], (rows, HD)),
            jnp.concatenate([cosine, cosine], 1),
            jnp.concatenate([-sine, sine], 1),
            in_vmem(keys),
            values,
            *[in_vmem(a) for a in arrived],
        )
        gathered = [heads] + [swap(heads, "gx", size_x, m) for m in range(1, size_x)]

        gathered = [in_vmem(a) for a in gathered]
        half = size_y // 2
        block = w_output.shape[1] // 2
        chunks = [list(range(1, size_x // 2)), [0]]

        def product(chunk, given, kind):
            pieces = gathered[2:] if chunk == 0 else gathered[:2]
            tall = rows * len(pieces)
            return pl.pallas_call(
                functools.partial(project_out, given),
                out_shape=pltpu.VMEM((tall, block), kind),
                in_specs=[VMEM] * (1 + len(pieces)),
                out_specs=VMEM,
                scratch_shapes=[pltpu.VMEM((tall, width), F32)],
                compiler_params=params(8),
                cost_estimate=cost(2 * tall * width * block, 2 * width * block),
                name="project_out",
            )(in_vmem(w_output), *pieces)

        near = [swap(product(chunk, 1, BF16), "gy", size_y, 1) for chunk in range(2)]
        blocks = []
        for chunk, distances in enumerate(chunks):
            tall = 2 * rows * len(distances)
            own = product(chunk, 0, F32)
            pair = pl.pallas_call(
                add_near,
                out_shape=pltpu.VMEM((tall, block), BF16),
                in_specs=[VMEM] * 2,
                out_specs=VMEM,
                compiler_params=params(4),
                name="add_near",
            )(in_vmem(own), in_vmem(near[chunk]))
            far = [pair] + [swap(pair, "gy", size_y, 2 * m) for m in range(1, half)]
            done = pl.pallas_call(
                functools.partial(finish, distances, rows),
                out_shape=pltpu.VMEM((tall, block), BF16),
                in_specs=[VMEM] * (1 + half),
                out_specs=VMEM,
                scratch_shapes=[pltpu.VMEM((half, tall, block), F32)],
                compiler_params=params(8),
                name="finish",
            )(in_vmem(inputs), *[in_vmem(a) for a in far])
            blocks += [done, swap(done, "gy", size_y, 1)]
        return pl.pallas_call(
            functools.partial(assemble, chunks, rows),
            out_shape=jax.ShapeDtypeStruct((batch, 2 * block), BF16),
            in_specs=[VMEM] * 4,
            out_specs=ANY,
            scratch_shapes=[sems(size_x)],
            compiler_params=params(4),
            name="assemble",
        )(*[in_vmem(b) for b in blocks])

    placed = (
        P("groups", "gx"),
        P("gx"),
        P("gx", "gy"),
        P("gx", "gy"),
        P("gx", "gy"),
        P("gy", "gx"),
        P(("groups", "gx"), None, "gy"),
        P(("groups", "gx"), None, "gy"),
        P(("groups", "gx")),
    )
    return jax.shard_map(
        shards, mesh=mesh, in_specs=placed, out_specs=P("groups", "gx"), check_vma=False
    )
```

```python
import functools
import math

import jax
import jax.numpy as jnp
from jax import lax
from jax.experimental import pallas as pl
from jax.experimental.pallas import tpu as pltpu
from jax.sharding import PartitionSpec as P

HD = 128
EPS = 1e-05
ROPE_BASE = 500000.0
CHUNK = 256
F32 = jnp.float32
BF16 = jnp.bfloat16
F16 = jnp.float16
SQUARES = 2.0**-8

ANY = pl.BlockSpec(memory_space=pl.ANY)
VMEM = pl.BlockSpec(memory_space=pltpu.VMEM)
MIB = 1 << 20


def columns(index, width):
    return pl.ds(pl.multiple_of(index * width, HD), width)


def params(mib):
    return pltpu.CompilerParams(vmem_limit_bytes=mib * MIB)


def cost(flops, nbytes):
    return pl.CostEstimate(flops=flops, bytes_accessed=nbytes, transcendentals=0)


def in_vmem(value):
    return pltpu.with_memory_space_constraint(value, pltpu.VMEM)


def in_hbm(value):
    return pltpu.with_memory_space_constraint(value, pltpu.HBM)


def project(x_hbm, gain_hbm, wq_hbm, wk_hbm, wv_hbm, *refs):
    total, x, gain, wq, wk, wv, scaled, sems = refs
    depth = x.shape[1]
    cuts = [*range(0, depth, 2 * CHUNK), depth - CHUNK, depth]
    spans = [slice(a, b) for a, b in zip(cuts, cuts[1:])]
    steps = len(spans)
    pairs = [(x_hbm, x), (gain_hbm, gain), (wk_hbm, wk), (wv_hbm, wv)]
    small = [pltpu.make_async_copy(a, b, sems.at[steps + i]) for i, (a, b) in enumerate(pairs)]
    large = []
    for step, span in enumerate(spans):
        part = pl.ds(span.start, span.stop - span.start)
        large.append(pltpu.make_async_copy(wq_hbm.at[part], wq.at[part], sems.at[step]))
    small[0].start()
    small[1].start()
    for copy in large[:2]:
        copy.start()
    small[2].start()
    small[3].start()
    for copy in large[2:]:
        copy.start()
    small[0].wait()
    small[1].wait()
    wide = x[...].astype(F32)
    scaled[...] = (wide * gain[...]).astype(BF16)
    squares = jnp.sum(wide * wide, 1, keepdims=True)
    width = wq.shape[1]
    dot = functools.partial(jnp.dot, preferred_element_type=F32)
    for step, copy in enumerate(large):
        copy.wait()
        part = spans[step]
        term = dot(scaled[:, part], wq[part])
        if step == 0:
            total[:, :width] = term
        else:
            total[:, :width] += term
        if step == 1:
            small[2].wait()
            total[:, width : width + HD] = dot(scaled[...], wk[...])
            small[3].wait()
            total[:, width + HD : width + 2 * HD] = dot(scaled[...], wv[...])
            total[:, width + 2 * HD :] = jnp.broadcast_to(squares, (squares.shape[0], HD))


def split(total, weights, *outs):
    del weights
    width = total.shape[1] - 3 * HD
    rows = outs[0].shape[0]
    me = lax.axis_index("gx")
    first = lax.broadcasted_iota(jnp.int32, (rows, HD), 1) < HD // 2
    for mask, out in enumerate(outs):
        start = pl.multiple_of((me ^ mask) * rows, 8)
        part = total[pl.ds(start, rows), :]
        if mask:
            whole = part[:, width + 2 * HD :] * SQUARES
            high = whole.astype(BF16).astype(F32)
            out[:, : width + 2 * HD] = part[:, : width + 2 * HD]
            out[:, width + 2 * HD :] = jnp.where(first, high, whole - high)
        else:
            out[...] = part


def turn_keys(after, k, v, k_turned):
    del after, v
    rows, slots = k.shape[0], k.shape[1]
    for row in range(rows):
        for start in range(0, slots, CHUNK):
            part = slice(start, start + CHUNK)
            k_turned[row, :, part] = k[row, part, :].T


def attention(size, model, weights, lengths, cosine, sine, k, v, *refs):
    del weights
    arrived = refs[:size]
    heads, q_rows, o_rows, scores = refs[size:]
    rows, slots = k.shape[0], k.shape[2]
    group = heads.shape[1] // HD
    width = group * HD
    summed = arrived[0][:, : width + 2 * HD]
    squares = arrived[0][:, width + 2 * HD :]
    for item in arrived[1:]:
        summed = summed + item[:, : width + 2 * HD].astype(F32)
        parts = item[:, width + 2 * HD :].astype(F32)
        squares = squares + (parts + pltpu.roll(parts, HD // 2, 1)) * (1.0 / SQUARES)
    scale = lax.rsqrt(squares / model + EPS)
    cosines, sines = cosine[...], sine[...]

    def turn(value):
        return value * cosines + pltpu.roll(value, HD // 2, 1) * sines

    for head in range(group):
        part = summed[:, head * HD : (head + 1) * HD] * scale
        q_rows[head * rows : (head + 1) * rows] = turn(part).astype(BF16).astype(F32)
    new_keys = turn(summed[:, width : width + HD] * scale).astype(BF16).astype(F32)
    new_values = (summed[:, width + HD : width + 2 * HD] * scale).astype(BF16).astype(F32)
    rate = HD ** (-0.5) * math.log2(math.e)
    half = slots // 2
    slot = lax.broadcasted_iota(jnp.int32, (2 * group, half), 1) + half
    second = lax.broadcasted_iota(jnp.int32, (2 * group, 1), 0) >= group
    empty = jnp.zeros((group, HD), F32)
    own, top = [], []
    for row in range(0, rows, 2):
        first = q_rows[pl.ds(row, group, stride=rows), :]
        other = q_rows[pl.ds(row + 1, group, stride=rows), :]
        queries = jnp.concatenate(
            [jnp.concatenate([first, empty], 1), jnp.concatenate([empty, other], 1)], 0
        )
        keys = jnp.concatenate([k[row], k[row + 1]], 0)
        raw = jnp.dot(queries.astype(BF16), keys, preferred_element_type=F32)
        low = raw[:, :half]
        limit = jnp.where(second, lengths[row + 1 : row + 2, :1], lengths[row : row + 1, :1])
        high = jnp.where(slot < limit, raw[:, half:], -jnp.inf)
        mine = slice(row * group, (row + 2) * group)
        scores[mine, :half] = low
        scores[mine, half:] = high
        both = jnp.concatenate(
            [first * new_keys[row : row + 1], other * new_keys[row + 1 : row + 2]], 0
        )
        own.append(jnp.sum(both, 1, keepdims=True))
        top.append(jnp.maximum(jnp.max(jnp.maximum(low, high), 1, keepdims=True), own[-1]))

    def soften(pair):
        mine = slice(2 * pair * group, (2 * pair + 2) * group)
        probs = jnp.exp2((scores[mine] - top[pair]) * rate)
        own_prob = jnp.exp2((own[pair] - top[pair]) * rate)
        share = 1.0 / (jnp.sum(probs, 1, keepdims=True) + own_prob)
        return (probs * share).astype(BF16), (own_prob * share).astype(BF16).astype(F32)

    ready = soften(0)
    for pair in range(rows // 2):
        weights, own_weight = ready
        if pair + 1 < rows // 2:
            ready = soften(pair + 1)
        sides = jnp.concatenate([v[2 * pair], v[2 * pair + 1]], 1)
        mixed = jnp.dot(weights, sides, preferred_element_type=F32)
        for side in range(2):
            row = 2 * pair + side
            mine = slice(side * group, (side + 1) * group)
            value = mixed[mine, side * HD : (side + 1) * HD]
            extra = own_weight[mine] * new_values[row : row + 1]
            o_rows[pl.ds(row, group, stride=rows), :] = value + extra
    for head in range(group):
        heads[:, head * HD : (head + 1) * HD] = o_rows[head * rows : (head + 1) * rows].astype(BF16)


def gather_rows(blocks, gathered):
    me = lax.axis_index("gx")
    rows = blocks[0].shape[0]
    for mask, block in enumerate(blocks):
        start = pl.multiple_of((me ^ mask) * rows, 8)
        gathered[pl.ds(start, rows), :] = block[...].astype(F32)
    return gathered[...].astype(BF16)


def place(chunk, given):
    return 2 * chunk + ((lax.axis_index("gy") ^ given) & 1)


def project_first(w, *refs):
    *blocks, out, heads, gathered = refs
    heads[...] = gather_rows(blocks, gathered)
    part = columns(place(0, 1), out.shape[1])
    out[...] = jnp.dot(heads[...], w[:, part], preferred_element_type=F32).astype(out.dtype)


def project_out(chunk, given, w, heads, out):
    part = columns(place(chunk, given), out.shape[1])
    out[...] = jnp.dot(heads[...], w[:, part], preferred_element_type=F32).astype(out.dtype)


def add_near(own, arrived, out):
    out[...] = (own[...] + arrived[...].astype(F32)).astype(BF16)


def finish(size, chunk, x, *refs):
    terms, out, ranked = refs[:size], refs[-2], refs[-1]
    rank = lax.axis_index("gy") // 2
    for mask, term in enumerate(terms):
        ranked[rank ^ mask] = term[...].astype(F32)
    total = ranked[0]
    for index in range(1, size):
        total = total + ranked[index]
    part = columns(place(chunk, 0), out.shape[1])
    out[...] = (x[:, part].astype(F32) + total).astype(BF16)


def write(places, *refs):
    blocks, out, sems = refs[: len(places)], refs[-2], refs[-1]
    copies = []
    for index, (block, (chunk, given)) in enumerate(zip(blocks, places)):
        target = out.at[:, columns(place(chunk, given), block.shape[1])]
        copies.append(pltpu.make_async_copy(block, target, sems.at[index]))
    for copy in copies:
        copy.start()
    for copy in copies:
        copy.wait()


def swap(value, axis, size, mask):
    return lax.ppermute(value, axis, [(i, i ^ mask) for i in range(size)])


def solution(mesh):
    size_x = mesh.shape["gx"]
    size_y = mesh.shape["gy"]
    sems = lambda n: pltpu.SemaphoreType.DMA((n,))

    def shards(inputs, gain, w_query, w_key, w_value, w_output, key_cache, value_cache, lengths):
        batch, depth = inputs.shape
        width = w_query.shape[1]
        rows = key_cache.shape[0]
        packed = width + 3 * HD
        block = w_output.shape[1] // 4

        total = pl.pallas_call(
            project,
            out_shape=pltpu.VMEM((batch, packed), F32),
            in_specs=[ANY] * 5,
            out_specs=VMEM,
            scratch_shapes=[
                pltpu.VMEM(inputs.shape, BF16),
                pltpu.VMEM((1, depth), F32),
                pltpu.VMEM(w_query.shape, BF16),
                pltpu.VMEM(w_key.shape, BF16),
                pltpu.VMEM(w_value.shape, BF16),
                pltpu.VMEM(inputs.shape, BF16),
                sems(depth // (2 * CHUNK) + 5),
            ],
            compiler_params=params(28),
            cost_estimate=cost(2 * batch * depth * packed, 2 * depth * packed),
            name="project",
        )(*[in_hbm(a) for a in (inputs, gain.reshape(1, depth), w_query, w_key, w_value)])
        sums = pl.pallas_call(
            split,
            out_shape=[pltpu.VMEM((rows, packed), F32)] * size_x,
            in_specs=[VMEM, ANY],
            out_specs=[VMEM] * size_x,
            compiler_params=params(4),
            name="split",
        )(in_vmem(total), in_hbm(w_query))
        arrived = [sums[0]]
        for mask in range(1, size_x):
            arrived.append(swap(sums[mask].astype(F16), "gx", size_x, mask).astype(F32))

        values = in_vmem(value_cache)
        keys = pl.pallas_call(
            turn_keys,
            out_shape=pltpu.VMEM((rows, HD, key_cache.shape[1]), BF16),
            in_specs=[ANY, VMEM, ANY],
            out_specs=VMEM,
            compiler_params=params(4),
            cost_estimate=cost(0, 2 * key_cache.size),
            name="turn_keys",
        )(sums[0], in_vmem(key_cache), values)

        half = HD // 2
        inverse = ROPE_BASE ** (-(jnp.arange(half, dtype=F32) * 2.0 / HD))
        angles = lengths.astype(F32)[:, None] * inverse[None, :]
        cosine, sine = jnp.cos(angles), jnp.sin(angles)
        lanes = rows * (width // HD)
        heads = pl.pallas_call(
            functools.partial(attention, size_x, depth * size_x),
            out_shape=pltpu.VMEM((rows, width), BF16),
            in_specs=[ANY] + [VMEM] * (5 + size_x),
            out_specs=VMEM,
            scratch_shapes=[
                pltpu.VMEM((lanes, HD), F32),
                pltpu.VMEM((lanes, HD), F32),
                pltpu.VMEM((lanes, key_cache.shape[1]), F32),
            ],
            compiler_params=params(8),
            cost_estimate=cost(4 * key_cache.size * (width // HD), 4 * key_cache.size),
            name="attention",
        )(
            in_hbm(w_query),
            jnp.broadcast_to(lengths[:, None], (rows, HD)),
            jnp.concatenate([cosine, cosine], 1),
            jnp.concatenate([-sine, sine], 1),
            in_vmem(keys),
            values,
            *[in_vmem(a) for a in arrived],
        )
        gathered = [heads] + [swap(heads, "gx", size_x, m) for m in range(1, size_x)]

        gathered = [in_vmem(a) for a in gathered]
        half = size_y // 2

        work = cost(2 * batch * width * block, 2 * width * block)
        first, everyone = pl.pallas_call(
            project_first,
            out_shape=[pltpu.VMEM((batch, block), BF16), pltpu.VMEM((batch, width), BF16)],
            in_specs=[VMEM] * (1 + size_x),
            out_specs=[VMEM] * 2,
            scratch_shapes=[pltpu.VMEM((batch, width), F32)],
            compiler_params=params(8),
            cost_estimate=work,
            name="project_first",
        )(in_vmem(w_output), *gathered)

        def product(chunk, given):
            return pl.pallas_call(
                functools.partial(project_out, chunk, given),
                out_shape=pltpu.VMEM((batch, block), BF16 if given else F32),
                in_specs=[VMEM] * 2,
                out_specs=VMEM,
                compiler_params=params(8),
                cost_estimate=work,
                name="project_out",
            )(in_vmem(w_output), in_vmem(everyone))

        near = [swap(term, "gy", size_y, 1) for term in (first, product(1, 1))]
        blocks = []
        for chunk in range(2):
            pair = pl.pallas_call(
                add_near,
                out_shape=pltpu.VMEM((batch, block), BF16),
                in_specs=[VMEM] * 2,
                out_specs=VMEM,
                compiler_params=params(4),
                name="add_near",
            )(in_vmem(product(chunk, 0)), in_vmem(near[chunk]))
            far = [pair] + [swap(pair, "gy", size_y, 2 * m) for m in range(1, half)]
            done = pl.pallas_call(
                functools.partial(finish, half, chunk),
                out_shape=pltpu.VMEM((batch, block), BF16),
                in_specs=[VMEM] * (1 + half),
                out_specs=VMEM,
                scratch_shapes=[pltpu.VMEM((half, batch, block), F32)],
                compiler_params=params(8),
                name="finish",
            )(in_vmem(inputs), *[in_vmem(a) for a in far])
            blocks += [done, swap(done, "gy", size_y, 1)]
        shape = jax.ShapeDtypeStruct((batch, block * 4), BF16)
        most = pl.pallas_call(
            functools.partial(write, [(0, 0), (0, 1), (1, 0)]),
            out_shape=shape,
            in_specs=[VMEM] * 3,
            out_specs=ANY,
            scratch_shapes=[sems(3)],
            compiler_params=params(4),
            name="write_most",
        )(*[in_vmem(b) for b in blocks[:3]])
        return pl.pallas_call(
            functools.partial(write, [(1, 1)]),
            out_shape=shape,
            in_specs=[VMEM, ANY],
            out_specs=ANY,
            scratch_shapes=[sems(1)],
            input_output_aliases={1: 0},
            compiler_params=params(4),
            name="write_last",
        )(in_vmem(blocks[3]), in_hbm(most))

    placed = (
        P("groups", "gx"),
        P("gx"),
        P("gx", "gy"),
        P("gx", "gy"),
        P("gx", "gy"),
        P("gy", "gx"),
        P(("groups", "gx"), None, "gy"),
        P(("groups", "gx"), None, "gy"),
        P(("groups", "gx")),
    )
    return jax.shard_map(
        shards, mesh=mesh, in_specs=placed, out_specs=P("groups", "gx"), check_vma=False
    )
```

```python
import functools
import math

import jax
import jax.numpy as jnp
from jax import lax
from jax.experimental import pallas as pl
from jax.experimental.pallas import tpu as pltpu
from jax.sharding import PartitionSpec as P

HD = 128
EPS = 1e-05
ROPE_BASE = 500000.0
CHUNK = 256
F32 = jnp.float32
BF16 = jnp.bfloat16
F16 = jnp.float16
SQUARES = 2.0**-8

ANY = pl.BlockSpec(memory_space=pl.ANY)
VMEM = pl.BlockSpec(memory_space=pltpu.VMEM)
MIB = 1 << 20


def columns(index, width):
    return pl.ds(pl.multiple_of(index * width, HD), width)


def params(mib):
    return pltpu.CompilerParams(vmem_limit_bytes=mib * MIB)


def cost(flops, nbytes):
    return pl.CostEstimate(flops=flops, bytes_accessed=nbytes, transcendentals=0)


def in_vmem(value):
    return pltpu.with_memory_space_constraint(value, pltpu.VMEM)


def in_hbm(value):
    return pltpu.with_memory_space_constraint(value, pltpu.HBM)


def project(x_hbm, gain_hbm, wq_hbm, wk_hbm, wv_hbm, *refs):
    total, x, gain, wq, wk, wv, scaled, sems = refs
    depth = x.shape[1]
    cuts = [*range(0, depth, 2 * CHUNK), depth - CHUNK, depth]
    spans = [slice(a, b) for a, b in zip(cuts, cuts[1:])]
    steps = len(spans)
    pairs = [(x_hbm, x), (gain_hbm, gain), (wk_hbm, wk), (wv_hbm, wv)]
    small = [pltpu.make_async_copy(a, b, sems.at[steps + i]) for i, (a, b) in enumerate(pairs)]
    large = []
    for step, span in enumerate(spans):
        part = pl.ds(span.start, span.stop - span.start)
        large.append(pltpu.make_async_copy(wq_hbm.at[part], wq.at[part], sems.at[step]))
    small[0].start()
    small[1].start()
    for copy in large[:2]:
        copy.start()
    small[2].start()
    small[3].start()
    for copy in large[2:]:
        copy.start()
    small[0].wait()
    small[1].wait()
    wide = x[...].astype(F32)
    scaled[...] = (wide * gain[...]).astype(BF16)
    squares = jnp.sum(wide * wide, 1, keepdims=True)
    width = wq.shape[1]
    dot = functools.partial(jnp.dot, preferred_element_type=F32)
    for step, copy in enumerate(large):
        copy.wait()
        part = spans[step]
        term = dot(scaled[:, part], wq[part])
        if step == 0:
            total[:, :width] = term
        else:
            total[:, :width] += term
        if step == 1:
            small[2].wait()
            total[:, width : width + HD] = dot(scaled[...], wk[...])
            small[3].wait()
            total[:, width + HD : width + 2 * HD] = dot(scaled[...], wv[...])
            total[:, width + 2 * HD :] = jnp.broadcast_to(squares, (squares.shape[0], HD))


def split(total, weights, *outs):
    del weights
    width = total.shape[1] - 3 * HD
    rows = outs[0].shape[0]
    me = lax.axis_index("gx")
    first = lax.broadcasted_iota(jnp.int32, (rows, HD), 1) < HD // 2
    for mask, out in enumerate(outs):
        start = pl.multiple_of((me ^ mask) * rows, 8)
        part = total[pl.ds(start, rows), :]
        if mask:
            whole = part[:, width + 2 * HD :] * SQUARES
            high = whole.astype(BF16).astype(F32)
            out[:, : width + 2 * HD] = part[:, : width + 2 * HD]
            out[:, width + 2 * HD :] = jnp.where(first, high, whole - high)
        else:
            out[...] = part


def turn_keys(after, k, v, k_turned):
    del after, v
    rows, slots = k.shape[0], k.shape[1]
    for row in range(rows):
        for start in range(0, slots, CHUNK):
            part = slice(start, start + CHUNK)
            k_turned[row, :, part] = k[row, part, :].T


def attention(size, model, weights, lengths, cosine, sine, k, v, *refs):
    del weights
    arrived = refs[:size]
    heads, q_rows, o_rows, scores = refs[size:]
    rows, slots = k.shape[0], k.shape[2]
    group = heads.shape[1] // HD
    width = group * HD
    summed = arrived[0][:, : width + 2 * HD]
    squares = arrived[0][:, width + 2 * HD :]
    for item in arrived[1:]:
        summed = summed + item[:, : width + 2 * HD].astype(F32)
        parts = item[:, width + 2 * HD :].astype(F32)
        squares = squares + (parts + pltpu.roll(parts, HD // 2, 1)) * (1.0 / SQUARES)
    scale = lax.rsqrt(squares / model + EPS)
    cosines, sines = cosine[...], sine[...]

    def turn(value):
        return value * cosines + pltpu.roll(value, HD // 2, 1) * sines

    for head in range(group):
        part = summed[:, head * HD : (head + 1) * HD] * scale
        q_rows[head * rows : (head + 1) * rows] = turn(part).astype(BF16).astype(F32)
    new_keys = turn(summed[:, width : width + HD] * scale).astype(BF16).astype(F32)
    new_values = (summed[:, width + HD : width + 2 * HD] * scale).astype(BF16).astype(F32)
    rate = HD ** (-0.5) * math.log2(math.e)
    half = slots // 2
    slot = lax.broadcasted_iota(jnp.int32, (2 * group, half), 1) + half
    second = lax.broadcasted_iota(jnp.int32, (2 * group, 1), 0) >= group
    empty = jnp.zeros((group, HD), F32)
    own, top = [], []
    for row in range(0, rows, 2):
        first = q_rows[pl.ds(row, group, stride=rows), :]
        other = q_rows[pl.ds(row + 1, group, stride=rows), :]
        queries = jnp.concatenate(
            [jnp.concatenate([first, empty], 1), jnp.concatenate([empty, other], 1)], 0
        )
        keys = jnp.concatenate([k[row], k[row + 1]], 0)
        raw = jnp.dot(queries.astype(BF16), keys, preferred_element_type=F32)
        low = raw[:, :half]
        limit = jnp.where(second, lengths[row + 1 : row + 2, :1], lengths[row : row + 1, :1])
        high = jnp.where(slot < limit, raw[:, half:], -jnp.inf)
        mine = slice(row * group, (row + 2) * group)
        scores[mine, :half] = low
        scores[mine, half:] = high
        both = jnp.concatenate(
            [first * new_keys[row : row + 1], other * new_keys[row + 1 : row + 2]], 0
        )
        own.append(jnp.sum(both, 1, keepdims=True))
        top.append(jnp.maximum(jnp.max(jnp.maximum(low, high), 1, keepdims=True), own[-1]))

    def soften(pair):
        mine = slice(2 * pair * group, (2 * pair + 2) * group)
        probs = jnp.exp2((scores[mine] - top[pair]) * rate)
        own_prob = jnp.exp2((own[pair] - top[pair]) * rate)
        share = 1.0 / (jnp.sum(probs, 1, keepdims=True) + own_prob)
        return (probs * share).astype(BF16), (own_prob * share).astype(BF16).astype(F32)

    ready = soften(0)
    for pair in range(rows // 2):
        weights, own_weight = ready
        if pair + 1 < rows // 2:
            ready = soften(pair + 1)
        sides = jnp.concatenate([v[2 * pair], v[2 * pair + 1]], 1)
        mixed = jnp.dot(weights, sides, preferred_element_type=F32)
        for side in range(2):
            row = 2 * pair + side
            mine = slice(side * group, (side + 1) * group)
            value = mixed[mine, side * HD : (side + 1) * HD]
            extra = own_weight[mine] * new_values[row : row + 1]
            o_rows[pl.ds(row, group, stride=rows), :] = value + extra
    for head in range(group):
        heads[:, head * HD : (head + 1) * HD] = o_rows[head * rows : (head + 1) * rows].astype(BF16)


def gather_rows(blocks, gathered):
    me = lax.axis_index("gx")
    rows = blocks[0].shape[0]
    for mask, block in enumerate(blocks):
        start = pl.multiple_of((me ^ mask) * rows, 8)
        gathered[pl.ds(start, rows), :] = block[...].astype(F32)
    return gathered[...].astype(BF16)


def place(chunk, given):
    return 2 * chunk + ((lax.axis_index("gy") ^ given) & 1)


def project_first(w, *refs):
    *blocks, out, heads, gathered = refs
    heads[...] = gather_rows(blocks, gathered)
    part = columns(place(0, 1), out.shape[1])
    out[...] = jnp.dot(heads[...], w[:, part], preferred_element_type=F32).astype(out.dtype)


def project_out(chunk, given, w, heads, out):
    part = columns(place(chunk, given), out.shape[1])
    out[...] = jnp.dot(heads[...], w[:, part], preferred_element_type=F32).astype(out.dtype)


def add_near(own, arrived, out):
    out[...] = (own[...] + arrived[...].astype(F32)).astype(BF16)


def finish(size, chunk, x, *refs):
    terms, out, ranked = refs[:size], refs[-2], refs[-1]
    rank = lax.axis_index("gy") // 2
    for mask, term in enumerate(terms):
        ranked[rank ^ mask] = term[...].astype(F32)
    total = ranked[0]
    for index in range(1, size):
        total = total + ranked[index]
    part = columns(place(chunk, 0), out.shape[1])
    out[...] = (x[:, part].astype(F32) + total).astype(BF16)


def write(places, *refs):
    blocks, out, sems = refs[: len(places)], refs[-2], refs[-1]
    copies = []
    for index, (block, (chunk, given)) in enumerate(zip(blocks, places)):
        target = out.at[:, columns(place(chunk, given), block.shape[1])]
        copies.append(pltpu.make_async_copy(block, target, sems.at[index]))
    for copy in copies:
        copy.start()
    for copy in copies:
        copy.wait()


def swap(value, axis, size, mask):
    return lax.ppermute(value, axis, [(i, i ^ mask) for i in range(size)])


def solution(mesh):
    size_x = mesh.shape["gx"]
    size_y = mesh.shape["gy"]
    sems = lambda n: pltpu.SemaphoreType.DMA((n,))

    def shards(inputs, gain, w_query, w_key, w_value, w_output, key_cache, value_cache, lengths):
        batch, depth = inputs.shape
        width = w_query.shape[1]
        rows = key_cache.shape[0]
        packed = width + 3 * HD
        block = w_output.shape[1] // 4

        total = pl.pallas_call(
            project,
            out_shape=pltpu.VMEM((batch, packed), F32),
            in_specs=[ANY] * 5,
            out_specs=VMEM,
            scratch_shapes=[
                pltpu.VMEM(inputs.shape, BF16),
                pltpu.VMEM((1, depth), F32),
                pltpu.VMEM(w_query.shape, BF16),
                pltpu.VMEM(w_key.shape, BF16),
                pltpu.VMEM(w_value.shape, BF16),
                pltpu.VMEM(inputs.shape, BF16),
                sems(depth // (2 * CHUNK) + 5),
            ],
            compiler_params=params(28),
            cost_estimate=cost(2 * batch * depth * packed, 2 * depth * packed),
            name="project",
        )(*[in_hbm(a) for a in (inputs, gain.reshape(1, depth), w_query, w_key, w_value)])
        sums = pl.pallas_call(
            split,
            out_shape=[pltpu.VMEM((rows, packed), F32)] * size_x,
            in_specs=[VMEM, ANY],
            out_specs=[VMEM] * size_x,
            compiler_params=params(4),
            name="split",
        )(in_vmem(total), in_hbm(w_query))
        arrived = [sums[0]]
        for mask in range(1, size_x):
            arrived.append(swap(sums[mask].astype(F16), "gx", size_x, mask).astype(F32))

        values = in_vmem(value_cache)
        keys = pl.pallas_call(
            turn_keys,
            out_shape=pltpu.VMEM((rows, HD, key_cache.shape[1]), BF16),
            in_specs=[ANY, VMEM, ANY],
            out_specs=VMEM,
            compiler_params=params(4),
            cost_estimate=cost(0, 2 * key_cache.size),
            name="turn_keys",
        )(sums[0], in_vmem(key_cache), values)

        half = HD // 2
        inverse = ROPE_BASE ** (-(jnp.arange(half, dtype=F32) * 2.0 / HD))
        angles = lengths.astype(F32)[:, None] * inverse[None, :]
        cosine, sine = jnp.cos(angles), jnp.sin(angles)
        lanes = rows * (width // HD)
        heads = pl.pallas_call(
            functools.partial(attention, size_x, depth * size_x),
            out_shape=pltpu.VMEM((rows, width), BF16),
            in_specs=[ANY] + [VMEM] * (5 + size_x),
            out_specs=VMEM,
            scratch_shapes=[
                pltpu.VMEM((lanes, HD), F32),
                pltpu.VMEM((lanes, HD), F32),
                pltpu.VMEM((lanes, key_cache.shape[1]), F32),
            ],
            compiler_params=params(8),
            cost_estimate=cost(4 * key_cache.size * (width // HD), 4 * key_cache.size),
            name="attention",
        )(
            in_hbm(w_query),
            jnp.broadcast_to(lengths[:, None], (rows, HD)),
            jnp.concatenate([cosine, cosine], 1),
            jnp.concatenate([-sine, sine], 1),
            in_vmem(keys),
            values,
            *[in_vmem(a) for a in arrived],
        )
        gathered = [heads] + [swap(heads, "gx", size_x, m) for m in range(1, size_x)]

        gathered = [in_vmem(a) for a in gathered]
        half = size_y // 2

        work = cost(2 * batch * width * block, 2 * width * block)
        first, everyone = pl.pallas_call(
            project_first,
            out_shape=[pltpu.VMEM((batch, block), BF16), pltpu.VMEM((batch, width), BF16)],
            in_specs=[VMEM] * (1 + size_x),
            out_specs=[VMEM] * 2,
            scratch_shapes=[pltpu.VMEM((batch, width), F32)],
            compiler_params=params(8),
            cost_estimate=work,
            name="project_first",
        )(in_vmem(w_output), *gathered)

        def product(chunk, given):
            return pl.pallas_call(
                functools.partial(project_out, chunk, given),
                out_shape=pltpu.VMEM((batch, block), BF16 if given else F32),
                in_specs=[VMEM] * 2,
                out_specs=VMEM,
                compiler_params=params(8),
                cost_estimate=work,
                name="project_out",
            )(in_vmem(w_output), in_vmem(everyone))

        near = [swap(term, "gy", size_y, 1) for term in (first, product(1, 1))]
        blocks = []
        for chunk in range(2):
            pair = pl.pallas_call(
                add_near,
                out_shape=pltpu.VMEM((batch, block), BF16),
                in_specs=[VMEM] * 2,
                out_specs=VMEM,
                compiler_params=params(4),
                name="add_near",
            )(in_vmem(product(chunk, 0)), in_vmem(near[chunk]))
            far = [pair] + [swap(pair, "gy", size_y, 2 * m) for m in range(1, half)]
            done = pl.pallas_call(
                functools.partial(finish, half, chunk),
                out_shape=pltpu.VMEM((batch, block), BF16),
                in_specs=[VMEM] * (1 + half),
                out_specs=VMEM,
                scratch_shapes=[pltpu.VMEM((half, batch, block), F32)],
                compiler_params=params(8),
                name="finish",
            )(in_vmem(inputs), *[in_vmem(a) for a in far])
            blocks += [done, swap(done, "gy", size_y, 1)]
        shape = jax.ShapeDtypeStruct((batch, block * 4), BF16)
        own_half = pl.pallas_call(
            functools.partial(write, [(0, 0), (1, 0)]),
            out_shape=shape,
            in_specs=[VMEM] * 2,
            out_specs=ANY,
            scratch_shapes=[sems(2)],
            compiler_params=params(4),
            name="write_own",
        )(*[in_vmem(b) for b in blocks[::2]])
        return pl.pallas_call(
            functools.partial(write, [(0, 1), (1, 1)]),
            out_shape=shape,
            in_specs=[VMEM, VMEM, ANY],
            out_specs=ANY,
            scratch_shapes=[sems(2)],
            input_output_aliases={2: 0},
            compiler_params=params(4),
            name="write_last",
        )(*[in_vmem(b) for b in blocks[1::2]], in_hbm(own_half))

    placed = (
        P("groups", "gx"),
        P("gx"),
        P("gx", "gy"),
        P("gx", "gy"),
        P("gx", "gy"),
        P("gy", "gx"),
        P(("groups", "gx"), None, "gy"),
        P(("groups", "gx"), None, "gy"),
        P(("groups", "gx")),
    )
    return jax.shard_map(
        shards, mesh=mesh, in_specs=placed, out_specs=P("groups", "gx"), check_vma=False
    )
```

```python
import functools
import math

import jax
import jax.numpy as jnp
from jax import lax
from jax.experimental import pallas as pl
from jax.experimental.pallas import tpu as pltpu
from jax.sharding import PartitionSpec as P

HD = 128
EPS = 1e-05
ROPE_BASE = 500000.0
CHUNK = 256
F32 = jnp.float32
BF16 = jnp.bfloat16
F16 = jnp.float16
SQUARES = 2.0**-8

ANY = pl.BlockSpec(memory_space=pl.ANY)
VMEM = pl.BlockSpec(memory_space=pltpu.VMEM)
MIB = 1 << 20


def columns(index, width):
    return pl.ds(pl.multiple_of(index * width, HD), width)


def params(mib):
    return pltpu.CompilerParams(vmem_limit_bytes=mib * MIB)


def cost(flops, nbytes):
    return pl.CostEstimate(flops=flops, bytes_accessed=nbytes, transcendentals=0)


def in_vmem(value):
    return pltpu.with_memory_space_constraint(value, pltpu.VMEM)


def in_hbm(value):
    return pltpu.with_memory_space_constraint(value, pltpu.HBM)


def project(x_hbm, gain_hbm, wq_hbm, wk_hbm, wv_hbm, *refs):
    total, x, gain, wq, wk, wv, scaled, sems = refs
    depth = x.shape[1]
    cuts = [*range(0, depth, 2 * CHUNK), depth - CHUNK, depth]
    spans = [slice(a, b) for a, b in zip(cuts, cuts[1:])]
    steps = len(spans)
    pairs = [(x_hbm, x), (gain_hbm, gain), (wk_hbm, wk), (wv_hbm, wv)]
    small = [pltpu.make_async_copy(a, b, sems.at[steps + i]) for i, (a, b) in enumerate(pairs)]
    large = []
    for step, span in enumerate(spans):
        part = pl.ds(span.start, span.stop - span.start)
        large.append(pltpu.make_async_copy(wq_hbm.at[part], wq.at[part], sems.at[step]))
    small[0].start()
    small[1].start()
    for copy in large[:2]:
        copy.start()
    small[2].start()
    small[3].start()
    for copy in large[2:]:
        copy.start()
    small[0].wait()
    small[1].wait()
    wide = x[...].astype(F32)
    scaled[...] = (wide * gain[...]).astype(BF16)
    squares = jnp.sum(wide * wide, 1, keepdims=True)
    width = wq.shape[1]
    dot = functools.partial(jnp.dot, preferred_element_type=F32)
    for step, copy in enumerate(large):
        copy.wait()
        part = spans[step]
        term = dot(scaled[:, part], wq[part])
        if step == 0:
            total[:, :width] = term
        else:
            total[:, :width] += term
        if step == 1:
            small[2].wait()
            total[:, width : width + HD] = dot(scaled[...], wk[...])
            small[3].wait()
            total[:, width + HD : width + 2 * HD] = dot(scaled[...], wv[...])
            total[:, width + 2 * HD :] = jnp.broadcast_to(squares, (squares.shape[0], HD))


def split(total, weights, *outs):
    del weights
    width = total.shape[1] - 3 * HD
    rows = outs[0].shape[0]
    me = lax.axis_index("gx")
    first = lax.broadcasted_iota(jnp.int32, (rows, HD), 1) < HD // 2
    for mask, out in enumerate(outs):
        start = pl.multiple_of((me ^ mask) * rows, 8)
        part = total[pl.ds(start, rows), :]
        if mask:
            whole = part[:, width + 2 * HD :] * SQUARES
            high = whole.astype(BF16).astype(F32)
            out[:, : width + 2 * HD] = part[:, : width + 2 * HD]
            out[:, width + 2 * HD :] = jnp.where(first, high, whole - high)
        else:
            out[...] = part


def turn_keys(after, k, v, k_turned):
    del after, v
    rows, slots = k.shape[0], k.shape[1]
    for row in range(rows):
        for start in range(0, slots, CHUNK):
            part = slice(start, start + CHUNK)
            k_turned[row, :, part] = k[row, part, :].T


def attention(size, model, weights, lengths, cosine, sine, k, v, *refs):
    del weights
    arrived = refs[:size]
    heads, q_rows, o_rows, scores = refs[size:]
    rows, slots = k.shape[0], k.shape[2]
    group = heads.shape[1] // HD
    width = group * HD
    summed = arrived[0][:, : width + 2 * HD]
    squares = arrived[0][:, width + 2 * HD :]
    for item in arrived[1:]:
        summed = summed + item[:, : width + 2 * HD].astype(F32)
        parts = item[:, width + 2 * HD :].astype(F32)
        squares = squares + (parts + pltpu.roll(parts, HD // 2, 1)) * (1.0 / SQUARES)
    scale = lax.rsqrt(squares / model + EPS)
    cosines, sines = cosine[...], sine[...]

    def turn(value):
        return value * cosines + pltpu.roll(value, HD // 2, 1) * sines

    for head in range(group):
        part = summed[:, head * HD : (head + 1) * HD] * scale
        q_rows[head * rows : (head + 1) * rows] = turn(part).astype(BF16).astype(F32)
    new_keys = turn(summed[:, width : width + HD] * scale).astype(BF16).astype(F32)
    new_values = (summed[:, width + HD : width + 2 * HD] * scale).astype(BF16).astype(F32)
    rate = HD ** (-0.5) * math.log2(math.e)
    half = slots // 2
    slot = lax.broadcasted_iota(jnp.int32, (2 * group, half), 1) + half
    second = lax.broadcasted_iota(jnp.int32, (2 * group, 1), 0) >= group
    empty = jnp.zeros((group, HD), F32)
    own, top = [], []
    for row in range(0, rows, 2):
        first = q_rows[pl.ds(row, group, stride=rows), :]
        other = q_rows[pl.ds(row + 1, group, stride=rows), :]
        queries = jnp.concatenate(
            [jnp.concatenate([first, empty], 1), jnp.concatenate([empty, other], 1)], 0
        )
        keys = jnp.concatenate([k[row], k[row + 1]], 0)
        raw = jnp.dot(queries.astype(BF16), keys, preferred_element_type=F32)
        low = raw[:, :half]
        limit = jnp.where(second, lengths[row + 1 : row + 2, :1], lengths[row : row + 1, :1])
        high = jnp.where(slot < limit, raw[:, half:], -jnp.inf)
        mine = slice(row * group, (row + 2) * group)
        scores[mine, :half] = low
        scores[mine, half:] = high
        both = jnp.concatenate(
            [first * new_keys[row : row + 1], other * new_keys[row + 1 : row + 2]], 0
        )
        own.append(jnp.sum(both, 1, keepdims=True))
        top.append(jnp.maximum(jnp.max(jnp.maximum(low, high), 1, keepdims=True), own[-1]))

    def soften(pair):
        mine = slice(2 * pair * group, (2 * pair + 2) * group)
        probs = jnp.exp2((scores[mine] - top[pair]) * rate)
        own_prob = jnp.exp2((own[pair] - top[pair]) * rate)
        share = 1.0 / (jnp.sum(probs, 1, keepdims=True) + own_prob)
        return (probs * share).astype(BF16), (own_prob * share).astype(BF16).astype(F32)

    ready = soften(0)
    for pair in range(rows // 2):
        weights, own_weight = ready
        if pair + 1 < rows // 2:
            ready = soften(pair + 1)
        sides = jnp.concatenate([v[2 * pair], v[2 * pair + 1]], 1)
        mixed = jnp.dot(weights, sides, preferred_element_type=F32)
        for side in range(2):
            row = 2 * pair + side
            mine = slice(side * group, (side + 1) * group)
            value = mixed[mine, side * HD : (side + 1) * HD]
            extra = own_weight[mine] * new_values[row : row + 1]
            o_rows[pl.ds(row, group, stride=rows), :] = value + extra
    for head in range(group):
        heads[:, head * HD : (head + 1) * HD] = o_rows[head * rows : (head + 1) * rows].astype(BF16)


def chip_rows(distance, rows):
    chip = (lax.axis_index("gx") // 2) ^ distance
    return pl.ds(pl.multiple_of(chip * 2 * rows, 16), 2 * rows)


def half_of(given, width):
    return columns((lax.axis_index("gy") ^ given) & 1, width)


def project_out(given, afters, w, *refs):
    blocks = refs[afters:-2]
    out, gathered = refs[-2:]
    rows = blocks[0].shape[0]
    core = lax.axis_index("gx") & 1
    for index, block in enumerate(blocks):
        start = (index // 2) * 2 * rows + ((core ^ index) & 1) * rows
        gathered[pl.ds(pl.multiple_of(start, 8), rows), :] = block[...].astype(F32)
    heads = gathered[...].astype(BF16)
    width = out.shape[1]
    total = jnp.dot(heads, w[:, half_of(given, width)], preferred_element_type=F32)
    out[...] = total.astype(out.dtype)


def add_near(own, arrived, out):
    out[...] = (own[...] + arrived[...].astype(F32)).astype(BF16)


def finish(distances, rows, x, *refs):
    *terms, out, ranked = refs
    rank = lax.axis_index("gy") // 2
    for mask, term in enumerate(terms):
        ranked[rank ^ mask] = term[...].astype(F32)
    part = half_of(0, out.shape[1])
    for index, distance in enumerate(distances):
        mine = slice(index * 2 * rows, (index + 1) * 2 * rows)
        total = ranked[0, mine]
        for other in range(1, len(terms)):
            total = total + ranked[other, mine]
        out[mine] = (x[chip_rows(distance, rows), part].astype(F32) + total).astype(BF16)


def assemble(chunks, rows, *refs):
    *blocks, out, sems = refs
    copies = []
    for index, block in enumerate(blocks):
        part = half_of(index % 2, block.shape[1])
        for place, distance in enumerate(chunks[index // 2]):
            source = block.at[pl.ds(place * 2 * rows, 2 * rows)]
            target = out.at[chip_rows(distance, rows), part]
            copies.append(pltpu.make_async_copy(source, target, sems.at[len(copies)]))
    for copy in copies:
        copy.start()
    for copy in copies:
        copy.wait()


def swap(value, axis, size, mask):
    return lax.ppermute(value, axis, [(i, i ^ mask) for i in range(size)])


def solution(mesh):
    size_x = mesh.shape["gx"]
    size_y = mesh.shape["gy"]
    sems = lambda n: pltpu.SemaphoreType.DMA((n,))

    def shards(inputs, gain, w_query, w_key, w_value, w_output, key_cache, value_cache, lengths):
        batch, depth = inputs.shape
        width = w_query.shape[1]
        rows = key_cache.shape[0]
        packed = width + 3 * HD

        total = pl.pallas_call(
            project,
            out_shape=pltpu.VMEM((batch, packed), F32),
            in_specs=[ANY] * 5,
            out_specs=VMEM,
            scratch_shapes=[
                pltpu.VMEM(inputs.shape, BF16),
                pltpu.VMEM((1, depth), F32),
                pltpu.VMEM(w_query.shape, BF16),
                pltpu.VMEM(w_key.shape, BF16),
                pltpu.VMEM(w_value.shape, BF16),
                pltpu.VMEM(inputs.shape, BF16),
                sems(depth // (2 * CHUNK) + 5),
            ],
            compiler_params=params(28),
            cost_estimate=cost(2 * batch * depth * packed, 2 * depth * packed),
            name="project",
        )(*[in_hbm(a) for a in (inputs, gain.reshape(1, depth), w_query, w_key, w_value)])
        sums = pl.pallas_call(
            split,
            out_shape=[pltpu.VMEM((rows, packed), F32)] * size_x,
            in_specs=[VMEM, ANY],
            out_specs=[VMEM] * size_x,
            compiler_params=params(4),
            name="split",
        )(in_vmem(total), in_hbm(w_query))
        arrived = [sums[0]]
        for mask in range(1, size_x):
            arrived.append(swap(sums[mask].astype(F16), "gx", size_x, mask).astype(F32))

        values = in_vmem(value_cache)
        keys = pl.pallas_call(
            turn_keys,
            out_shape=pltpu.VMEM((rows, HD, key_cache.shape[1]), BF16),
            in_specs=[ANY, VMEM, ANY],
            out_specs=VMEM,
            compiler_params=params(4),
            cost_estimate=cost(0, 2 * key_cache.size),
            name="turn_keys",
        )(sums[0], in_vmem(key_cache), values)

        half = HD // 2
        inverse = ROPE_BASE ** (-(jnp.arange(half, dtype=F32) * 2.0 / HD))
        angles = lengths.astype(F32)[:, None] * inverse[None, :]
        cosine, sine = jnp.cos(angles), jnp.sin(angles)
        lanes = rows * (width // HD)
        heads = pl.pallas_call(
            functools.partial(attention, size_x, depth * size_x),
            out_shape=pltpu.VMEM((rows, width), BF16),
            in_specs=[ANY] + [VMEM] * (5 + size_x),
            out_specs=VMEM,
            scratch_shapes=[
                pltpu.VMEM((lanes, HD), F32),
                pltpu.VMEM((lanes, HD), F32),
                pltpu.VMEM((lanes, key_cache.shape[1]), F32),
            ],
            compiler_params=params(8),
            cost_estimate=cost(4 * key_cache.size * (width // HD), 4 * key_cache.size),
            name="attention",
        )(
            in_hbm(w_query),
            jnp.broadcast_to(lengths[:, None], (rows, HD)),
            jnp.concatenate([cosine, cosine], 1),
            jnp.concatenate([-sine, sine], 1),
            in_vmem(keys),
            values,
            *[in_vmem(a) for a in arrived],
        )
        gathered = [heads] + [swap(heads, "gx", size_x, m) for m in range(1, size_x)]

        gathered = [in_vmem(a) for a in gathered]
        half = size_y // 2
        block = w_output.shape[1] // 2
        chunks = [list(range(1, size_x // 2)), [0]]

        def product(chunk, given, kind, *after):
            pieces = gathered[2:] if chunk == 0 else gathered[:2]
            tall = rows * len(pieces)
            return pl.pallas_call(
                functools.partial(project_out, given, len(after)),
                out_shape=pltpu.VMEM((tall, block), kind),
                in_specs=[VMEM] + [ANY] * len(after) + [VMEM] * len(pieces),
                out_specs=VMEM,
                scratch_shapes=[pltpu.VMEM((tall, width), F32)],
                compiler_params=params(8),
                cost_estimate=cost(2 * tall * width * block, 2 * width * block),
                name="project_out",
            )(in_vmem(w_output), *after, *pieces)

        given_near = product(1, 1, BF16)
        near_near = swap(given_near, "gy", size_y, 1)
        own_near = product(1, 0, F32, gathered[2])
        given_far = product(0, 1, BF16)
        near_far = swap(given_far, "gy", size_y, 1)
        owns = [product(0, 0, F32, near_near), own_near]
        near = [near_far, near_near]
        blocks = []
        for chunk, distances in enumerate(chunks):
            tall = 2 * rows * len(distances)
            pair = pl.pallas_call(
                add_near,
                out_shape=pltpu.VMEM((tall, block), BF16),
                in_specs=[VMEM] * 2,
                out_specs=VMEM,
                compiler_params=params(4),
                name="add_near",
            )(in_vmem(owns[chunk]), in_vmem(near[chunk]))
            far = [pair] + [swap(pair, "gy", size_y, 2 * m) for m in range(1, half)]
            done = pl.pallas_call(
                functools.partial(finish, distances, rows),
                out_shape=pltpu.VMEM((tall, block), BF16),
                in_specs=[VMEM] * (1 + half),
                out_specs=VMEM,
                scratch_shapes=[pltpu.VMEM((half, tall, block), F32)],
                compiler_params=params(8),
                name="finish",
            )(in_vmem(inputs), *[in_vmem(a) for a in far])
            blocks += [done, swap(done, "gy", size_y, 1)]
        return pl.pallas_call(
            functools.partial(assemble, chunks[::-1], rows),
            out_shape=jax.ShapeDtypeStruct((batch, 2 * block), BF16),
            in_specs=[VMEM] * 4,
            out_specs=ANY,
            scratch_shapes=[sems(size_x)],
            compiler_params=params(4),
            name="assemble",
        )(*[in_vmem(b) for b in blocks[2:] + blocks[:2]])

    placed = (
        P("groups", "gx"),
        P("gx"),
        P("gx", "gy"),
        P("gx", "gy"),
        P("gx", "gy"),
        P("gy", "gx"),
        P(("groups", "gx"), None, "gy"),
        P(("groups", "gx"), None, "gy"),
        P(("groups", "gx")),
    )
    return jax.shard_map(
        shards, mesh=mesh, in_specs=placed, out_specs=P("groups", "gx"), check_vma=False
    )
```

```python
import functools
import math

import jax
import jax.numpy as jnp
from jax import lax
from jax.experimental import pallas as pl
from jax.experimental.pallas import tpu as pltpu
from jax.sharding import PartitionSpec as P

HD = 128
EPS = 1e-05
ROPE_BASE = 500000.0
CHUNK = 256
F32 = jnp.float32
BF16 = jnp.bfloat16
F16 = jnp.float16
SQUARES = 2.0**-8

ANY = pl.BlockSpec(memory_space=pl.ANY)
VMEM = pl.BlockSpec(memory_space=pltpu.VMEM)
MIB = 1 << 20


def columns(index, width):
    return pl.ds(pl.multiple_of(index * width, HD), width)


def params(mib):
    return pltpu.CompilerParams(vmem_limit_bytes=mib * MIB)


def cost(flops, nbytes):
    return pl.CostEstimate(flops=flops, bytes_accessed=nbytes, transcendentals=0)


def in_vmem(value):
    return pltpu.with_memory_space_constraint(value, pltpu.VMEM)


def in_hbm(value):
    return pltpu.with_memory_space_constraint(value, pltpu.HBM)


def project(x_hbm, gain_hbm, wq_hbm, wk_hbm, wv_hbm, *refs):
    total, x, gain, wq, wkv, scaled, sems = refs
    depth = x.shape[1]
    cuts = [*range(0, depth, 2 * CHUNK), depth - CHUNK, depth]
    spans = [slice(a, b) for a, b in zip(cuts, cuts[1:])]
    steps = len(spans)
    pairs = [(x_hbm, x), (gain_hbm, gain), (wk_hbm, wkv.at[:, :HD]), (wv_hbm, wkv.at[:, HD:])]
    small = [pltpu.make_async_copy(a, b, sems.at[steps + i]) for i, (a, b) in enumerate(pairs)]
    large = []
    for step, span in enumerate(spans):
        part = pl.ds(span.start, span.stop - span.start)
        large.append(pltpu.make_async_copy(wq_hbm.at[part], wq.at[part], sems.at[step]))
    small[0].start()
    small[1].start()
    for copy in large[:2]:
        copy.start()
    small[2].start()
    small[3].start()
    for copy in large[2:]:
        copy.start()
    small[0].wait()
    small[1].wait()
    wide = x[...].astype(F32)
    scaled[...] = (wide * gain[...]).astype(BF16)
    squares = jnp.sum(wide * wide, 1, keepdims=True)
    width = wq.shape[1]
    dot = functools.partial(jnp.dot, preferred_element_type=F32)
    for step, copy in enumerate(large):
        copy.wait()
        part = spans[step]
        term = dot(scaled[:, part], wq[part])
        if step == 0:
            total[:, :width] = term
        else:
            total[:, :width] += term
        if step == 1:
            small[2].wait()
            small[3].wait()
            total[:, width : width + 2 * HD] = dot(scaled[...], wkv[...])
            total[:, width + 2 * HD :] = jnp.broadcast_to(squares, (squares.shape[0], HD))


def split(total, weights, *outs):
    del weights
    width = total.shape[1] - 3 * HD
    rows = outs[0].shape[0]
    me = lax.axis_index("gx")
    first = lax.broadcasted_iota(jnp.int32, (rows, HD), 1) < HD // 2
    for mask, out in enumerate(outs):
        start = pl.multiple_of((me ^ mask) * rows, 8)
        part = total[pl.ds(start, rows), :]
        if mask:
            whole = part[:, width + 2 * HD :] * SQUARES
            high = whole.astype(BF16).astype(F32)
            out[:, : width + 2 * HD] = part[:, : width + 2 * HD]
            out[:, width + 2 * HD :] = jnp.where(first, high, whole - high)
        else:
            out[...] = part


def turn_keys(after, k, v, limits, k_turned):
    del after, v, limits
    rows, slots = k.shape[0], k.shape[1]
    for row in range(rows):
        for start in range(0, slots, CHUNK):
            part = slice(start, start + CHUNK)
            k_turned[row, :, part] = k[row, part, :].T


def attention(size, model, weights, lengths, cosine, sine, k, v, *refs):
    del weights
    arrived = refs[:size]
    heads, q_rows, o_rows, scores = refs[size:]
    rows, slots = k.shape[0], k.shape[2]
    group = heads.shape[1] // HD
    width = group * HD
    summed = arrived[0][:, : width + 2 * HD]
    squares = arrived[0][:, width + 2 * HD :]
    for item in arrived[1:]:
        summed = summed + item[:, : width + 2 * HD].astype(F32)
        parts = item[:, width + 2 * HD :].astype(F32)
        squares = squares + (parts + pltpu.roll(parts, HD // 2, 1)) * (1.0 / SQUARES)
    scale = lax.rsqrt(squares / model + EPS)
    cosines, sines = cosine[...], sine[...]

    def turn(value):
        return value * cosines + pltpu.roll(value, HD // 2, 1) * sines

    for head in range(group):
        part = summed[:, head * HD : (head + 1) * HD] * scale
        q_rows[head * rows : (head + 1) * rows] = turn(part).astype(BF16).astype(F32)
    new_keys = turn(summed[:, width : width + HD] * scale).astype(BF16).astype(F32)
    new_values = (summed[:, width + HD : width + 2 * HD] * scale).astype(BF16).astype(F32)
    rate = HD ** (-0.5) * math.log2(math.e)
    half = slots // 2
    slot = lax.broadcasted_iota(jnp.int32, (2 * group, half), 1) + half
    second = lax.broadcasted_iota(jnp.int32, (2 * group, 1), 0) >= group
    empty = jnp.zeros((group, HD), F32)
    own, top = [], []
    for row in range(0, rows, 2):
        first = q_rows[pl.ds(row, group, stride=rows), :]
        other = q_rows[pl.ds(row + 1, group, stride=rows), :]
        queries = jnp.concatenate(
            [jnp.concatenate([first, empty], 1), jnp.concatenate([empty, other], 1)], 0
        )
        keys = jnp.concatenate([k[row], k[row + 1]], 0)
        raw = jnp.dot(queries.astype(BF16), keys, preferred_element_type=F32)
        low = raw[:, :half]
        limit = jnp.where(second, lengths[row + 1 : row + 2, :1], lengths[row : row + 1, :1])
        high = jnp.where(slot < limit, raw[:, half:], -jnp.inf)
        mine = slice(row * group, (row + 2) * group)
        scores[mine, :half] = low
        scores[mine, half:] = high
        both = jnp.concatenate(
            [first * new_keys[row : row + 1], other * new_keys[row + 1 : row + 2]], 0
        )
        own.append(jnp.sum(both, 1, keepdims=True))
        top.append(jnp.maximum(jnp.max(jnp.maximum(low, high), 1, keepdims=True), own[-1]))

    def soften(pair):
        mine = slice(2 * pair * group, (2 * pair + 2) * group)
        probs = jnp.exp2((scores[mine] - top[pair]) * rate)
        own_prob = jnp.exp2((own[pair] - top[pair]) * rate)
        share = 1.0 / (jnp.sum(probs, 1, keepdims=True) + own_prob)
        return (probs * share).astype(BF16), (own_prob * share).astype(BF16).astype(F32)

    ready = soften(0)
    for pair in range(rows // 2):
        weights, own_weight = ready
        if pair + 1 < rows // 2:
            ready = soften(pair + 1)
        sides = jnp.concatenate([v[2 * pair], v[2 * pair + 1]], 1)
        mixed = jnp.dot(weights, sides, preferred_element_type=F32)
        for side in range(2):
            row = 2 * pair + side
            mine = slice(side * group, (side + 1) * group)
            value = mixed[mine, side * HD : (side + 1) * HD]
            extra = own_weight[mine] * new_values[row : row + 1]
            o_rows[pl.ds(row, group, stride=rows), :] = value + extra
    for head in range(group):
        heads[:, head * HD : (head + 1) * HD] = o_rows[head * rows : (head + 1) * rows].astype(BF16)


def gather_rows(blocks, gathered):
    me = lax.axis_index("gx")
    rows = blocks[0].shape[0]
    for mask, block in enumerate(blocks):
        start = pl.multiple_of((me ^ mask) * rows, 8)
        gathered[pl.ds(start, rows), :] = block[...].astype(F32)
    return gathered[...].astype(BF16)


def place(chunk, given):
    return 2 * chunk + ((lax.axis_index("gy") ^ given) & 1)


def project_first(w, *refs):
    *blocks, out, heads, gathered = refs
    heads[...] = gather_rows(blocks, gathered)
    part = columns(place(0, 1), out.shape[1])
    out[...] = jnp.dot(heads[...], w[:, part], preferred_element_type=F32).astype(out.dtype)


def project_out(chunk, given, w, heads, out):
    part = columns(place(chunk, given), out.shape[1])
    out[...] = jnp.dot(heads[...], w[:, part], preferred_element_type=F32).astype(out.dtype)


def add_near(own, arrived, out):
    out[...] = (own[...] + arrived[...].astype(F32)).astype(BF16)


def finish(size, chunk, x, *refs):
    terms, out, ranked = refs[:size], refs[-2], refs[-1]
    rank = lax.axis_index("gy") // 2
    for mask, term in enumerate(terms):
        ranked[rank ^ mask] = term[...].astype(F32)
    total = ranked[0]
    for index in range(1, size):
        total = total + ranked[index]
    part = columns(place(chunk, 0), out.shape[1])
    out[...] = (x[:, part].astype(F32) + total).astype(BF16)


def write(places, *refs):
    blocks, out, sems = refs[: len(places)], refs[-2], refs[-1]
    copies = []
    for index, (block, (chunk, given)) in enumerate(zip(blocks, places)):
        target = out.at[:, columns(place(chunk, given), block.shape[1])]
        copies.append(pltpu.make_async_copy(block, target, sems.at[index]))
    for copy in copies:
        copy.start()
    for copy in copies:
        copy.wait()


def swap(value, axis, size, mask):
    return lax.ppermute(value, axis, [(i, i ^ mask) for i in range(size)])


def solution(mesh):
    size_x = mesh.shape["gx"]
    size_y = mesh.shape["gy"]
    sems = lambda n: pltpu.SemaphoreType.DMA((n,))

    def shards(inputs, gain, w_query, w_key, w_value, w_output, key_cache, value_cache, lengths):
        batch, depth = inputs.shape
        width = w_query.shape[1]
        rows = key_cache.shape[0]
        packed = width + 3 * HD
        block = w_output.shape[1] // 4

        total = pl.pallas_call(
            project,
            out_shape=pltpu.VMEM((batch, packed), F32),
            in_specs=[ANY] * 5,
            out_specs=VMEM,
            scratch_shapes=[
                pltpu.VMEM(inputs.shape, BF16),
                pltpu.VMEM((1, depth), F32),
                pltpu.VMEM(w_query.shape, BF16),
                pltpu.VMEM((depth, 2 * HD), BF16),
                pltpu.VMEM(inputs.shape, BF16),
                sems(depth // (2 * CHUNK) + 5),
            ],
            compiler_params=params(28),
            cost_estimate=cost(2 * batch * depth * packed, 2 * depth * packed),
            name="project",
        )(*[in_hbm(a) for a in (inputs, gain.reshape(1, depth), w_query, w_key, w_value)])
        sums = pl.pallas_call(
            split,
            out_shape=[pltpu.VMEM((rows, packed), F32)] * size_x,
            in_specs=[VMEM, ANY],
            out_specs=[VMEM] * size_x,
            compiler_params=params(4),
            name="split",
        )(in_vmem(total), in_hbm(w_query))
        arrived = [sums[0]]
        for mask in range(1, size_x):
            arrived.append(swap(sums[mask].astype(F16), "gx", size_x, mask).astype(F32))

        values = in_vmem(value_cache)
        limits = jnp.broadcast_to(lengths[:, None], (rows, HD))
        keys = pl.pallas_call(
            turn_keys,
            out_shape=pltpu.VMEM((rows, HD, key_cache.shape[1]), BF16),
            in_specs=[ANY, VMEM, ANY, ANY],
            out_specs=VMEM,
            compiler_params=params(4),
            cost_estimate=cost(0, 2 * key_cache.size),
            name="turn_keys",
        )(sums[0], in_vmem(key_cache), values, limits)

        half = HD // 2
        inverse = ROPE_BASE ** (-(jnp.arange(half, dtype=F32) * 2.0 / HD))
        angles = lengths.astype(F32)[:, None] * inverse[None, :]
        cosine, sine = jnp.cos(angles), jnp.sin(angles)
        lanes = rows * (width // HD)
        heads = pl.pallas_call(
            functools.partial(attention, size_x, depth * size_x),
            out_shape=pltpu.VMEM((rows, width), BF16),
            in_specs=[ANY] + [VMEM] * (5 + size_x),
            out_specs=VMEM,
            scratch_shapes=[
                pltpu.VMEM((lanes, HD), F32),
                pltpu.VMEM((lanes, HD), F32),
                pltpu.VMEM((lanes, key_cache.shape[1]), F32),
            ],
            compiler_params=params(8),
            cost_estimate=cost(4 * key_cache.size * (width // HD), 4 * key_cache.size),
            name="attention",
        )(
            in_hbm(w_query),
            limits,
            jnp.concatenate([cosine, cosine], 1),
            jnp.concatenate([-sine, sine], 1),
            in_vmem(keys),
            values,
            *[in_vmem(a) for a in arrived],
        )
        gathered = [heads] + [swap(heads, "gx", size_x, m) for m in range(1, size_x)]

        gathered = [in_vmem(a) for a in gathered]
        half = size_y // 2

        work = cost(2 * batch * width * block, 2 * width * block)
        first, everyone = pl.pallas_call(
            project_first,
            out_shape=[pltpu.VMEM((batch, block), BF16), pltpu.VMEM((batch, width), BF16)],
            in_specs=[VMEM] * (1 + size_x),
            out_specs=[VMEM] * 2,
            scratch_shapes=[pltpu.VMEM((batch, width), F32)],
            compiler_params=params(8),
            cost_estimate=work,
            name="project_first",
        )(in_vmem(w_output), *gathered)

        def product(chunk, given):
            return pl.pallas_call(
                functools.partial(project_out, chunk, given),
                out_shape=pltpu.VMEM((batch, block), BF16 if given else F32),
                in_specs=[VMEM] * 2,
                out_specs=VMEM,
                compiler_params=params(8),
                cost_estimate=work,
                name="project_out",
            )(in_vmem(w_output), in_vmem(everyone))

        near = [swap(term, "gy", size_y, 1) for term in (first, product(1, 1))]
        blocks = []
        for chunk in range(2):
            pair = pl.pallas_call(
                add_near,
                out_shape=pltpu.VMEM((batch, block), BF16),
                in_specs=[VMEM] * 2,
                out_specs=VMEM,
                compiler_params=params(4),
                name="add_near",
            )(in_vmem(product(chunk, 0)), in_vmem(near[chunk]))
            far = [pair] + [swap(pair, "gy", size_y, 2 * m) for m in range(1, half)]
            done = pl.pallas_call(
                functools.partial(finish, half, chunk),
                out_shape=pltpu.VMEM((batch, block), BF16),
                in_specs=[VMEM] * (1 + half),
                out_specs=VMEM,
                scratch_shapes=[pltpu.VMEM((half, batch, block), F32)],
                compiler_params=params(8),
                name="finish",
            )(in_vmem(inputs), *[in_vmem(a) for a in far])
            blocks += [done, swap(done, "gy", size_y, 1)]
        shape = jax.ShapeDtypeStruct((batch, block * 4), BF16)
        most = pl.pallas_call(
            functools.partial(write, [(0, 0), (0, 1), (1, 0)]),
            out_shape=shape,
            in_specs=[VMEM] * 3,
            out_specs=ANY,
            scratch_shapes=[sems(3)],
            compiler_params=params(4),
            name="write_most",
        )(*[in_vmem(b) for b in blocks[:3]])
        return pl.pallas_call(
            functools.partial(write, [(1, 1)]),
            out_shape=shape,
            in_specs=[VMEM, ANY],
            out_specs=ANY,
            scratch_shapes=[sems(1)],
            input_output_aliases={1: 0},
            compiler_params=params(4),
            name="write_last",
        )(in_vmem(blocks[3]), in_hbm(most))

    placed = (
        P("groups", "gx"),
        P("gx"),
        P("gx", "gy"),
        P("gx", "gy"),
        P("gx", "gy"),
        P("gy", "gx"),
        P(("groups", "gx"), None, "gy"),
        P(("groups", "gx"), None, "gy"),
        P(("groups", "gx")),
    )
    return jax.shard_map(
        shards, mesh=mesh, in_specs=placed, out_specs=P("groups", "gx"), check_vma=False
    )
```

```python
import functools
import math

import jax
import jax.numpy as jnp
from jax import lax
from jax.experimental import pallas as pl
from jax.experimental.pallas import tpu as pltpu
from jax.sharding import PartitionSpec as P

HD = 128
EPS = 1e-05
ROPE_BASE = 500000.0
CHUNK = 256
F32 = jnp.float32
BF16 = jnp.bfloat16
F16 = jnp.float16
SQUARES = 2.0**-8

ANY = pl.BlockSpec(memory_space=pl.ANY)
VMEM = pl.BlockSpec(memory_space=pltpu.VMEM)
MIB = 1 << 20


def columns(index, width):
    return pl.ds(pl.multiple_of(index * width, HD), width)


def params(mib):
    return pltpu.CompilerParams(vmem_limit_bytes=mib * MIB)


def cost(flops, nbytes):
    return pl.CostEstimate(flops=flops, bytes_accessed=nbytes, transcendentals=0)


def in_vmem(value):
    return pltpu.with_memory_space_constraint(value, pltpu.VMEM)


def in_hbm(value):
    return pltpu.with_memory_space_constraint(value, pltpu.HBM)


def project(x_hbm, gain_hbm, wq_hbm, wk_hbm, wv_hbm, *refs):
    total, x, gain, wq, wk, wv, scaled, sems = refs
    depth = x.shape[1]
    cuts = [*range(0, depth, 2 * CHUNK), depth - CHUNK, depth]
    spans = [slice(a, b) for a, b in zip(cuts, cuts[1:])]
    steps = len(spans)
    pairs = [(x_hbm, x), (gain_hbm, gain), (wk_hbm, wk), (wv_hbm, wv)]
    small = [pltpu.make_async_copy(a, b, sems.at[steps + i]) for i, (a, b) in enumerate(pairs)]
    large = []
    for step, span in enumerate(spans):
        part = pl.ds(span.start, span.stop - span.start)
        large.append(pltpu.make_async_copy(wq_hbm.at[part], wq.at[part], sems.at[step]))
    small[0].start()
    small[1].start()
    for copy in large[:2]:
        copy.start()
    small[2].start()
    small[3].start()
    for copy in large[2:]:
        copy.start()
    small[0].wait()
    small[1].wait()
    wide = x[...].astype(F32)
    scaled[...] = (wide * gain[...]).astype(BF16)
    squares = jnp.sum(wide * wide, 1, keepdims=True)
    width = wq.shape[1]
    dot = functools.partial(jnp.dot, preferred_element_type=F32)
    for step, copy in enumerate(large):
        copy.wait()
        part = spans[step]
        term = dot(scaled[:, part], wq[part])
        if step == 0:
            total[:, :width] = term
        else:
            total[:, :width] += term
        if step == 1:
            small[2].wait()
            total[:, width : width + HD] = dot(scaled[...], wk[...])
            small[3].wait()
            total[:, width + HD : width + 2 * HD] = dot(scaled[...], wv[...])
            total[:, width + 2 * HD :] = jnp.broadcast_to(squares, (squares.shape[0], HD))


def split(total, weights, *outs):
    del weights
    width = total.shape[1] - 3 * HD
    rows = outs[0].shape[0]
    me = lax.axis_index("gx")
    first = lax.broadcasted_iota(jnp.int32, (rows, HD), 1) < HD // 2
    for mask, out in enumerate(outs):
        start = pl.multiple_of((me ^ mask) * rows, 8)
        part = total[pl.ds(start, rows), :]
        if mask:
            whole = part[:, width + 2 * HD :] * SQUARES
            high = whole.astype(BF16).astype(F32)
            out[:, : width + 2 * HD] = part[:, : width + 2 * HD]
            out[:, width + 2 * HD :] = jnp.where(first, high, whole - high)
        else:
            out[...] = part


def turn_keys(after, k, k_turned):
    del after
    rows, slots = k.shape[0], k.shape[1]
    for row in range(rows):
        for start in range(0, slots, CHUNK):
            part = slice(start, start + CHUNK)
            k_turned[row, :, part] = k[row, part, :].T


def attention(size, model, weights, lengths, cosine, sine, k, v, *refs):
    del weights
    arrived = refs[:size]
    heads, q_rows, o_rows, scores = refs[size:]
    rows, slots = k.shape[0], k.shape[2]
    group = heads.shape[1] // HD
    width = group * HD
    summed = arrived[0][:, : width + 2 * HD]
    squares = arrived[0][:, width + 2 * HD :]
    for item in arrived[1:]:
        summed = summed + item[:, : width + 2 * HD].astype(F32)
        parts = item[:, width + 2 * HD :].astype(F32)
        squares = squares + (parts + pltpu.roll(parts, HD // 2, 1)) * (1.0 / SQUARES)
    scale = lax.rsqrt(squares / model + EPS)
    cosines, sines = cosine[...], sine[...]

    def turn(value):
        return value * cosines + pltpu.roll(value, HD // 2, 1) * sines

    for head in range(group):
        part = summed[:, head * HD : (head + 1) * HD] * scale
        q_rows[head * rows : (head + 1) * rows] = turn(part).astype(BF16).astype(F32)
    new_keys = turn(summed[:, width : width + HD] * scale).astype(BF16).astype(F32)
    new_values = (summed[:, width + HD : width + 2 * HD] * scale).astype(BF16).astype(F32)
    rate = HD ** (-0.5) * math.log2(math.e)
    half = slots // 2
    slot = lax.broadcasted_iota(jnp.int32, (2 * group, half), 1) + half
    second = lax.broadcasted_iota(jnp.int32, (2 * group, 1), 0) >= group
    empty = jnp.zeros((group, HD), F32)
    own, top = [], []
    for row in range(0, rows, 2):
        first = q_rows[pl.ds(row, group, stride=rows), :]
        other = q_rows[pl.ds(row + 1, group, stride=rows), :]
        queries = jnp.concatenate(
            [jnp.concatenate([first, empty], 1), jnp.concatenate([empty, other], 1)], 0
        )
        keys = jnp.concatenate([k[row], k[row + 1]], 0)
        raw = jnp.dot(queries.astype(BF16), keys, preferred_element_type=F32)
        low = raw[:, :half]
        limit = jnp.where(second, lengths[row + 1 : row + 2, :1], lengths[row : row + 1, :1])
        high = jnp.where(slot < limit, raw[:, half:], -jnp.inf)
        mine = slice(row * group, (row + 2) * group)
        scores[mine, :half] = low
        scores[mine, half:] = high
        both = jnp.concatenate(
            [first * new_keys[row : row + 1], other * new_keys[row + 1 : row + 2]], 0
        )
        own.append(jnp.sum(both, 1, keepdims=True))
        top.append(jnp.maximum(jnp.max(jnp.maximum(low, high), 1, keepdims=True), own[-1]))

    def soften(pair):
        mine = slice(2 * pair * group, (2 * pair + 2) * group)
        probs = jnp.exp2((scores[mine] - top[pair]) * rate)
        own_prob = jnp.exp2((own[pair] - top[pair]) * rate)
        share = 1.0 / (jnp.sum(probs, 1, keepdims=True) + own_prob)
        return (probs * share).astype(BF16), (own_prob * share).astype(BF16).astype(F32)

    ready = soften(0)
    for pair in range(rows // 2):
        weights, own_weight = ready
        if pair + 1 < rows // 2:
            ready = soften(pair + 1)
        sides = jnp.concatenate([v[2 * pair], v[2 * pair + 1]], 1)
        mixed = jnp.dot(weights, sides, preferred_element_type=F32)
        for side in range(2):
            row = 2 * pair + side
            mine = slice(side * group, (side + 1) * group)
            value = mixed[mine, side * HD : (side + 1) * HD]
            extra = own_weight[mine] * new_values[row : row + 1]
            o_rows[pl.ds(row, group, stride=rows), :] = value + extra
    for head in range(group):
        heads[:, head * HD : (head + 1) * HD] = o_rows[head * rows : (head + 1) * rows].astype(BF16)


def gather_rows(blocks, gathered):
    me = lax.axis_index("gx")
    rows = blocks[0].shape[0]
    for mask, block in enumerate(blocks):
        start = pl.multiple_of((me ^ mask) * rows, 8)
        gathered[pl.ds(start, rows), :] = block[...].astype(F32)
    return gathered[...].astype(BF16)


def place(chunk, given):
    return 2 * chunk + ((lax.axis_index("gy") ^ given) & 1)


def project_first(w, *refs):
    *blocks, out, heads, gathered = refs
    heads[...] = gather_rows(blocks, gathered)
    part = columns(place(0, 1), out.shape[1])
    out[...] = jnp.dot(heads[...], w[:, part], preferred_element_type=F32).astype(out.dtype)


def project_out(chunk, given, w, heads, out):
    part = columns(place(chunk, given), out.shape[1])
    out[...] = jnp.dot(heads[...], w[:, part], preferred_element_type=F32).astype(out.dtype)


def add_near(own, arrived, out):
    out[...] = (own[...] + arrived[...].astype(F32)).astype(BF16)


def finish(size, chunk, x, *refs):
    terms, out, ranked = refs[:size], refs[-2], refs[-1]
    rank = lax.axis_index("gy") // 2
    for mask, term in enumerate(terms):
        ranked[rank ^ mask] = term[...].astype(F32)
    total = ranked[0]
    for index in range(1, size):
        total = total + ranked[index]
    part = columns(place(chunk, 0), out.shape[1])
    out[...] = (x[:, part].astype(F32) + total).astype(BF16)


def write(places, *refs):
    blocks, out, sems = refs[: len(places)], refs[-2], refs[-1]
    copies = []
    for index, (block, (chunk, given)) in enumerate(zip(blocks, places)):
        target = out.at[:, columns(place(chunk, given), block.shape[1])]
        copies.append(pltpu.make_async_copy(block, target, sems.at[index]))
    for copy in copies:
        copy.start()
    for copy in copies:
        copy.wait()


def swap(value, axis, size, mask):
    return lax.ppermute(value, axis, [(i, i ^ mask) for i in range(size)])


def solution(mesh):
    size_x = mesh.shape["gx"]
    size_y = mesh.shape["gy"]
    sems = lambda n: pltpu.SemaphoreType.DMA((n,))

    def shards(inputs, gain, w_query, w_key, w_value, w_output, key_cache, value_cache, lengths):
        batch, depth = inputs.shape
        width = w_query.shape[1]
        rows = key_cache.shape[0]
        packed = width + 3 * HD
        block = w_output.shape[1] // 4

        total = pl.pallas_call(
            project,
            out_shape=pltpu.VMEM((batch, packed), F32),
            in_specs=[ANY] * 5,
            out_specs=VMEM,
            scratch_shapes=[
                pltpu.VMEM(inputs.shape, BF16),
                pltpu.VMEM((1, depth), F32),
                pltpu.VMEM(w_query.shape, BF16),
                pltpu.VMEM(w_key.shape, BF16),
                pltpu.VMEM(w_value.shape, BF16),
                pltpu.VMEM(inputs.shape, BF16),
                sems(depth // (2 * CHUNK) + 5),
            ],
            compiler_params=params(28),
            cost_estimate=cost(2 * batch * depth * packed, 2 * depth * packed),
            name="project",
        )(*[in_hbm(a) for a in (inputs, gain.reshape(1, depth), w_query, w_key, w_value)])
        sums = pl.pallas_call(
            split,
            out_shape=[pltpu.VMEM((rows, packed), F32)] * size_x,
            in_specs=[VMEM, ANY],
            out_specs=[VMEM] * size_x,
            compiler_params=params(4),
            name="split",
        )(in_vmem(total), in_hbm(w_query))
        arrived = [sums[0]]
        for mask in range(1, size_x):
            arrived.append(swap(sums[mask].astype(F16), "gx", size_x, mask).astype(F32))

        values = in_vmem(value_cache)
        keys = pl.pallas_call(
            turn_keys,
            out_shape=pltpu.VMEM((rows, HD, key_cache.shape[1]), BF16),
            in_specs=[ANY, VMEM],
            out_specs=VMEM,
            compiler_params=params(4),
            cost_estimate=cost(0, 2 * key_cache.size),
            name="turn_keys",
        )(sums[0], in_vmem(key_cache))

        half = HD // 2
        inverse = ROPE_BASE ** (-(jnp.arange(half, dtype=F32) * 2.0 / HD))
        angles = lengths.astype(F32)[:, None] * inverse[None, :]
        cosine, sine = jnp.cos(angles), jnp.sin(angles)
        lanes = rows * (width // HD)
        heads = pl.pallas_call(
            functools.partial(attention, size_x, depth * size_x),
            out_shape=pltpu.VMEM((rows, width), BF16),
            in_specs=[ANY] + [VMEM] * (5 + size_x),
            out_specs=VMEM,
            scratch_shapes=[
                pltpu.VMEM((lanes, HD), F32),
                pltpu.VMEM((lanes, HD), F32),
                pltpu.VMEM((lanes, key_cache.shape[1]), F32),
            ],
            compiler_params=params(8),
            cost_estimate=cost(4 * key_cache.size * (width // HD), 4 * key_cache.size),
            name="attention",
        )(
            in_hbm(w_query),
            jnp.broadcast_to(lengths[:, None], (rows, HD)),
            jnp.concatenate([cosine, cosine], 1),
            jnp.concatenate([-sine, sine], 1),
            in_vmem(keys),
            values,
            *[in_vmem(a) for a in arrived],
        )
        gathered = [heads] + [swap(heads, "gx", size_x, m) for m in range(1, size_x)]

        gathered = [in_vmem(a) for a in gathered]
        half = size_y // 2

        work = cost(2 * batch * width * block, 2 * width * block)
        first, everyone = pl.pallas_call(
            project_first,
            out_shape=[pltpu.VMEM((batch, block), BF16), pltpu.VMEM((batch, width), BF16)],
            in_specs=[VMEM] * (1 + size_x),
            out_specs=[VMEM] * 2,
            scratch_shapes=[pltpu.VMEM((batch, width), F32)],
            compiler_params=params(8),
            cost_estimate=work,
            name="project_first",
        )(in_vmem(w_output), *gathered)

        def product(chunk, given):
            return pl.pallas_call(
                functools.partial(project_out, chunk, given),
                out_shape=pltpu.VMEM((batch, block), BF16 if given else F32),
                in_specs=[VMEM] * 2,
                out_specs=VMEM,
                compiler_params=params(8),
                cost_estimate=work,
                name="project_out",
            )(in_vmem(w_output), in_vmem(everyone))

        near = [swap(term, "gy", size_y, 1) for term in (first, product(1, 1))]
        blocks = []
        for chunk in range(2):
            pair = pl.pallas_call(
                add_near,
                out_shape=pltpu.VMEM((batch, block), BF16),
                in_specs=[VMEM] * 2,
                out_specs=VMEM,
                compiler_params=params(4),
                name="add_near",
            )(in_vmem(product(chunk, 0)), in_vmem(near[chunk]))
            far = [pair] + [swap(pair, "gy", size_y, 2 * m) for m in range(1, half)]
            done = pl.pallas_call(
                functools.partial(finish, half, chunk),
                out_shape=pltpu.VMEM((batch, block), BF16),
                in_specs=[VMEM] * (1 + half),
                out_specs=VMEM,
                scratch_shapes=[pltpu.VMEM((half, batch, block), F32)],
                compiler_params=params(8),
                name="finish",
            )(in_vmem(inputs), *[in_vmem(a) for a in far])
            blocks += [done, swap(done, "gy", size_y, 1)]
        shape = jax.ShapeDtypeStruct((batch, block * 4), BF16)
        most = pl.pallas_call(
            functools.partial(write, [(0, 0), (0, 1), (1, 0)]),
            out_shape=shape,
            in_specs=[VMEM] * 3,
            out_specs=ANY,
            scratch_shapes=[sems(3)],
            compiler_params=params(4),
            name="write_most",
        )(*[in_vmem(b) for b in blocks[:3]])
        return pl.pallas_call(
            functools.partial(write, [(1, 1)]),
            out_shape=shape,
            in_specs=[VMEM, ANY],
            out_specs=ANY,
            scratch_shapes=[sems(1)],
            input_output_aliases={1: 0},
            compiler_params=params(4),
            name="write_last",
        )(in_vmem(blocks[3]), in_hbm(most))

    placed = (
        P("groups", "gx"),
        P("gx"),
        P("gx", "gy"),
        P("gx", "gy"),
        P("gx", "gy"),
        P("gy", "gx"),
        P(("groups", "gx"), None, "gy"),
        P(("groups", "gx"), None, "gy"),
        P(("groups", "gx")),
    )
    return jax.shard_map(
        shards, mesh=mesh, in_specs=placed, out_specs=P("groups", "gx"), check_vma=False
    )
```
